32 devices in a mesh: ctx: 4 (over x, core), tp: 8 (over z, y).
Axes of the slice: x: 2, y: 2, z: 4, core: 2. Of those that a mesh axis runs over, the one named last changes fastest.
Arguments:
- tokens: bfloat16 [512, 8192], P('ctx', 'tp'), may hold values from -6 to 6
- in_weight: bfloat16 [8192, 3, 8192], P(None, None, 'tp'), may hold values from -0.0625 to 0.0625
- filter_taps: float32 [3, 3, 8192], P(None, None, 'tp'), may hold values from -2.4 to 2.4
- decay_rate: float32 [16, 8192], P(None, 'tp'), may hold values from 0.000390625 to 0.08, as said below
- residue: float32 [16, 8192], P(None, 'tp'), may hold values from -80 to 80
Outputs:
- gated: bfloat16 [512, 8192], P('ctx', 'tp')
The draws below stay inside these ranges and needn't reach their ends.
Inputs may be any that keep to these rules, and one draw needn't show every extreme that they name: `decay_rate`: every decay rate lies between 0.2 / 512 and 0.08.
All inputs are finite; a program needn't handle non-finite values.
Results may differ from the reference program's by a relative error of at most 0.015.
Values may be sent and summed in bfloat16 or wider, within the bound.
No kernel may reach another device: no remote copies, remote signals or barrier semaphores. Data moves between devices by JAX's collectives and lax.ppermute only.
A program may use at most 192 MiB of HBM per device.

```python
import jax
import jax.numpy as jnp
from jax import lax

D = 8192
ORDER = 16
TAPS = 3
BLOCK = 128
SEQ = 512


def group_law(key):
    groups = ORDER // 4
    spacing = jax.random.uniform(jax.random.fold_in(key, 101), (groups, 1, D), jnp.float32, 0.095, 0.18)
    place = jax.random.uniform(jax.random.fold_in(key, 102), (groups, 1, D), jnp.float32)
    size = jax.random.uniform(jax.random.fold_in(key, 103), (groups, 1, D), jnp.float32, 0.3, 0.7)
    flips = jax.random.uniform(jax.random.fold_in(key, 104), (groups, 1, D), jnp.float32)
    sign = jnp.where(flips < 0.5, -1.0, 1.0).astype(jnp.float32)
    return (spacing, place, size, sign)


def draw_decay_rate(key, part):
    spacing, place, size, sign = group_law(key)
    low_end = jnp.log(0.2 / SEQ)
    high_end = jnp.log(0.08) - 3.0 * spacing
    base = low_end + (high_end - low_end) * place
    steps_in_group = jnp.arange(4, dtype=jnp.float32)[None, :, None]
    rates = jnp.exp(base + spacing * steps_in_group)
    return rates.reshape(ORDER, D).astype(jnp.float32)


def draw_residue(key, part):
    spacing, place, size, sign = group_law(key)
    pattern = jnp.array([1.0, -1.0, -1.0, 1.0], jnp.float32)[None, :, None]
    values = sign * size / (spacing * spacing) * pattern
    return values.reshape(ORDER, D).astype(jnp.float32)


def block_scale(key, dims, cuts, low, top_value):
    gain = 1.0
    for dim, shards_of in cuts:
        steps = jax.random.uniform(jax.random.fold_in(jax.random.fold_in(key, 6), dim), (shards_of,), jnp.float32, low / len(cuts), top_value / len(cuts))
        gain = gain * jnp.repeat(jnp.exp(steps), dims[dim] // shards_of).reshape((-1,) + (1,) * (len(dims) - 1 - dim))
    return gain


def noise(key, shape, scale, reach, pieces=(), held_as=jnp.bfloat16):
    gain = block_scale(key, shape, pieces, -0.22, 0.18) if pieces else 1.0
    drawn = jax.random.normal(key, shape, jnp.float32) * scale * gain
    return jnp.minimum(jnp.maximum(drawn, -reach), reach).astype(held_as)


def setup_inputs(seed: int = 0) -> dict:
    keys = jax.random.split(jax.random.key(seed), 6)
    return {
        "tokens": noise(keys[0], (SEQ, D), 1.0, 6.0, ((0, 4), (1, 8))),
        "in_weight": noise(keys[1], (D, 3, D), D ** -0.5, 0.0625, ((2, 8),)),
        "filter_taps": noise(keys[2], (TAPS, 3, D), 0.4, 2.4, ((2, 8),), jnp.float32),
        "decay_rate": draw_decay_rate(jax.random.fold_in(keys[5], 71), 0),
        "residue": draw_residue(jax.random.fold_in(keys[5], 71), 0),
    }


def reference(tokens, in_weight, filter_taps, decay_rate, residue):
    seq_len = tokens.shape[0]
    weight_flat = in_weight.reshape(D, 3 * D)
    projected = jnp.dot(tokens, weight_flat, preferred_element_type=jnp.float32)
    projected = projected.astype(jnp.bfloat16).reshape(seq_len, 3, D)
    lead_rows = TAPS - 1
    padded = jnp.concatenate([jnp.zeros((lead_rows, 3, D), projected.dtype), projected], axis=0)
    features = jnp.zeros((seq_len, 3, D), jnp.float32)
    for lag_index in range(TAPS):
        window = padded[lead_rows - lag_index:lead_rows - lag_index + seq_len].astype(jnp.float32)
        features = features + filter_taps[lag_index] * window
    query_part = features[:, 0]
    source = features[:, 1] * features[:, 2]
    coeffs = residue * jnp.sqrt(1.0 - jnp.exp(-2.0 * decay_rate))
    offsets = jnp.arange(BLOCK, dtype=jnp.float32)
    kernel = lax.optimization_barrier(jnp.sum(coeffs[None] * jnp.exp(-decay_rate[None] * offsets[:, None, None]), axis=1))
    gap_counts = jnp.arange(BLOCK)[:, None] - jnp.arange(BLOCK)[None, :]
    toeplitz = jnp.where((gap_counts >= 0)[:, :, None], kernel[jnp.maximum(gap_counts, 0)], 0.0)
    end_weights = jnp.exp(-decay_rate[None] * (BLOCK - 1.0 - offsets)[:, None, None])
    read_weights = coeffs[None] * jnp.exp(-decay_rate[None] * (offsets + 1.0)[:, None, None])
    block_decay = jnp.exp(-decay_rate * BLOCK)
    blocks = source.reshape(seq_len // BLOCK, BLOCK, D)

    def advance(carry_state, block_rows):
        inner_part = jnp.einsum('ijc,jc->ic', toeplitz, block_rows, precision=lax.Precision.HIGHEST)
        carried = jnp.einsum('inc,nc->ic', read_weights, carry_state, precision=lax.Precision.HIGHEST)
        state_next = block_decay * carry_state + jnp.einsum('jnc,jc->nc', end_weights, block_rows, precision=lax.Precision.HIGHEST)
        return (state_next, inner_part + carried)
    _, outputs = lax.scan(advance, jnp.zeros((ORDER, D), jnp.float32), blocks)
    response = outputs.reshape(seq_len, D)
    return (query_part * response).astype(jnp.bfloat16)
```

```python
import functools

import jax
import jax.numpy as jnp
from jax import lax
from jax.experimental import pallas as pl
from jax.experimental.pallas import tpu as pltpu
from jax.sharding import PartitionSpec as P

LANES = 128
DEPTH = 256
SLOTS = 6
GRID_ROWS = 4
VMEM = pl.BlockSpec(memory_space=pltpu.VMEM)
ANY = pl.BlockSpec(memory_space=pl.ANY)


def ring_order(count):
    if count % (2 * GRID_ROWS):
        return list(range(count))
    cols = count // GRID_ROWS
    cells = [(0, c) for c in range(cols)]
    for r in range(1, GRID_ROWS):
        inner = list(range(1, cols))
        cells += [(r, c) for c in (reversed(inner) if r % 2 else inner)]
    cells += [(r, 0) for r in range(GRID_ROWS - 1, 0, -1)]
    return [r * cols + c for r, c in cells]


def owner_at(order, step):
    me = lax.axis_index("tp")
    owner = jnp.int32(0)
    for place, index in enumerate(order):
        owner = jnp.where(me == index, order[(place - step) % len(order)], owner)
    return owner


def accumulate(order, steps, xs, w_ref, total, buf, sem, fresh):
    width = xs[0][0].shape[1]
    depth = min(DEPTH, width)
    jobs = [(b, k) for b in range(len(xs)) for k in range(width // depth)]
    owners = [owner_at(order, step) for step in steps]

    def copy(i):
        b, k = jobs[i]
        start = pl.multiple_of(owners[b] * width + k * depth, depth)
        slot = i % SLOTS
        return pltpu.make_async_copy(
            w_ref.at[:, pl.ds(start, depth), :], buf.at[slot], sem.at[slot]
        )

    for i in range(min(SLOTS, len(jobs))):
        copy(i).start()
    for i, (b, k) in enumerate(jobs):
        copy(i).wait()
        row = 0
        for part in xs[b]:
            rows = part.shape[0]
            x = part[:, k * depth : (k + 1) * depth]
            for s in range(total.shape[0]):
                term = jnp.dot(x, buf[i % SLOTS, s], preferred_element_type=jnp.float32)
                if fresh and i == 0:
                    total[s, row : row + rows] = term
                else:
                    total[s, row : row + rows] += term
            row += rows
        if i + SLOTS < len(jobs):
            copy(i + SLOTS).start()


def first_kernel(order, x_ref, w_ref, total, buf, sem):
    accumulate(order, [0], [[x_ref]], w_ref, total, buf, sem, True)


def middle_kernel(order, steps, count, *refs):
    xs = [[ref] for ref in refs[:count]]
    w_ref, _, total, buf, sem = refs[count:]
    accumulate(order, steps, xs, w_ref, total, buf, sem, False)


def last_kernel(order, step, xa_ref, xb_ref, w_ref, taps, decay, _, total, p_ref, out_ref, buf, sem):
    accumulate(order, [step], [[xa_ref, xb_ref]], w_ref, total, buf, sem, False)
    streams, rows, groups, lanes = p_ref.shape
    modes = decay.shape[0]
    for s in range(streams):
        value = total[s].astype(jnp.bfloat16).astype(jnp.float32)
        for g in range(groups):
            p_ref[s, :, g, :] = value[:, g * lanes : (g + 1) * lanes]
    rate = [decay[n] for n in range(modes)]

    def step_row(t, state):
        u = filtered(taps, p_ref, 1, t) * filtered(taps, p_ref, 2, t)
        return [r * s + u for r, s in zip(rate, state)]

    state = [jnp.zeros((groups, lanes), jnp.float32)] * modes
    for t in range(2, 8):
        state = step_row(t, state)

    def eight(i, state):
        for j in range(8):
            state = step_row(i * 8 + j, state)
        return state

    state = lax.fori_loop(1, rows // 8, eight, state)
    for n in range(modes):
        out_ref[n] = state[n]
    for s in (1, 2):
        for j, t in enumerate((0, 1)):
            out_ref[modes + (s - 1) * 2 + j] = p_ref[s, t]
    for s in range(streams):
        for j, t in enumerate((rows - 2, rows - 1)):
            out_ref[modes + 4 + s * 2 + j] = p_ref[s, t]


def filtered(taps, p_ref, s, t):
    return taps[0, s] * p_ref[s, t] + taps[1, s] * p_ref[s, t - 1] + taps[2, s] * p_ref[s, t - 2]


def edge(taps, s, first, second, before, last):
    return (
        taps[0, s] * first + taps[1, s] * last + taps[2, s] * before,
        taps[0, s] * second + taps[1, s] * first + taps[2, s] * last,
    )


def final_kernel(count, *refs):
    sent = refs[:count]
    p_ref, taps, table, out_ref, work = refs[count:]
    streams, rows, groups, lanes = p_ref.shape
    modes = table.shape[1]
    zero = jnp.zeros((groups, lanes), jnp.float32)

    def rim(d, s):
        if d >= count:
            return zero, zero
        return sent[d][modes + 4 + s * 2], sent[d][modes + 4 + s * 2 + 1]

    state = [zero] * modes
    for d in reversed(range(count)):
        ends = []
        for s in (1, 2):
            first, second = sent[d][modes + (s - 1) * 2], sent[d][modes + (s - 1) * 2 + 1]
            ends.append(edge(taps, s, first, second, *rim(d + 1, s)))
        u0, u1 = ends[0][0] * ends[1][0], ends[0][1] * ends[1][1]
        state = [
            table[1, n] * state[n] + (sent[d][n] + table[2, n] * u0 + table[3, n] * u1)
            for n in range(modes)
        ]

    def advance(t, q, u, state):
        state = [table[0, n] * state[n] + u for n in range(modes)]
        terms = [table[4, n] * state[n] for n in range(modes)]
        while len(terms) > 1:
            terms = [a + b for a, b in zip(terms[::2], terms[1::2])] + terms[len(terms) & ~1 :]
        work[t] = q * terms[0]
        return state

    edges = [edge(taps, s, p_ref[s, 0], p_ref[s, 1], *rim(0, s)) for s in range(streams)]
    for t in range(2):
        state = advance(t, edges[0][t], edges[1][t] * edges[2][t], state)

    def row(t, state):
        q, f1, f2 = [filtered(taps, p_ref, s, t) for s in range(3)]
        return advance(t, q, f1 * f2, state)

    for t in range(2, 8):
        state = row(t, state)

    def eight(i, state):
        for j in range(8):
            state = row(i * 8 + j, state)
        return state

    lax.fori_loop(1, rows // 8, eight, state)
    for g in range(groups):
        out_ref[:, g * lanes : (g + 1) * lanes] = work[:, g, :].astype(out_ref.dtype)


def on_device(tokens, in_weight, filter_taps, decay_rate, residue):
    rows, width = tokens.shape
    streams, chans = in_weight.shape[1:]
    modes = decay_rate.shape[0]
    groups = chans // LANES
    tp, ctx = lax.axis_size("tp"), lax.axis_size("ctx")
    order = ring_order(tp)
    weight = jnp.transpose(in_weight, (1, 0, 2))
    half = tp // 2
    ahead = [(order[i], order[(i + 1) % tp]) for i in range(tp)]
    back = [(b, a) for a, b in ahead]

    taps = filter_taps.reshape(filter_taps.shape[0], streams, groups, LANES)
    coeffs = residue * jnp.sqrt(1.0 - jnp.exp(-2.0 * decay_rate))
    table = jnp.stack(
        [jnp.exp(-decay_rate * k) for k in (1, rows, rows - 1, rows - 2)] + [coeffs]
    ).reshape(5, modes, groups, LANES)

    depth = min(DEPTH, width)
    stream_scratch = [
        pltpu.VMEM((SLOTS, streams, depth, chans), jnp.bfloat16),
        pltpu.SemaphoreType.DMA((SLOTS,)),
    ]
    sums = jax.ShapeDtypeStruct((streams, rows, chans), jnp.float32)
    params = pltpu.CompilerParams(vmem_limit_bytes=24 << 20)

    def cost(blocks):
        work = blocks * width * streams * chans
        return pl.CostEstimate(flops=2 * rows * work, bytes_accessed=2 * work, transcendentals=0)

    fore, aft = tokens, tokens
    total = pl.pallas_call(
        functools.partial(first_kernel, order),
        out_shape=sums,
        in_specs=[VMEM, ANY],
        out_specs=VMEM,
        scratch_shapes=stream_scratch,
        compiler_params=params,
        cost_estimate=cost(1),
        name="project_own",
    )(tokens, weight)
    for step in range(1, half):
        fore = lax.ppermute(fore, "tp", ahead)
        aft = lax.ppermute(aft, "tp", back)
        total = pl.pallas_call(
            functools.partial(middle_kernel, order, [step, -step], 2),
            out_shape=sums,
            in_specs=[VMEM, VMEM, ANY, VMEM],
            out_specs=VMEM,
            scratch_shapes=stream_scratch,
            input_output_aliases={3: 0},
            compiler_params=params,
            cost_estimate=cost(2),
            name="project_pair",
        )(fore, aft, weight, total)
    fore = lax.ppermute(fore[: rows // 2], "tp", ahead)
    aft = lax.ppermute(aft[rows // 2 :], "tp", back)
    _, projected, local = pl.pallas_call(
        functools.partial(last_kernel, order, half),
        out_shape=[
            sums,
            jax.ShapeDtypeStruct((streams, rows, groups, LANES), jnp.float32),
            jax.ShapeDtypeStruct((modes + 10, groups, LANES), jnp.float32),
        ],
        in_specs=[VMEM, VMEM, ANY, VMEM, VMEM, VMEM],
        out_specs=[VMEM, VMEM, VMEM],
        scratch_shapes=stream_scratch,
        input_output_aliases={5: 0},
        compiler_params=params,
        cost_estimate=cost(1),
        name="project_last",
    )(fore, aft, weight, taps, table[0], total)

    sent = [
        lax.ppermute(local, "ctx", [(j, j + d) for j in range(ctx - d)]) for d in range(1, ctx)
    ]
    return pl.pallas_call(
        functools.partial(final_kernel, len(sent)),
        out_shape=jax.ShapeDtypeStruct((rows, chans), jnp.bfloat16),
        in_specs=[VMEM] * (len(sent) + 3),
        out_specs=VMEM,
        scratch_shapes=[pltpu.VMEM((rows, groups, LANES), jnp.float32)],
        compiler_params=params,
        name="long_filter",
    )(*sent, projected, taps, table)


def solution(mesh):
    return jax.shard_map(
        on_device,
        mesh=mesh,
        in_specs=(
            P("ctx", "tp"),
            P(None, None, "tp"),
            P(None, None, "tp"),
            P(None, "tp"),
            P(None, "tp"),
        ),
        out_specs=P("ctx", "tp"),
        check_vma=False,
    )
```

```python
import functools

import jax
import jax.numpy as jnp
from jax import lax
from jax.experimental import pallas as pl
from jax.experimental.pallas import tpu as pltpu
from jax.sharding import PartitionSpec as P

LANES = 128
COLS = 256
DEPTH = 256
GRID_ROWS = 4
EDGE = 10
VMEM = pl.BlockSpec(memory_space=pltpu.VMEM)
HBM = pl.BlockSpec(memory_space=pltpu.HBM)


def ring_order(count):
    if count % (2 * GRID_ROWS):
        return list(range(count))
    cols = count // GRID_ROWS
    cells = [(0, c) for c in range(cols)]
    for r in range(1, GRID_ROWS):
        inner = list(range(1, cols))
        cells += [(r, c) for c in (reversed(inner) if r % 2 else inner)]
    cells += [(r, 0) for r in range(GRID_ROWS - 1, 0, -1)]
    return [r * cols + c for r, c in cells]


def owner_at(order, step):
    me = lax.axis_index("tp")
    owner = jnp.int32(0)
    for place, index in enumerate(order):
        owner = jnp.where(me == index, order[(place - step) % len(order)], owner)
    return owner


def block_loads(order, steps, w_ref, held, sem):
    count, streams, width, _ = held.shape
    copies = []
    for b, step in enumerate(steps):
        start = pl.multiple_of(owner_at(order, step) * width, width)
        for s in range(streams):
            copies.append(
                pltpu.make_async_copy(
                    w_ref.at[s, pl.ds(start, width), :], held.at[b, s], sem.at[b, s]
                )
            )
    return copies


def add_products(xs, held, total):
    streams, _, chans = total.shape
    for s in range(streams):
        for c in range(0, chans, COLS):
            at = slice(c, c + COLS)
            terms = [
                jnp.dot(x, held[b, s, :, at], preferred_element_type=jnp.float32)
                for b, x in enumerate(xs)
            ]
            total[s, :, at] += sum(terms)


def spread(out_ref, value):
    groups, lanes = out_ref.shape[-2:]
    for g in range(groups):
        out_ref[..., g, :] = value[..., g * lanes : (g + 1) * lanes]


def first_kernel(order, steps, x_ref, w_ref, total, held, own, own_sem, held_sem):
    width = x_ref.shape[1]
    depth = min(DEPTH, width)
    start = pl.multiple_of(owner_at(order, 0) * width, width)
    chunks = [
        pltpu.make_async_copy(
            w_ref.at[:, pl.ds(start + k * depth, depth), :],
            own.at[:, pl.ds(k * depth, depth), :],
            own_sem.at[k],
        )
        for k in range(width // depth)
    ]
    ahead = block_loads(order, steps, w_ref, held, held_sem)
    for copy in chunks + ahead:
        copy.start()
    for k, copy in enumerate(chunks):
        copy.wait()
        at = slice(k * depth, (k + 1) * depth)
        for s in range(total.shape[0]):
            for c in range(0, total.shape[2], COLS):
                to = slice(c, c + COLS)
                term = jnp.dot(x_ref[:, at], own[s, at, to], preferred_element_type=jnp.float32)
                if k:
                    total[s, :, to] += term
                else:
                    total[s, :, to] = term
    for copy in ahead:
        copy.wait()


def middle_kernel(order, steps, xa_ref, xb_ref, held, w_ref, _, total, next_held, sem):
    ahead = block_loads(order, steps, w_ref, next_held, sem)
    for copy in ahead:
        copy.start()
    add_products([xa_ref[...], xb_ref[...]], held, total)
    for copy in ahead:
        copy.wait()


def second_kernel(
    order, steps, xa_ref, xb_ref, held, w_ref, _, taps_in, decay, residue,
    total, next_held, taps, table, sem,
):
    ahead = block_loads(order, steps, w_ref, next_held, sem)
    for copy in ahead:
        copy.start()
    rate = decay[...]
    rows = total.shape[1]
    for i, power in enumerate((1, rows, rows - 1, rows - 2)):
        spread(table.at[i], jnp.exp(-rate * power))
    spread(table.at[4], residue[...] * jnp.sqrt(1.0 - jnp.exp(-2.0 * rate)))
    spread(taps, taps_in[...])
    add_products([xa_ref[...], xb_ref[...]], held, total)
    for copy in ahead:
        copy.wait()


def filtered(taps, p_ref, s, t):
    return (
        taps[0, s] * p_ref[s - 1, t]
        + taps[1, s] * p_ref[s - 1, t - 1]
        + taps[2, s] * p_ref[s - 1, t - 2]
    )


def last_kernel(xa_ref, xb_ref, held, taps, table, _, total, source, out_ref, p_ref, tail):
    add_products([jnp.concatenate([xa_ref[...], xb_ref[...]], axis=0)], held, total)
    rows, groups, lanes = source.shape
    modes = table.shape[1]
    for s in (1, 2):
        spread(p_ref.at[s - 1], rounded(total[s]))
    spread(tail, rounded(total[0, rows - 8 :]))
    rate = [table[0, n] for n in range(modes)]

    def step_row(t, state):
        u = filtered(taps, p_ref, 1, t) * filtered(taps, p_ref, 2, t)
        source[t] = u
        return [r * s + u for r, s in zip(rate, state)]

    state = [jnp.zeros((groups, lanes), jnp.float32)] * modes
    for t in range(2, 8):
        state = step_row(t, state)

    def eight(i, state):
        for j in range(8):
            state = step_row(i * 8 + j, state)
        return state

    state = lax.fori_loop(1, rows // 8, eight, state)
    for n in range(modes):
        out_ref[n] = state[n]
    for s in (1, 2):
        for j in range(2):
            out_ref[modes + (s - 1) * 2 + j] = p_ref[s - 1, j]
            out_ref[modes + 4 + s * 2 + j] = p_ref[s - 1, rows - 2 + j]
    for j in range(2):
        out_ref[modes + 4 + j] = tail[6 + j]


def rounded(value):
    return value.astype(jnp.bfloat16).astype(jnp.float32)


def tree_sum(terms):
    while len(terms) > 1:
        terms = [a + b for a, b in zip(terms[::2], terms[1::2])] + terms[len(terms) & ~1 :]
    return terms[0]


def local_kernel(total, source, taps, table, query, response, p_ref):
    rows, groups, lanes = source.shape
    modes = table.shape[1]
    spread(p_ref, rounded(total[0]))
    for j in range(2):
        query[j] = p_ref[j]

    def step_row(t, state):
        query[t] = taps[0, 0] * p_ref[t] + taps[1, 0] * p_ref[t - 1] + taps[2, 0] * p_ref[t - 2]
        u = source[t]
        state = [table[0, n] * state[n] + u for n in range(modes)]
        response[t] = tree_sum([table[4, n] * state[n] for n in range(modes)])
        return state

    state = [jnp.zeros((groups, lanes), jnp.float32)] * modes
    for t in range(2, 8):
        state = step_row(t, state)

    def eight(i, state):
        for j in range(8):
            state = step_row(i * 8 + j, state)
        return state

    lax.fori_loop(1, rows // 8, eight, state)


def edge(taps, s, first, second, before, last):
    return (
        taps[0, s] * first + taps[1, s] * last + taps[2, s] * before,
        taps[0, s] * second + taps[1, s] * first + taps[2, s] * last,
    )


def final_kernel(count, *refs):
    sent = refs[:count]
    local, query, response, taps, table, out_ref, work = refs[count:]
    rows, groups, lanes = query.shape
    modes = table.shape[1]
    zero = jnp.zeros((groups, lanes), jnp.float32)

    def rim(d, s):
        if d >= count:
            return zero, zero
        return sent[d][modes + 4 + s * 2], sent[d][modes + 4 + s * 2 + 1]

    def sources(block, d):
        ends = [
            edge(taps, s, block[modes + s * 2 - 2], block[modes + s * 2 - 1], *rim(d, s))
            for s in (1, 2)
        ]
        return ends[0][0] * ends[1][0], ends[0][1] * ends[1][1]

    state = [zero] * modes
    for d in reversed(range(count)):
        u0, u1 = sources(sent[d], d + 1)
        state = [
            table[1, n] * state[n] + (sent[d][n] + table[2, n] * u0 + table[3, n] * u1)
            for n in range(modes)
        ]
    heads = edge(taps, 0, query[0], query[1], *rim(0, 0))
    for t, u in enumerate(sources(local, 0)):
        state = [table[0, n] * state[n] + u for n in range(modes)]
        work[t] = heads[t] * tree_sum([table[4, n] * state[n] for n in range(modes)])
    carried = [table[4, n] * state[n] for n in range(modes)]

    def row(t, carried):
        carried = [table[0, n] * carried[n] for n in range(modes)]
        work[t] = query[t] * (response[t] + tree_sum(carried))
        return carried

    for t in range(2, 8):
        carried = row(t, carried)

    def eight(i, carried):
        for j in range(8):
            carried = row(i * 8 + j, carried)
        return carried

    lax.fori_loop(1, rows // 8, eight, carried)
    for g in range(groups):
        out_ref[:, g * lanes : (g + 1) * lanes] = work[:, g, :].astype(out_ref.dtype)


def on_device(tokens, in_weight, filter_taps, decay_rate, residue):
    rows, width = tokens.shape
    streams, chans = in_weight.shape[1:]
    lags = filter_taps.shape[0]
    modes = decay_rate.shape[0]
    groups = chans // LANES
    tp, ctx = lax.axis_size("tp"), lax.axis_size("ctx")
    order = ring_order(tp)
    weight = jnp.transpose(in_weight, (1, 0, 2))
    half = tp // 2
    ahead = [(order[i], order[(i + 1) % tp]) for i in range(tp)]
    back = [(b, a) for a, b in ahead]

    def f32(*shape):
        return jax.ShapeDtypeStruct(shape, jnp.float32)

    def held(count):
        return jax.ShapeDtypeStruct((count, streams, width, chans), jnp.bfloat16)

    def loads(step):
        return [step, -step] if step < half else [step]

    sums = f32(streams, rows, chans)
    wide = f32(rows, groups, LANES)
    params = pltpu.CompilerParams(vmem_limit_bytes=12 << 20)
    cost = pl.CostEstimate(flops=0, bytes_accessed=16 << 20, transcendentals=0)

    depth = min(DEPTH, width)
    total, weights = pl.pallas_call(
        functools.partial(first_kernel, order, loads(1)),
        out_shape=[sums, held(len(loads(1)))],
        in_specs=[VMEM, HBM],
        out_specs=[VMEM] * 2,
        scratch_shapes=[
            pltpu.VMEM((streams, width, chans), jnp.bfloat16),
            pltpu.SemaphoreType.DMA((width // depth,)),
            pltpu.SemaphoreType.DMA((len(loads(1)), streams)),
        ],
        compiler_params=params,
        cost_estimate=cost,
        name="project_own",
    )(tokens, weight)
    fore, aft = tokens, tokens
    for step in range(1, half):
        fore = lax.ppermute(fore, "tp", ahead)
        aft = lax.ppermute(aft, "tp", back)
        fore, aft, total, weights = lax.optimization_barrier((fore, aft, total, weights))
        coming = loads(step + 1)
        tables = [f32(lags, streams, groups, LANES), f32(5, modes, groups, LANES)]
        with_tables = step == 1
        total, weights, *made = pl.pallas_call(
            functools.partial(second_kernel if with_tables else middle_kernel, order, coming),
            out_shape=[sums, held(len(coming))] + tables * with_tables,
            in_specs=[VMEM, VMEM, VMEM, HBM, VMEM] + [VMEM] * 3 * with_tables,
            out_specs=[VMEM, VMEM] + [VMEM] * 2 * with_tables,
            scratch_shapes=[pltpu.SemaphoreType.DMA((len(coming), streams))],
            input_output_aliases={4: 0},
            compiler_params=params,
            cost_estimate=cost,
            name="project_pair",
        )(fore, aft, weights, weight, total, *[filter_taps, decay_rate, residue][: 3 * with_tables])
        if with_tables:
            taps, table = made
    fore = lax.ppermute(fore[: rows // 2], "tp", ahead)
    aft = lax.ppermute(aft[rows // 2 :], "tp", back)
    total, source, local = pl.pallas_call(
        last_kernel,
        out_shape=[sums, wide, f32(modes + EDGE, groups, LANES)],
        in_specs=[VMEM] * 6,
        out_specs=[VMEM] * 3,
        scratch_shapes=[
            pltpu.VMEM((2, rows, groups, LANES), jnp.float32),
            pltpu.VMEM((8, groups, LANES), jnp.float32),
        ],
        input_output_aliases={5: 0},
        compiler_params=params,
        cost_estimate=cost,
        name="project_last",
    )(fore, aft, weights, taps, table, total)

    sent = [
        lax.ppermute(local, "ctx", [(j, j + d) for j in range(ctx - d)]) for d in range(1, ctx)
    ]
    query, response = pl.pallas_call(
        local_kernel,
        out_shape=[wide, wide],
        in_specs=[VMEM] * 4,
        out_specs=[VMEM] * 2,
        scratch_shapes=[pltpu.VMEM((rows, groups, LANES), jnp.float32)],
        compiler_params=params,
        cost_estimate=cost,
        name="local_response",
    )(total, source, taps, table)
    return pl.pallas_call(
        functools.partial(final_kernel, len(sent)),
        out_shape=jax.ShapeDtypeStruct((rows, chans), jnp.bfloat16),
        in_specs=[VMEM] * (len(sent) + 5),
        out_specs=VMEM,
        scratch_shapes=[pltpu.VMEM((rows, groups, LANES), jnp.float32)],
        compiler_params=params,
        name="carried_response",
    )(*sent, local, query, response, taps, table)


def solution(mesh):
    return jax.shard_map(
        on_device,
        mesh=mesh,
        in_specs=(
            P("ctx", "tp"),
            P(None, None, "tp"),
            P(None, None, "tp"),
            P(None, "tp"),
            P(None, "tp"),
        ),
        out_specs=P("ctx", "tp"),
        check_vma=False,
    )
```

```python
import functools

import jax
import jax.numpy as jnp
from jax import lax
from jax.experimental import pallas as pl
from jax.experimental.pallas import tpu as pltpu
from jax.sharding import PartitionSpec as P

LANES = 128
COLS = 256
DEPTH = 256
GRID_ROWS = 4
EDGE = 10
VMEM = pl.BlockSpec(memory_space=pltpu.VMEM)
HBM = pl.BlockSpec(memory_space=pltpu.HBM)


def ring_order(count):
    if count % (2 * GRID_ROWS):
        return list(range(count))
    cols = count // GRID_ROWS
    cells = [(0, c) for c in range(cols)]
    for r in range(1, GRID_ROWS):
        inner = list(range(1, cols))
        cells += [(r, c) for c in (reversed(inner) if r % 2 else inner)]
    cells += [(r, 0) for r in range(GRID_ROWS - 1, 0, -1)]
    return [r * cols + c for r, c in cells]


def owner_at(order, step):
    me = lax.axis_index("tp")
    owner = jnp.int32(0)
    for place, index in enumerate(order):
        owner = jnp.where(me == index, order[(place - step) % len(order)], owner)
    return owner


def block_loads(order, steps, w_ref, held, sem):
    count, streams, width, _ = held.shape
    copies = []
    for b, step in enumerate(steps):
        start = pl.multiple_of(owner_at(order, step) * width, width)
        for s in range(streams):
            copies.append(
                pltpu.make_async_copy(
                    w_ref.at[s, pl.ds(start, width), :], held.at[b, s], sem.at[b, s]
                )
            )
    return copies


def add_products(xs, held, total, s):
    for c in range(0, total.shape[2], COLS):
        at = slice(c, c + COLS)
        terms = [
            jnp.dot(x, held[b, s, :, at], preferred_element_type=jnp.float32)
            for b, x in enumerate(xs)
        ]
        total[s, :, at] += sum(terms)


def multiply_beside(loads, xa_ref, xb_ref, held, total):
    @pl.loop(0, total.shape[0])
    def _(s):
        add_products([xa_ref[...], xb_ref[...]], held, total, s)

    for copy in loads:
        copy.wait()


def spread(out_ref, value):
    groups, lanes = out_ref.shape[-2:]
    for g in range(groups):
        out_ref[..., g, :] = value[..., g * lanes : (g + 1) * lanes]


def first_kernel(order, steps, x_ref, w_ref, total, held, own, own_sem, held_sem):
    width = x_ref.shape[1]
    depth = min(DEPTH, width)
    start = pl.multiple_of(owner_at(order, 0) * width, width)
    chunks = [
        pltpu.make_async_copy(
            w_ref.at[:, pl.ds(start + k * depth, depth), :],
            own.at[:, pl.ds(k * depth, depth), :],
            own_sem.at[k],
        )
        for k in range(width // depth)
    ]
    ahead = block_loads(order, steps, w_ref, held, held_sem)
    for copy in chunks + ahead:
        copy.start()
    for k, copy in enumerate(chunks):
        copy.wait()
        at = slice(k * depth, (k + 1) * depth)
        for s in range(total.shape[0]):
            for c in range(0, total.shape[2], COLS):
                to = slice(c, c + COLS)
                term = jnp.dot(x_ref[:, at], own[s, at, to], preferred_element_type=jnp.float32)
                if k:
                    total[s, :, to] += term
                else:
                    total[s, :, to] = term
    for copy in ahead:
        copy.wait()


def middle_kernel(order, steps, xa_ref, xb_ref, held, w_ref, _, total, next_held, sem):
    ahead = block_loads(order, steps, w_ref, next_held, sem)
    for copy in ahead:
        copy.start()
    multiply_beside(ahead, xa_ref, xb_ref, held, total)


def second_kernel(
    order, steps, xa_ref, xb_ref, held, w_ref, _, taps_in, decay, residue,
    total, next_held, taps, table, sem,
):
    ahead = block_loads(order, steps, w_ref, next_held, sem)
    for copy in ahead:
        copy.start()
    rate = decay[...]
    rows = total.shape[1]
    for i, power in enumerate((1, rows, rows - 1, rows - 2)):
        spread(table.at[i], jnp.exp(-rate * power))
    spread(table.at[4], residue[...] * jnp.sqrt(1.0 - jnp.exp(-2.0 * rate)))
    spread(taps, taps_in[...])
    multiply_beside(ahead, xa_ref, xb_ref, held, total)


def filtered(taps, p_ref, s, t):
    return (
        taps[0, s] * p_ref[s - 1, t]
        + taps[1, s] * p_ref[s - 1, t - 1]
        + taps[2, s] * p_ref[s - 1, t - 2]
    )


def last_kernel(xa_ref, xb_ref, held, taps, table, _, total, source, out_ref, p_ref, tail):
    x = jnp.concatenate([xa_ref[...], xb_ref[...]], axis=0)
    for s in range(total.shape[0]):
        add_products([x], held, total, s)
    rows, groups, lanes = source.shape
    modes = table.shape[1]
    for s in (1, 2):
        spread(p_ref.at[s - 1], rounded(total[s]))
    spread(tail, rounded(total[0, rows - 8 :]))
    rate = [table[0, n] for n in range(modes)]

    def step_row(t, state):
        u = filtered(taps, p_ref, 1, t) * filtered(taps, p_ref, 2, t)
        source[t] = u
        return [r * s + u for r, s in zip(rate, state)]

    state = [jnp.zeros((groups, lanes), jnp.float32)] * modes
    for t in range(2, 8):
        state = step_row(t, state)

    def eight(i, state):
        for j in range(8):
            state = step_row(i * 8 + j, state)
        return state

    state = lax.fori_loop(1, rows // 8, eight, state)
    for n in range(modes):
        out_ref[n] = state[n]
    for s in (1, 2):
        for j in range(2):
            out_ref[modes + (s - 1) * 2 + j] = p_ref[s - 1, j]
            out_ref[modes + 4 + s * 2 + j] = p_ref[s - 1, rows - 2 + j]
    for j in range(2):
        out_ref[modes + 4 + j] = tail[6 + j]


def rounded(value):
    return value.astype(jnp.bfloat16).astype(jnp.float32)


def tree_sum(terms):
    while len(terms) > 1:
        terms = [a + b for a, b in zip(terms[::2], terms[1::2])] + terms[len(terms) & ~1 :]
    return terms[0]


def local_kernel(total, source, taps, table, query, response, p_ref):
    rows, groups, lanes = source.shape
    modes = table.shape[1]
    spread(p_ref, rounded(total[0]))
    for j in range(2):
        query[j] = p_ref[j]

    def step_row(t, state):
        query[t] = taps[0, 0] * p_ref[t] + taps[1, 0] * p_ref[t - 1] + taps[2, 0] * p_ref[t - 2]
        u = source[t]
        state = [table[0, n] * state[n] + u for n in range(modes)]
        response[t] = tree_sum([table[4, n] * state[n] for n in range(modes)])
        return state

    state = [jnp.zeros((groups, lanes), jnp.float32)] * modes
    for t in range(2, 8):
        state = step_row(t, state)

    def eight(i, state):
        for j in range(8):
            state = step_row(i * 8 + j, state)
        return state

    lax.fori_loop(1, rows // 8, eight, state)


def edge(taps, s, first, second, before, last):
    return (
        taps[0, s] * first + taps[1, s] * last + taps[2, s] * before,
        taps[0, s] * second + taps[1, s] * first + taps[2, s] * last,
    )


def lead_sources(taps, heads, rims):
    one = edge(taps, 1, heads[0], heads[1], rims[2], rims[3])
    two = edge(taps, 2, heads[2], heads[3], rims[4], rims[5])
    return one[0] * two[0], one[1] * two[1]


class Summary:
    def __init__(self, rows, modes):
        self.state = rows[:modes]
        self.heads = rows[modes : modes + 4]
        self.rims = rows[modes + 4 :]

    @classmethod
    def read(cls, ref, modes):
        return cls([ref[i] for i in range(ref.shape[0])], modes)

    @classmethod
    def chosen(cls, odd, when_odd, when_even, modes):
        pairs = zip(when_odd.rows(), when_even.rows())
        return cls([jnp.where(odd, a, b) for a, b in pairs], modes)

    def rows(self):
        return self.state + self.heads + self.rims

    def complete(self, taps, rims, by_first, by_second):
        u0, u1 = lead_sources(taps, self.heads, rims)
        return [x + f * u0 + g * u1 for x, f, g in zip(self.state, by_first, by_second)]


def powers(table):
    return [[table[i, n] for n in range(table.shape[1])] for i in range(table.shape[0])]


def chip_kernel(local, partner, taps, table, out_ref):
    modes = table.shape[1]
    odd = lax.rem(lax.axis_index("ctx"), 2) == 1
    mine, other = Summary.read(local, modes), Summary.read(partner, modes)
    first = Summary.chosen(odd, other, mine, modes)
    second = Summary.chosen(odd, mine, other, modes)
    _, block, less_one, less_two, _ = powers(table)
    end = second.complete(taps, first.rims, less_one, less_two)
    joined = [d * x + y for d, x, y in zip(block, first.state, end)]
    for i, value in enumerate(joined + first.heads + second.rims):
        out_ref[i] = value


def final_kernel(count, *refs):
    sent = refs[:count]
    local, partner, query, response, taps, table, out_ref, work = refs[count:]
    rows, groups, lanes = query.shape
    modes = table.shape[1]
    nothing = [jnp.zeros((groups, lanes), jnp.float32)] * 6
    odd = lax.rem(lax.axis_index("ctx"), 2) == 1
    _, block, less_one, less_two, _ = powers(table)
    chips = [Summary.read(ref, modes) for ref in sent]
    rims = [chip.rims for chip in chips] + [nothing]

    state = [nothing[0]] * modes
    for d in reversed(range(count)):
        end = chips[d].complete(
            taps,
            rims[d + 1],
            [a * b for a, b in zip(block, less_one)],
            [a * b for a, b in zip(block, less_two)],
        )
        state = [d * d * x + y for d, x, y in zip(block, state, end)]
    before = Summary.read(partner, modes)
    end = before.complete(taps, rims[0], less_one, less_two)
    state = [jnp.where(odd, d * x + y, x) for d, x, y in zip(block, state, end)]
    rim = [jnp.where(odd, a, b) for a, b in zip(before.rims, rims[0])]

    leads = lead_sources(taps, Summary.read(local, modes).heads, rim)
    heads = edge(taps, 0, query[0], query[1], rim[0], rim[1])
    for t, u in enumerate(leads):
        state = [table[0, n] * state[n] + u for n in range(modes)]
        work[t] = heads[t] * tree_sum([table[4, n] * state[n] for n in range(modes)])
    carried = [table[4, n] * state[n] for n in range(modes)]

    def row(t, carried):
        carried = [table[0, n] * carried[n] for n in range(modes)]
        work[t] = query[t] * (response[t] + tree_sum(carried))
        return carried

    for t in range(2, 8):
        carried = row(t, carried)

    def eight(i, carried):
        for j in range(8):
            carried = row(i * 8 + j, carried)
        return carried

    lax.fori_loop(1, rows // 8, eight, carried)
    for g in range(groups):
        out_ref[:, g * lanes : (g + 1) * lanes] = work[:, g, :].astype(out_ref.dtype)


def on_device(tokens, in_weight, filter_taps, decay_rate, residue):
    rows, width = tokens.shape
    streams, chans = in_weight.shape[1:]
    lags = filter_taps.shape[0]
    modes = decay_rate.shape[0]
    groups = chans // LANES
    tp, ctx = lax.axis_size("tp"), lax.axis_size("ctx")
    order = ring_order(tp)
    weight = jnp.transpose(in_weight, (1, 0, 2))
    half = tp // 2
    ahead = [(order[i], order[(i + 1) % tp]) for i in range(tp)]
    back = [(b, a) for a, b in ahead]

    def f32(*shape):
        return jax.ShapeDtypeStruct(shape, jnp.float32)

    def held(count):
        return jax.ShapeDtypeStruct((count, streams, width, chans), jnp.bfloat16)

    def loads(step):
        return [step, -step] if step < half else [step]

    sums = f32(streams, rows, chans)
    wide = f32(rows, groups, LANES)
    params = pltpu.CompilerParams(vmem_limit_bytes=12 << 20)
    cost = pl.CostEstimate(flops=0, bytes_accessed=16 << 20, transcendentals=0)

    depth = min(DEPTH, width)
    total, weights = pl.pallas_call(
        functools.partial(first_kernel, order, loads(1)),
        out_shape=[sums, held(len(loads(1)))],
        in_specs=[VMEM, HBM],
        out_specs=[VMEM] * 2,
        scratch_shapes=[
            pltpu.VMEM((streams, width, chans), jnp.bfloat16),
            pltpu.SemaphoreType.DMA((width // depth,)),
            pltpu.SemaphoreType.DMA((len(loads(1)), streams)),
        ],
        compiler_params=params,
        cost_estimate=cost,
        name="project_own",
    )(tokens, weight)
    fore, aft = tokens, tokens
    for step in range(1, half):
        fore = lax.ppermute(fore, "tp", ahead)
        aft = lax.ppermute(aft, "tp", back)
        fore, aft, total, weights = lax.optimization_barrier((fore, aft, total, weights))
        coming = loads(step + 1)
        tables = [f32(lags, streams, groups, LANES), f32(5, modes, groups, LANES)]
        with_tables = step == 1
        total, weights, *made = pl.pallas_call(
            functools.partial(second_kernel if with_tables else middle_kernel, order, coming),
            out_shape=[sums, held(len(coming))] + tables * with_tables,
            in_specs=[VMEM, VMEM, VMEM, HBM, VMEM] + [VMEM] * 3 * with_tables,
            out_specs=[VMEM, VMEM] + [VMEM] * 2 * with_tables,
            scratch_shapes=[pltpu.SemaphoreType.DMA((len(coming), streams))],
            input_output_aliases={4: 0},
            compiler_params=params,
            cost_estimate=cost,
            name="project_pair",
        )(fore, aft, weights, weight, total, *[filter_taps, decay_rate, residue][: 3 * with_tables])
        if with_tables:
            taps, table = made
    fore = lax.ppermute(fore[: rows // 2], "tp", ahead)
    aft = lax.ppermute(aft[rows // 2 :], "tp", back)
    total, source, local = pl.pallas_call(
        last_kernel,
        out_shape=[sums, wide, f32(modes + EDGE, groups, LANES)],
        in_specs=[VMEM] * 6,
        out_specs=[VMEM] * 3,
        scratch_shapes=[
            pltpu.VMEM((2, rows, groups, LANES), jnp.float32),
            pltpu.VMEM((8, groups, LANES), jnp.float32),
        ],
        input_output_aliases={5: 0},
        compiler_params=params,
        cost_estimate=cost,
        name="project_last",
    )(fore, aft, weights, taps, table, total)

    partner = lax.ppermute(local, "ctx", [(j, j ^ 1) for j in range(ctx)])
    chip = pl.pallas_call(
        chip_kernel,
        out_shape=f32(modes + EDGE, groups, LANES),
        in_specs=[VMEM] * 4,
        out_specs=VMEM,
        compiler_params=params,
        name="chip_state",
    )(local, partner, taps, table)
    sent = [
        lax.ppermute(chip, "ctx", [(j, j + d) for j in range(ctx - d)]) for d in range(2, ctx, 2)
    ]
    query, response = pl.pallas_call(
        local_kernel,
        out_shape=[wide, wide],
        in_specs=[VMEM] * 4,
        out_specs=[VMEM] * 2,
        scratch_shapes=[pltpu.VMEM((rows, groups, LANES), jnp.float32)],
        compiler_params=params,
        cost_estimate=cost,
        name="local_response",
    )(total, source, taps, table)
    return pl.pallas_call(
        functools.partial(final_kernel, len(sent)),
        out_shape=jax.ShapeDtypeStruct((rows, chans), jnp.bfloat16),
        in_specs=[VMEM] * (len(sent) + 6),
        out_specs=VMEM,
        scratch_shapes=[pltpu.VMEM((rows, groups, LANES), jnp.float32)],
        compiler_params=params,
        name="carried_response",
    )(*sent, local, partner, query, response, taps, table)


def solution(mesh):
    return jax.shard_map(
        on_device,
        mesh=mesh,
        in_specs=(
            P("ctx", "tp"),
            P(None, None, "tp"),
            P(None, None, "tp"),
            P(None, "tp"),
            P(None, "tp"),
        ),
        out_specs=P("ctx", "tp"),
        check_vma=False,
    )
```

```python
import functools

import jax
import jax.numpy as jnp
from jax import lax
from jax.experimental import pallas as pl
from jax.experimental.pallas import tpu as pltpu
from jax.sharding import PartitionSpec as P

LANES = 128
COLS = 256
DEPTH = 256
GRID_ROWS = 4
EDGE = 10
EARLY = 2
PIECE = 32
VMEM = pl.BlockSpec(memory_space=pltpu.VMEM)
HBM = pl.BlockSpec(memory_space=pltpu.HBM)


def ring_order(count):
    if count % (2 * GRID_ROWS):
        return list(range(count))
    cols = count // GRID_ROWS
    cells = [(0, c) for c in range(cols)]
    for r in range(1, GRID_ROWS):
        inner = list(range(1, cols))
        cells += [(r, c) for c in (reversed(inner) if r % 2 else inner)]
    cells += [(r, 0) for r in range(GRID_ROWS - 1, 0, -1)]
    return [r * cols + c for r, c in cells]


def owner_at(order, step):
    me = lax.axis_index("tp")
    owner = jnp.int32(0)
    for place, index in enumerate(order):
        owner = jnp.where(me == index, order[(place - step) % len(order)], owner)
    return owner


def block_loads(order, steps, w_ref, held, sem, first=0):
    _, streams, width, _ = held.shape
    copies = []
    for b, step in enumerate(steps):
        start = pl.multiple_of(owner_at(order, step) * width, width)
        for s in range(streams):
            copies.append(
                pltpu.make_async_copy(
                    w_ref.at[first + s, pl.ds(start, width), :], held.at[b, s], sem.at[b, s]
                )
            )
    return copies


def add_products(xs, held, total, s, first=0):
    for c in range(0, total.shape[2], COLS):
        at = slice(c, c + COLS)
        terms = [
            jnp.dot(x, held[b, s, :, at], preferred_element_type=jnp.float32)
            for b, x in enumerate(xs)
        ]
        total[first + s, :, at] += sum(terms)


def add_held(xa_ref, xb_ref, held, total):
    @pl.loop(0, held.shape[1])
    def _(s):
        add_products([xa_ref[...], xb_ref[...]], held, total, s)


def spread(out_ref, value):
    groups, lanes = out_ref.shape[-2:]
    for g in range(groups):
        out_ref[..., g, :] = value[..., g * lanes : (g + 1) * lanes]


def first_kernel(order, steps, x_ref, w_ref, total, held, own, own_sem, held_sem):
    width = x_ref.shape[1]
    depth = min(DEPTH, width)
    start = pl.multiple_of(owner_at(order, 0) * width, width)
    chunks = [
        pltpu.make_async_copy(
            w_ref.at[:, pl.ds(start + k * depth, depth), :],
            own.at[:, pl.ds(k * depth, depth), :],
            own_sem.at[k],
        )
        for k in range(width // depth)
    ]
    ahead = block_loads(order, steps, w_ref, held, held_sem)
    for copy in chunks + ahead:
        copy.start()
    for k, copy in enumerate(chunks):
        copy.wait()
        at = slice(k * depth, (k + 1) * depth)
        for s in range(total.shape[0]):
            for c in range(0, total.shape[2], COLS):
                to = slice(c, c + COLS)
                term = jnp.dot(x_ref[:, at], own[s, at, to], preferred_element_type=jnp.float32)
                if k:
                    total[s, :, to] += term
                else:
                    total[s, :, to] = term
    for copy in ahead:
        copy.wait()


def middle_kernel(order, steps, xa_ref, xb_ref, held, w_ref, _, total, next_held, sem):
    ahead = block_loads(order, steps, w_ref, next_held, sem)
    for copy in ahead:
        copy.start()
    add_held(xa_ref, xb_ref, held, total)
    for copy in ahead:
        copy.wait()


def second_kernel(
    order, here, steps, xa_ref, xb_ref, held, w_ref, _, taps_in, decay, residue,
    total, next_held, taps, table, rest, rest_sem, sem,
):
    first = held.shape[1]
    late = block_loads(order, here, w_ref, rest, rest_sem, first)
    ahead = block_loads(order, steps, w_ref, next_held, sem)
    for copy in late + ahead:
        copy.start()
    rate = decay[...]
    rows = total.shape[1]
    for i, power in enumerate((1, rows, rows - 1, rows - 2)):
        spread(table.at[i], jnp.exp(-rate * power))
    spread(table.at[4], residue[...] * jnp.sqrt(1.0 - jnp.exp(-2.0 * rate)))
    spread(taps, taps_in[...])
    add_held(xa_ref, xb_ref, held, total)
    for copy in late:
        copy.wait()
    for s in range(rest.shape[1]):
        add_products([xa_ref[...], xb_ref[...]], rest, total, s, first)
    for copy in ahead:
        copy.wait()


def filtered(taps, p_ref, s, t):
    return (
        taps[0, s] * p_ref[s - 1, t]
        + taps[1, s] * p_ref[s - 1, t - 1]
        + taps[2, s] * p_ref[s - 1, t - 2]
    )


def last_kernel(xa_ref, xb_ref, held, taps, table, _, total, source, out_ref, p_ref, tail):
    x = jnp.concatenate([xa_ref[...], xb_ref[...]], axis=0)
    for s in range(total.shape[0]):
        add_products([x], held, total, s)
    rows, groups, lanes = source.shape
    modes = table.shape[1]
    for s in (1, 2):
        spread(p_ref.at[s - 1], rounded(total[s]))
    spread(tail, rounded(total[0, rows - 8 :]))
    rate = [table[0, n] for n in range(modes)]

    def step_row(t, state):
        u = filtered(taps, p_ref, 1, t) * filtered(taps, p_ref, 2, t)
        source[t] = u
        return [r * s + u for r, s in zip(rate, state)]

    state = [jnp.zeros((groups, lanes), jnp.float32)] * modes
    for t in range(2, 8):
        state = step_row(t, state)

    def eight(i, state):
        for j in range(8):
            state = step_row(i * 8 + j, state)
        return state

    state = lax.fori_loop(1, rows // 8, eight, state)
    for n in range(modes):
        out_ref[n] = state[n]
    for s in (1, 2):
        for j in range(2):
            out_ref[modes + (s - 1) * 2 + j] = p_ref[s - 1, j]
            out_ref[modes + 4 + s * 2 + j] = p_ref[s - 1, rows - 2 + j]
    for j in range(2):
        out_ref[modes + 4 + j] = tail[6 + j]


def rounded(value):
    return value.astype(jnp.bfloat16).astype(jnp.float32)


def tree_sum(terms):
    while len(terms) > 1:
        terms = [a + b for a, b in zip(terms[::2], terms[1::2])] + terms[len(terms) & ~1 :]
    return terms[0]


def local_kernel(total, source, taps, table, query, response, p_ref):
    rows, groups, lanes = source.shape
    modes = table.shape[1]
    spread(p_ref, rounded(total[0]))
    for j in range(2):
        query[j] = p_ref[j]

    def step_row(t, state):
        query[t] = taps[0, 0] * p_ref[t] + taps[1, 0] * p_ref[t - 1] + taps[2, 0] * p_ref[t - 2]
        u = source[t]
        state = [table[0, n] * state[n] + u for n in range(modes)]
        response[t] = tree_sum([table[4, n] * state[n] for n in range(modes)])
        return state

    state = [jnp.zeros((groups, lanes), jnp.float32)] * modes
    for t in range(2, 8):
        state = step_row(t, state)

    def eight(i, state):
        for j in range(8):
            state = step_row(i * 8 + j, state)
        return state

    lax.fori_loop(1, rows // 8, eight, state)


def edge(taps, s, first, second, before, last):
    return (
        taps[0, s] * first + taps[1, s] * last + taps[2, s] * before,
        taps[0, s] * second + taps[1, s] * first + taps[2, s] * last,
    )


def lead_sources(taps, heads, rims):
    one = edge(taps, 1, heads[0], heads[1], rims[2], rims[3])
    two = edge(taps, 2, heads[2], heads[3], rims[4], rims[5])
    return one[0] * two[0], one[1] * two[1]


class Summary:
    def __init__(self, rows, modes):
        self.state = rows[:modes]
        self.heads = rows[modes : modes + 4]
        self.rims = rows[modes + 4 :]

    @classmethod
    def read(cls, ref, modes):
        return cls([ref[i] for i in range(ref.shape[0])], modes)

    @classmethod
    def chosen(cls, odd, when_odd, when_even, modes):
        pairs = zip(when_odd.rows(), when_even.rows())
        return cls([jnp.where(odd, a, b) for a, b in pairs], modes)

    def rows(self):
        return self.state + self.heads + self.rims

    def complete(self, taps, rims, by_first, by_second):
        u0, u1 = lead_sources(taps, self.heads, rims)
        return [x + f * u0 + g * u1 for x, f, g in zip(self.state, by_first, by_second)]


def powers(table):
    return [[table[i, n] for n in range(table.shape[1])] for i in range(table.shape[0])]


def chip_kernel(lone, local, partner, taps, table, out_ref):
    modes = table.shape[1]
    odd = lax.rem(lax.axis_index("ctx"), 2) == 1
    mine, other = Summary.read(local, modes), Summary.read(partner, modes)
    first = Summary.chosen(odd, other, mine, modes)
    second = Summary.chosen(odd, mine, other, modes)
    _, block, less_one, less_two, _ = powers(table)
    start, heads = first.state, first.heads
    if lone:
        start, heads = first.complete(taps, [jnp.zeros_like(heads[0])] * 6, less_one, less_two), []
    end = second.complete(taps, first.rims, less_one, less_two)
    joined = [d * x + y for d, x, y in zip(block, start, end)]
    for i, value in enumerate(joined + heads + second.rims):
        out_ref[i] = value


def final_kernel(lone, count, *refs):
    sent = refs[:count]
    local, partner, query, response, taps, table, out_ref, work, rounded_out, out_sem = refs[count:]
    rows, groups, lanes = query.shape
    modes = table.shape[1]
    zero = jnp.zeros((groups, lanes), jnp.float32)
    index = lax.axis_index("ctx")
    odd = lax.rem(index, 2) == 1
    _, block, less_one, less_two, _ = powers(table)
    values = [
        [jnp.where(index >= 2 * (d + 1), ref[i], zero) for i in range(ref.shape[0])]
        for d, ref in enumerate(sent)
    ]
    rims = [value[-6:] for value in values] + [[zero] * 6]
    state = [zero] * modes
    for d in reversed(range(count)):
        end = values[d][:modes]
        if not lone:
            end = Summary(values[d], modes).complete(
                taps,
                rims[d + 1],
                [a * b for a, b in zip(block, less_one)],
                [a * b for a, b in zip(block, less_two)],
            )
        state = [d * d * x + y for d, x, y in zip(block, state, end)]
    before = Summary.read(partner, modes)
    end = before.complete(taps, rims[0], less_one, less_two)
    state = [jnp.where(odd, d * x + y, x) for d, x, y in zip(block, state, end)]
    rim = [jnp.where(odd, a, b) for a, b in zip(before.rims, rims[0])]

    leads = lead_sources(taps, Summary.read(local, modes).heads, rim)
    heads = edge(taps, 0, query[0], query[1], rim[0], rim[1])
    for t, u in enumerate(leads):
        state = [table[0, n] * state[n] + u for n in range(modes)]
        work[t] = heads[t] * tree_sum([table[4, n] * state[n] for n in range(modes)])
    carried = [table[4, n] * state[n] for n in range(modes)]

    def row(t, carried):
        carried = [table[0, n] * carried[n] for n in range(modes)]
        work[t] = query[t] * (response[t] + tree_sum(carried))
        return carried

    def eight(i, carried):
        for j in range(8):
            carried = row(i * 8 + j, carried)
        return carried

    for t in range(2, 8):
        carried = row(t, carried)
    copies = []
    for i in range(rows // PIECE):
        at = slice(i * PIECE, (i + 1) * PIECE)
        first = 0 if i else 1
        carried = lax.fori_loop(i * PIECE // 8 + first, (i + 1) * PIECE // 8, eight, carried)
        for g in range(groups):
            rounded_out[at, g * lanes : (g + 1) * lanes] = work[at, g, :].astype(out_ref.dtype)
        copies.append(pltpu.make_async_copy(rounded_out.at[at], out_ref.at[at], out_sem.at[i]))
        copies[-1].start()
    for copy in copies:
        copy.wait()


def on_device(tokens, in_weight, filter_taps, decay_rate, residue):
    rows, width = tokens.shape
    streams, chans = in_weight.shape[1:]
    lags = filter_taps.shape[0]
    modes = decay_rate.shape[0]
    groups = chans // LANES
    tp, ctx = lax.axis_size("tp"), lax.axis_size("ctx")
    order = ring_order(tp)
    weight = jnp.transpose(in_weight, (1, 0, 2))
    half = tp // 2
    ahead = [(order[i], order[(i + 1) % tp]) for i in range(tp)]
    back = [(b, a) for a, b in ahead]

    def f32(*shape):
        return jax.ShapeDtypeStruct(shape, jnp.float32)

    def held(count, streams=streams):
        return jax.ShapeDtypeStruct((count, streams, width, chans), jnp.bfloat16)

    def loads(step):
        return [step, -step] if step < half else [step]

    sums = f32(streams, rows, chans)
    wide = f32(rows, groups, LANES)
    params = pltpu.CompilerParams(vmem_limit_bytes=12 << 20)
    cost = pl.CostEstimate(flops=0, bytes_accessed=16 << 20, transcendentals=0)

    depth = min(DEPTH, width)
    total, weights = pl.pallas_call(
        functools.partial(first_kernel, order, loads(1)),
        out_shape=[sums, held(2, EARLY)],
        in_specs=[VMEM, HBM],
        out_specs=[VMEM] * 2,
        scratch_shapes=[
            pltpu.VMEM((streams, width, chans), jnp.bfloat16),
            pltpu.SemaphoreType.DMA((width // depth,)),
            pltpu.SemaphoreType.DMA((2, EARLY)),
        ],
        compiler_params=params,
        cost_estimate=cost,
        name="project_own",
    )(tokens, weight)
    fore, aft = tokens, tokens
    for step in range(1, half):
        fore = lax.ppermute(fore, "tp", ahead)
        aft = lax.ppermute(aft, "tp", back)
        fore, aft, total, weights = lax.optimization_barrier((fore, aft, total, weights))
        coming = loads(step + 1)
        body, extra, made, scratch = functools.partial(middle_kernel, order), [], [], []
        if step == 1:
            body = functools.partial(second_kernel, order, loads(1))
            extra = [filter_taps, decay_rate, residue]
            made = [f32(lags, streams, groups, LANES), f32(5, modes, groups, LANES)]
            scratch = [
                pltpu.VMEM((2, streams - EARLY, width, chans), jnp.bfloat16),
                pltpu.SemaphoreType.DMA((2, streams - EARLY)),
            ]
        total, weights, *made = pl.pallas_call(
            functools.partial(body, coming),
            out_shape=[sums, held(len(coming))] + made,
            in_specs=[VMEM, VMEM, VMEM, HBM, VMEM] + [VMEM] * len(extra),
            out_specs=[VMEM] * (2 + len(made)),
            scratch_shapes=scratch + [pltpu.SemaphoreType.DMA((len(coming), streams))],
            input_output_aliases={4: 0},
            compiler_params=params,
            cost_estimate=cost,
            name="project_pair",
        )(fore, aft, weights, weight, total, *extra)
        if made:
            taps, table = made
    fore = lax.ppermute(fore[: rows // 2], "tp", ahead)
    aft = lax.ppermute(aft[rows // 2 :], "tp", back)
    total, source, local = pl.pallas_call(
        last_kernel,
        out_shape=[sums, wide, f32(modes + EDGE, groups, LANES)],
        in_specs=[VMEM] * 6,
        out_specs=[VMEM] * 3,
        scratch_shapes=[
            pltpu.VMEM((2, rows, groups, LANES), jnp.float32),
            pltpu.VMEM((8, groups, LANES), jnp.float32),
        ],
        input_output_aliases={5: 0},
        compiler_params=params,
        cost_estimate=cost,
        name="project_last",
    )(fore, aft, weights, taps, table, total)

    partner = lax.ppermute(local, "ctx", [(j, j ^ 1) for j in range(ctx)])
    lone = ctx == 4
    chip = pl.pallas_call(
        functools.partial(chip_kernel, lone),
        out_shape=f32(modes + (6 if lone else EDGE), groups, LANES),
        in_specs=[VMEM] * 4,
        out_specs=VMEM,
        compiler_params=params,
        name="chip_state",
    )(local, partner, taps, table)
    sent = [
        lax.ppermute(chip, "ctx", [(j, (j + d) % ctx) for j in range(ctx)])
        for d in range(2, ctx, 2)
    ]
    query, response = pl.pallas_call(
        local_kernel,
        out_shape=[wide, wide],
        in_specs=[VMEM] * 4,
        out_specs=[VMEM] * 2,
        scratch_shapes=[pltpu.VMEM((rows, groups, LANES), jnp.float32)],
        compiler_params=params,
        cost_estimate=cost,
        name="local_response",
    )(total, source, taps, table)
    return pl.pallas_call(
        functools.partial(final_kernel, lone, len(sent)),
        out_shape=jax.ShapeDtypeStruct((rows, chans), jnp.bfloat16),
        in_specs=[VMEM] * (len(sent) + 6),
        out_specs=HBM,
        scratch_shapes=[
            pltpu.VMEM((rows, groups, LANES), jnp.float32),
            pltpu.VMEM((rows, chans), jnp.bfloat16),
            pltpu.SemaphoreType.DMA((rows // PIECE,)),
        ],
        compiler_params=params,
        name="carried_response",
    )(*sent, local, partner, query, response, taps, table)


def solution(mesh):
    return jax.shard_map(
        on_device,
        mesh=mesh,
        in_specs=(
            P("ctx", "tp"),
            P(None, None, "tp"),
            P(None, None, "tp"),
            P(None, "tp"),
            P(None, "tp"),
        ),
        out_specs=P("ctx", "tp"),
        check_vma=False,
    )
```

```python
import functools

import jax
import jax.numpy as jnp
from jax import lax
from jax.experimental import pallas as pl
from jax.experimental.pallas import tpu as pltpu
from jax.sharding import PartitionSpec as P

LANES = 128
COLS = 256
DEPTH = 256
GRID_ROWS = 4
EDGE = 10
EARLY = 2
PIECE = 32
VMEM = pl.BlockSpec(memory_space=pltpu.VMEM)
HBM = pl.BlockSpec(memory_space=pltpu.HBM)


def ring_order(count):
    if count % (2 * GRID_ROWS):
        return list(range(count))
    cols = count // GRID_ROWS
    cells = [(0, c) for c in range(cols)]
    for r in range(1, GRID_ROWS):
        inner = list(range(1, cols))
        cells += [(r, c) for c in (reversed(inner) if r % 2 else inner)]
    cells += [(r, 0) for r in range(GRID_ROWS - 1, 0, -1)]
    return [r * cols + c for r, c in cells]


def owner_at(order, step):
    me = lax.axis_index("tp")
    owner = jnp.int32(0)
    for place, index in enumerate(order):
        owner = jnp.where(me == index, order[(place - step) % len(order)], owner)
    return owner


def block_loads(order, steps, w_ref, held, sem, first=0):
    _, streams, width, _ = held.shape
    copies = []
    for b, step in enumerate(steps):
        start = pl.multiple_of(owner_at(order, step) * width, width)
        for s in range(streams):
            copies.append(
                pltpu.make_async_copy(
                    w_ref.at[first + s, pl.ds(start, width), :], held.at[b, s], sem.at[b, s]
                )
            )
    return copies


def add_products(xs, held, total, s, first=0):
    for c in range(0, total.shape[2], COLS):
        at = slice(c, c + COLS)
        terms = [
            jnp.dot(x, held[b, s, :, at], preferred_element_type=jnp.float32)
            for b, x in enumerate(xs)
        ]
        total[first + s, :, at] += sum(terms)


def joined(parts):
    return jnp.concatenate([part[...] for part in parts], axis=0)


def spread(out_ref, value):
    groups, lanes = out_ref.shape[-2:]
    for g in range(groups):
        out_ref[..., g, :] = value[..., g * lanes : (g + 1) * lanes]


def first_kernel(order, steps, x_ref, w_ref, total, held, own, own_sem, held_sem):
    width = x_ref.shape[1]
    depth = min(DEPTH, width)
    start = pl.multiple_of(owner_at(order, 0) * width, width)
    chunks = [
        pltpu.make_async_copy(
            w_ref.at[:, pl.ds(start + k * depth, depth), :],
            own.at[:, pl.ds(k * depth, depth), :],
            own_sem.at[k],
        )
        for k in range(width // depth)
    ]
    ahead = block_loads(order, steps, w_ref, held, held_sem)
    for copy in chunks + ahead:
        copy.start()
    for k, copy in enumerate(chunks):
        copy.wait()
        at = slice(k * depth, (k + 1) * depth)
        for s in range(total.shape[0]):
            for c in range(0, total.shape[2], COLS):
                to = slice(c, c + COLS)
                term = jnp.dot(x_ref[:, at], own[s, at, to], preferred_element_type=jnp.float32)
                if k:
                    total[s, :, to] += term
                else:
                    total[s, :, to] = term
    for copy in ahead:
        copy.wait()


def middle_kernel(order, here, steps, count, inputs_count, *refs):
    fore, aft = refs[:count], refs[count : 2 * count]
    held, w_ref, _, *refs = refs[2 * count :]
    *refs, rest, rest_sem, sem = refs
    inputs, (total, next_held, *made) = refs[:inputs_count], refs[inputs_count:]
    first = held.shape[1]
    late = block_loads(order, here, w_ref, rest, rest_sem, first)
    ahead = block_loads(order, steps, w_ref, next_held, sem)
    for copy in late + ahead:
        copy.start()
    if made:
        make_tables(*inputs, *made, total.shape[1])

    @pl.loop(0, first)
    def _(s):
        add_products([joined(fore), joined(aft)], held, total, s)

    for copy in late:
        copy.wait()

    @pl.loop(0, rest.shape[1])
    def _(s):
        add_products([joined(fore), joined(aft)], rest, total, s, first)

    for copy in ahead:
        copy.wait()


def make_tables(taps_in, decay, residue, taps, table, rows):
    rate = decay[...]
    for i, power in enumerate((1, rows, rows - 1, rows - 2)):
        spread(table.at[i], jnp.exp(-rate * power))
    spread(table.at[4], residue[...] * jnp.sqrt(1.0 - jnp.exp(-2.0 * rate)))
    spread(taps, taps_in[...])


def filtered(taps, p_ref, s, t):
    return (
        taps[0, s] * p_ref[s - 1, t]
        + taps[1, s] * p_ref[s - 1, t - 1]
        + taps[2, s] * p_ref[s - 1, t - 2]
    )


def last_kernel(count, *refs):
    x = joined(refs[:count])
    held, taps, table, _, total, source, out_ref, p_ref, tail = refs[count:]
    for s in range(total.shape[0]):
        add_products([x], held, total, s)
    rows, groups, lanes = source.shape
    modes = table.shape[1]
    for s in (1, 2):
        spread(p_ref.at[s - 1], rounded(total[s]))
    spread(tail, rounded(total[0, rows - 8 :]))
    rate = [table[0, n] for n in range(modes)]

    def step_row(t, state):
        u = filtered(taps, p_ref, 1, t) * filtered(taps, p_ref, 2, t)
        source[t] = u
        return [r * s + u for r, s in zip(rate, state)]

    state = [jnp.zeros((groups, lanes), jnp.float32)] * modes
    for t in range(2, 8):
        state = step_row(t, state)

    def eight(i, state):
        for j in range(8):
            state = step_row(i * 8 + j, state)
        return state

    state = lax.fori_loop(1, rows // 8, eight, state)
    for n in range(modes):
        out_ref[n] = state[n]
    for s in (1, 2):
        for j in range(2):
            out_ref[modes + (s - 1) * 2 + j] = p_ref[s - 1, j]
            out_ref[modes + 4 + s * 2 + j] = p_ref[s - 1, rows - 2 + j]
    for j in range(2):
        out_ref[modes + 4 + j] = tail[6 + j]


def rounded(value):
    return value.astype(jnp.bfloat16).astype(jnp.float32)


def tree_sum(terms):
    while len(terms) > 1:
        terms = [a + b for a, b in zip(terms[::2], terms[1::2])] + terms[len(terms) & ~1 :]
    return terms[0]


def local_kernel(total, source, taps, table, query, response, p_ref):
    rows, groups, lanes = source.shape
    modes = table.shape[1]
    spread(p_ref, rounded(total[0]))
    for j in range(2):
        query[j] = p_ref[j]

    def step_row(t, state):
        query[t] = taps[0, 0] * p_ref[t] + taps[1, 0] * p_ref[t - 1] + taps[2, 0] * p_ref[t - 2]
        u = source[t]
        state = [table[0, n] * state[n] + u for n in range(modes)]
        response[t] = tree_sum([table[4, n] * state[n] for n in range(modes)])
        return state

    state = [jnp.zeros((groups, lanes), jnp.float32)] * modes
    for t in range(2, 8):
        state = step_row(t, state)

    def eight(i, state):
        for j in range(8):
            state = step_row(i * 8 + j, state)
        return state

    lax.fori_loop(1, rows // 8, eight, state)


def edge(taps, s, first, second, before, last):
    return (
        taps[0, s] * first + taps[1, s] * last + taps[2, s] * before,
        taps[0, s] * second + taps[1, s] * first + taps[2, s] * last,
    )


def lead_sources(taps, heads, rims):
    one = edge(taps, 1, heads[0], heads[1], rims[2], rims[3])
    two = edge(taps, 2, heads[2], heads[3], rims[4], rims[5])
    return one[0] * two[0], one[1] * two[1]


class Summary:
    def __init__(self, rows, modes):
        self.state = rows[:modes]
        self.heads = rows[modes : modes + 4]
        self.rims = rows[modes + 4 :]

    @classmethod
    def read(cls, ref, modes):
        return cls([ref[i] for i in range(ref.shape[0])], modes)

    @classmethod
    def chosen(cls, odd, when_odd, when_even, modes):
        pairs = zip(when_odd.rows(), when_even.rows())
        return cls([jnp.where(odd, a, b) for a, b in pairs], modes)

    def rows(self):
        return self.state + self.heads + self.rims

    def complete(self, taps, rims, by_first, by_second):
        u0, u1 = lead_sources(taps, self.heads, rims)
        return [x + f * u0 + g * u1 for x, f, g in zip(self.state, by_first, by_second)]


def powers(table):
    return [[table[i, n] for n in range(table.shape[1])] for i in range(table.shape[0])]


def chip_kernel(lone, local, partner, taps, table, out_ref):
    modes = table.shape[1]
    odd = lax.rem(lax.axis_index("ctx"), 2) == 1
    mine, other = Summary.read(local, modes), Summary.read(partner, modes)
    first = Summary.chosen(odd, other, mine, modes)
    second = Summary.chosen(odd, mine, other, modes)
    _, block, less_one, less_two, _ = powers(table)
    start, heads = first.state, first.heads
    if lone:
        start, heads = first.complete(taps, [jnp.zeros_like(heads[0])] * 6, less_one, less_two), []
    end = second.complete(taps, first.rims, less_one, less_two)
    joined = [d * x + y for d, x, y in zip(block, start, end)]
    for i, value in enumerate(joined + heads + second.rims):
        out_ref[i] = value


def final_kernel(lone, count, *refs):
    sent = refs[:count]
    local, partner, query, response, taps, table, out_ref, work, rounded_out, out_sem = refs[count:]
    rows, groups, lanes = query.shape
    modes = table.shape[1]
    zero = jnp.zeros((groups, lanes), jnp.float32)
    index = lax.axis_index("ctx")
    odd = lax.rem(index, 2) == 1
    _, block, less_one, less_two, _ = powers(table)
    values = [
        [jnp.where(index >= 2 * (d + 1), ref[i], zero) for i in range(ref.shape[0])]
        for d, ref in enumerate(sent)
    ]
    rims = [value[-6:] for value in values] + [[zero] * 6]
    state = [zero] * modes
    for d in reversed(range(count)):
        end = values[d][:modes]
        if not lone:
            end = Summary(values[d], modes).complete(
                taps,
                rims[d + 1],
                [a * b for a, b in zip(block, less_one)],
                [a * b for a, b in zip(block, less_two)],
            )
        state = [d * d * x + y for d, x, y in zip(block, state, end)]
    before = Summary.read(partner, modes)
    end = before.complete(taps, rims[0], less_one, less_two)
    state = [jnp.where(odd, d * x + y, x) for d, x, y in zip(block, state, end)]
    rim = [jnp.where(odd, a, b) for a, b in zip(before.rims, rims[0])]

    leads = lead_sources(taps, Summary.read(local, modes).heads, rim)
    heads = edge(taps, 0, query[0], query[1], rim[0], rim[1])
    for t, u in enumerate(leads):
        state = [table[0, n] * state[n] + u for n in range(modes)]
        work[t] = heads[t] * tree_sum([table[4, n] * state[n] for n in range(modes)])
    carried = [table[4, n] * state[n] for n in range(modes)]

    def row(t, carried):
        carried = [table[0, n] * carried[n] for n in range(modes)]
        work[t] = query[t] * (response[t] + tree_sum(carried))
        return carried

    def eight(i, carried):
        for j in range(8):
            carried = row(i * 8 + j, carried)
        return carried

    for t in range(2, 8):
        carried = row(t, carried)
    copies = []
    for i in range(rows // PIECE):
        at = slice(i * PIECE, (i + 1) * PIECE)
        first = 0 if i else 1
        carried = lax.fori_loop(i * PIECE // 8 + first, (i + 1) * PIECE // 8, eight, carried)
        for g in range(groups):
            rounded_out[at, g * lanes : (g + 1) * lanes] = work[at, g, :].astype(out_ref.dtype)
        copies.append(pltpu.make_async_copy(rounded_out.at[at], out_ref.at[at], out_sem.at[i]))
        copies[-1].start()
    for copy in copies:
        copy.wait()


def on_device(tokens, in_weight, filter_taps, decay_rate, residue):
    rows, width = tokens.shape
    streams, chans = in_weight.shape[1:]
    lags = filter_taps.shape[0]
    modes = decay_rate.shape[0]
    groups = chans // LANES
    tp, ctx = lax.axis_size("tp"), lax.axis_size("ctx")
    order = ring_order(tp)
    weight = jnp.transpose(in_weight, (1, 0, 2))
    half = tp // 2
    ahead = [(order[i], order[(i + 1) % tp]) for i in range(tp)]
    back = [(b, a) for a, b in ahead]

    def f32(*shape):
        return jax.ShapeDtypeStruct(shape, jnp.float32)

    def held(count, streams=streams):
        return jax.ShapeDtypeStruct((count, streams, width, chans), jnp.bfloat16)

    def loads(step):
        return [step, -step] if step < half else [step]

    sums = f32(streams, rows, chans)
    wide = f32(rows, groups, LANES)
    params = pltpu.CompilerParams(vmem_limit_bytes=12 << 20)
    cost = pl.CostEstimate(flops=0, bytes_accessed=16 << 20, transcendentals=0)

    depth = min(DEPTH, width)
    total, weights = pl.pallas_call(
        functools.partial(first_kernel, order, loads(1)),
        out_shape=[sums, held(2, EARLY)],
        in_specs=[VMEM, HBM],
        out_specs=[VMEM] * 2,
        scratch_shapes=[
            pltpu.VMEM((streams, width, chans), jnp.bfloat16),
            pltpu.SemaphoreType.DMA((width // depth,)),
            pltpu.SemaphoreType.DMA((2, EARLY)),
        ],
        compiler_params=params,
        cost_estimate=cost,
        name="project_own",
    )(tokens, weight)
    def passed(parts, pairs):
        return [lax.ppermute(part, "tp", pairs) for part in parts]

    def halves(part):
        middle = part.shape[0] // 2
        return [part[:middle], part[middle:]]

    fore, aft = [tokens], [tokens]
    for step in range(1, half):
        fore, aft = passed(fore, ahead), passed(aft, back)
        fore, aft, total, weights = lax.optimization_barrier((fore, aft, total, weights))
        if step == 1:
            fore, aft = halves(fore[0]), halves(aft[0])
        coming = loads(step + 1)
        extra = [filter_taps, decay_rate, residue] if step == 1 else []
        made = [f32(lags, streams, groups, LANES), f32(5, modes, groups, LANES)] if step == 1 else []
        early = EARLY if step + 1 < half else streams
        total, weights, *made = pl.pallas_call(
            functools.partial(
                middle_kernel, order, loads(step), coming, len(fore), len(extra)
            ),
            out_shape=[sums, held(len(coming), early)] + made,
            in_specs=[VMEM] * (2 * len(fore) + 1) + [HBM, VMEM] + [VMEM] * len(extra),
            out_specs=[VMEM] * (2 + len(made)),
            scratch_shapes=[
                pltpu.VMEM((2, streams - EARLY, width, chans), jnp.bfloat16),
                pltpu.SemaphoreType.DMA((2, streams - EARLY)),
                pltpu.SemaphoreType.DMA((len(coming), early)),
            ],
            input_output_aliases={2 * len(fore) + 2: 0},
            compiler_params=params,
            cost_estimate=cost,
            name="project_pair",
        )(*fore, *aft, weights, weight, total, *extra)
        if made:
            taps, table = made
    last = passed(halves(fore[0]), ahead) + passed(halves(aft[1]), back)
    total, source, local = pl.pallas_call(
        functools.partial(last_kernel, len(last)),
        out_shape=[sums, wide, f32(modes + EDGE, groups, LANES)],
        in_specs=[VMEM] * (len(last) + 4),
        out_specs=[VMEM] * 3,
        scratch_shapes=[
            pltpu.VMEM((2, rows, groups, LANES), jnp.float32),
            pltpu.VMEM((8, groups, LANES), jnp.float32),
        ],
        input_output_aliases={len(last) + 3: 0},
        compiler_params=params,
        cost_estimate=cost,
        name="project_last",
    )(*last, weights, taps, table, total)

    partner = lax.ppermute(local, "ctx", [(j, j ^ 1) for j in range(ctx)])
    lone = ctx == 4
    chip = pl.pallas_call(
        functools.partial(chip_kernel, lone),
        out_shape=f32(modes + (6 if lone else EDGE), groups, LANES),
        in_specs=[VMEM] * 4,
        out_specs=VMEM,
        compiler_params=params,
        name="chip_state",
    )(local, partner, taps, table)
    sent = [
        lax.ppermute(chip, "ctx", [(j, (j + d) % ctx) for j in range(ctx)])
        for d in range(2, ctx, 2)
    ]
    query, response = pl.pallas_call(
        local_kernel,
        out_shape=[wide, wide],
        in_specs=[VMEM] * 4,
        out_specs=[VMEM] * 2,
        scratch_shapes=[pltpu.VMEM((rows, groups, LANES), jnp.float32)],
        compiler_params=params,
        cost_estimate=cost,
        name="local_response",
    )(total, source, taps, table)
    return pl.pallas_call(
        functools.partial(final_kernel, lone, len(sent)),
        out_shape=jax.ShapeDtypeStruct((rows, chans), jnp.bfloat16),
        in_specs=[VMEM] * (len(sent) + 6),
        out_specs=HBM,
        scratch_shapes=[
            pltpu.VMEM((rows, groups, LANES), jnp.float32),
            pltpu.VMEM((rows, chans), jnp.bfloat16),
            pltpu.SemaphoreType.DMA((rows // PIECE,)),
        ],
        compiler_params=params,
        name="carried_response",
    )(*sent, local, partner, query, response, taps, table)


def solution(mesh):
    return jax.shard_map(
        on_device,
        mesh=mesh,
        in_specs=(
            P("ctx", "tp"),
            P(None, None, "tp"),
            P(None, None, "tp"),
            P(None, "tp"),
            P(None, "tp"),
        ),
        out_specs=P("ctx", "tp"),
        check_vma=False,
    )
```

```python
import functools

import jax
import jax.numpy as jnp
from jax import lax
from jax.experimental import pallas as pl
from jax.experimental.pallas import tpu as pltpu
from jax.sharding import PartitionSpec as P

LANES = 128
COLS = 256
DEPTH = 256
GRID_ROWS = 4
EDGE = 10
UNROLL = 16
PIECE = 32
VMEM = pl.BlockSpec(memory_space=pltpu.VMEM)
HBM = pl.BlockSpec(memory_space=pltpu.HBM)


def ring_order(count):
    if count % (2 * GRID_ROWS):
        return list(range(count))
    cols = count // GRID_ROWS
    cells = [(0, c) for c in range(cols)]
    for r in range(1, GRID_ROWS):
        inner = list(range(1, cols))
        cells += [(r, c) for c in (reversed(inner) if r % 2 else inner)]
    cells += [(r, 0) for r in range(GRID_ROWS - 1, 0, -1)]
    return [r * cols + c for r, c in cells]


def owner_at(order, step):
    me = lax.axis_index("tp")
    owner = jnp.int32(0)
    for place, index in enumerate(order):
        owner = jnp.where(me == index, order[(place - step) % len(order)], owner)
    return owner


def piece_loads(order, steps, pieces, w_ref, target, sem):
    width = w_ref.shape[1] // len(order)
    starts = [pl.multiple_of(owner_at(order, step) * width, width) for step in steps]
    return [
        pltpu.make_async_copy(
            w_ref.at[s, pl.ds(starts[b], width), :], target(i, b, s), sem.at[i]
        )
        for i, (b, s) in enumerate(pieces)
    ]


def add_products(xs, weights, total, s):
    for c in range(0, total.shape[2], COLS):
        at = slice(c, c + COLS)
        terms = [
            jnp.dot(x, weights(b, at), preferred_element_type=jnp.float32) for b, x in enumerate(xs)
        ]
        total[s, :, at] += sum(terms)


def spread(out_ref, value):
    groups, lanes = out_ref.shape[-2:]
    for g in range(groups):
        out_ref[..., g, :] = value[..., g * lanes : (g + 1) * lanes]


def first_kernel(order, steps, pieces, x_ref, w_ref, total, held, own, own_sem, held_sem):
    width = x_ref.shape[1]
    depth = min(DEPTH, width)
    start = pl.multiple_of(owner_at(order, 0) * width, width)
    chunks = [
        pltpu.make_async_copy(
            w_ref.at[:, pl.ds(start + k * depth, depth), :],
            own.at[:, pl.ds(k * depth, depth), :],
            own_sem.at[k],
        )
        for k in range(width // depth)
    ]
    ahead = piece_loads(order, steps, pieces, w_ref, lambda i, b, s: held.at[b, s], held_sem)
    for copy in chunks + ahead:
        copy.start()
    for k, copy in enumerate(chunks):
        copy.wait()
        at = slice(k * depth, (k + 1) * depth)
        for s in range(total.shape[0]):
            for c in range(0, total.shape[2], COLS):
                to = slice(c, c + COLS)
                term = jnp.dot(x_ref[:, at], own[s, at, to], preferred_element_type=jnp.float32)
                if k:
                    total[s, :, to] += term
                else:
                    total[s, :, to] = term
    for copy in ahead:
        copy.wait()


def middle_kernel(order, here, missing, steps, pieces, inputs_count, fore, aft, held, w_ref, _, *refs):
    *refs, rest, rest_sem, sem = refs
    inputs, (total, next_held, *made) = refs[:inputs_count], refs[inputs_count:]
    late = piece_loads(order, here, missing, w_ref, lambda i, b, s: rest.at[i], rest_sem)
    ahead = piece_loads(order, steps, pieces, w_ref, lambda i, b, s: next_held.at[b, s], sem)
    for copy in late + ahead:
        copy.start()
    if made:
        make_tables(*inputs, *made, total.shape[1])
    whole = min([s for _, s in missing], default=held.shape[1])

    @pl.loop(0, whole)
    def _(s):
        add_products([fore[...], aft[...]], lambda b, at: held[b, s, :, at], total, s)

    for copy in late:
        copy.wait()

    for s in range(whole, held.shape[1]):

        def weights(b, at):
            if (b, s) in missing:
                return rest[missing.index((b, s)), :, at]
            return held[b, s, :, at]

        add_products([fore[...], aft[...]], weights, total, s)

    for copy in ahead:
        copy.wait()


def half_kernel(x_ref, held, _, total):
    depth = x_ref.shape[1]
    for s in range(total.shape[0]):
        add_products([x_ref[...]], lambda b, at: held[0, s, :depth, at], total, s)


def make_tables(taps_in, decay, residue, taps, table, rows):
    rate = decay[...]
    for i, power in enumerate((1, rows, rows - 1, rows - 2)):
        spread(table.at[i], jnp.exp(-rate * power))
    spread(table.at[4], residue[...] * jnp.sqrt(1.0 - jnp.exp(-2.0 * rate)))
    spread(taps, taps_in[...])


def over_rows(step, start, stop, carry):
    aligned = -(-start // UNROLL) * UNROLL
    for t in range(start, aligned):
        carry = step(t, carry)

    def group(i, carry):
        for j in range(UNROLL):
            carry = step(i * UNROLL + j, carry)
        return carry

    return lax.fori_loop(aligned // UNROLL, stop // UNROLL, group, carry)


def filtered(taps, p_ref, s, t):
    return (
        taps[0, s] * p_ref[s - 1, t]
        + taps[1, s] * p_ref[s - 1, t - 1]
        + taps[2, s] * p_ref[s - 1, t - 2]
    )


def last_kernel(x_ref, held, taps, table, _, total, source, out_ref, p_ref, tail):
    depth = x_ref.shape[1]
    for s in range(total.shape[0]):
        add_products([x_ref[...]], lambda b, at: held[0, s, depth:, at], total, s)
    rows, groups, lanes = source.shape
    modes = table.shape[1]
    for s in (1, 2):
        spread(p_ref.at[s - 1], rounded(total[s]))
    spread(tail, rounded(total[0, rows - 8 :]))
    rate = [table[0, n] for n in range(modes)]

    def step_row(t, state):
        u = filtered(taps, p_ref, 1, t) * filtered(taps, p_ref, 2, t)
        source[t] = u
        return [r * s + u for r, s in zip(rate, state)]

    state = [jnp.zeros((groups, lanes), jnp.float32)] * modes
    state = over_rows(step_row, 2, rows, state)
    for n in range(modes):
        out_ref[n] = state[n]
    for s in (1, 2):
        for j in range(2):
            out_ref[modes + (s - 1) * 2 + j] = p_ref[s - 1, j]
            out_ref[modes + 4 + s * 2 + j] = p_ref[s - 1, rows - 2 + j]
    for j in range(2):
        out_ref[modes + 4 + j] = tail[6 + j]


def rounded(value):
    return value.astype(jnp.bfloat16).astype(jnp.float32)


def tree_sum(terms):
    while len(terms) > 1:
        terms = [a + b for a, b in zip(terms[::2], terms[1::2])] + terms[len(terms) & ~1 :]
    return terms[0]


def local_kernel(total, source, taps, table, query, response, p_ref):
    rows, groups, lanes = source.shape
    modes = table.shape[1]
    spread(p_ref, rounded(total[0]))
    for j in range(2):
        query[j] = p_ref[j]

    def step_row(t, state):
        query[t] = taps[0, 0] * p_ref[t] + taps[1, 0] * p_ref[t - 1] + taps[2, 0] * p_ref[t - 2]
        u = source[t]
        state = [table[0, n] * state[n] + u for n in range(modes)]
        response[t] = tree_sum([table[4, n] * state[n] for n in range(modes)])
        return state

    state = [jnp.zeros((groups, lanes), jnp.float32)] * modes
    over_rows(step_row, 2, rows, state)


def edge(taps, s, first, second, before, last):
    return (
        taps[0, s] * first + taps[1, s] * last + taps[2, s] * before,
        taps[0, s] * second + taps[1, s] * first + taps[2, s] * last,
    )


def lead_sources(taps, heads, rims):
    one = edge(taps, 1, heads[0], heads[1], rims[2], rims[3])
    two = edge(taps, 2, heads[2], heads[3], rims[4], rims[5])
    return one[0] * two[0], one[1] * two[1]


class Summary:
    def __init__(self, rows, modes):
        self.state = rows[:modes]
        self.heads = rows[modes : modes + 4]
        self.rims = rows[modes + 4 :]

    @classmethod
    def read(cls, ref, modes):
        return cls([ref[i] for i in range(ref.shape[0])], modes)

    @classmethod
    def chosen(cls, odd, when_odd, when_even, modes):
        pairs = zip(when_odd.rows(), when_even.rows())
        return cls([jnp.where(odd, a, b) for a, b in pairs], modes)

    def rows(self):
        return self.state + self.heads + self.rims

    def complete(self, taps, rims, by_first, by_second):
        u0, u1 = lead_sources(taps, self.heads, rims)
        return [x + f * u0 + g * u1 for x, f, g in zip(self.state, by_first, by_second)]


def powers(table):
    return [[table[i, n] for n in range(table.shape[1])] for i in range(table.shape[0])]


def chip_kernel(lone, local, partner, taps, table, out_ref):
    modes = table.shape[1]
    odd = lax.rem(lax.axis_index("ctx"), 2) == 1
    mine, other = Summary.read(local, modes), Summary.read(partner, modes)
    first = Summary.chosen(odd, other, mine, modes)
    second = Summary.chosen(odd, mine, other, modes)
    _, block, less_one, less_two, _ = powers(table)
    start, heads = first.state, first.heads
    if lone:
        start, heads = first.complete(taps, [jnp.zeros_like(heads[0])] * 6, less_one, less_two), []
    end = second.complete(taps, first.rims, less_one, less_two)
    joined = [d * x + y for d, x, y in zip(block, start, end)]
    for i, value in enumerate(joined + heads + second.rims):
        out_ref[i] = value


def final_kernel(lone, count, *refs):
    sent = refs[:count]
    local, partner, query, response, taps, table, out_ref, work, rounded_out, out_sem = refs[count:]
    rows, groups, lanes = query.shape
    modes = table.shape[1]
    zero = jnp.zeros((groups, lanes), jnp.float32)
    index = lax.axis_index("ctx")
    odd = lax.rem(index, 2) == 1
    _, block, less_one, less_two, _ = powers(table)
    values = [
        [jnp.where(index >= 2 * (d + 1), ref[i], zero) for i in range(ref.shape[0])]
        for d, ref in enumerate(sent)
    ]
    rims = [value[-6:] for value in values] + [[zero] * 6]
    state = [zero] * modes
    for d in reversed(range(count)):
        end = values[d][:modes]
        if not lone:
            end = Summary(values[d], modes).complete(
                taps,
                rims[d + 1],
                [a * b for a, b in zip(block, less_one)],
                [a * b for a, b in zip(block, less_two)],
            )
        state = [d * d * x + y for d, x, y in zip(block, state, end)]
    before = Summary.read(partner, modes)
    end = before.complete(taps, rims[0], less_one, less_two)
    state = [jnp.where(odd, d * x + y, x) for d, x, y in zip(block, state, end)]
    rim = [jnp.where(odd, a, b) for a, b in zip(before.rims, rims[0])]

    leads = lead_sources(taps, Summary.read(local, modes).heads, rim)
    heads = edge(taps, 0, query[0], query[1], rim[0], rim[1])
    for t, u in enumerate(leads):
        state = [table[0, n] * state[n] + u for n in range(modes)]
        work[t] = heads[t] * tree_sum([table[4, n] * state[n] for n in range(modes)])
    carried = [table[4, n] * state[n] for n in range(modes)]

    def row(t, carried):
        carried = [table[0, n] * carried[n] for n in range(modes)]
        work[t] = query[t] * (response[t] + tree_sum(carried))
        return carried

    copies = []
    for i in range(rows // PIECE):
        at = slice(i * PIECE, (i + 1) * PIECE)
        carried = over_rows(row, max(i * PIECE, 2), (i + 1) * PIECE, carried)
        for g in range(groups):
            rounded_out[at, g * lanes : (g + 1) * lanes] = work[at, g, :].astype(out_ref.dtype)
        copies.append(pltpu.make_async_copy(rounded_out.at[at], out_ref.at[at], out_sem.at[i]))
        copies[-1].start()
    for copy in copies:
        copy.wait()


def on_device(tokens, in_weight, filter_taps, decay_rate, residue):
    rows, width = tokens.shape
    streams, chans = in_weight.shape[1:]
    lags = filter_taps.shape[0]
    modes = decay_rate.shape[0]
    groups = chans // LANES
    tp, ctx = lax.axis_size("tp"), lax.axis_size("ctx")
    order = ring_order(tp)
    weight = jnp.transpose(in_weight, (1, 0, 2))
    half = tp // 2
    ahead = [(order[i], order[(i + 1) % tp]) for i in range(tp)]
    back = [(b, a) for a, b in ahead]

    def f32(*shape):
        return jax.ShapeDtypeStruct(shape, jnp.float32)

    def held(count):
        return jax.ShapeDtypeStruct((count, streams, width, chans), jnp.bfloat16)

    def loads(step):
        return [step, -step] if step < half else [step]

    sums = f32(streams, rows, chans)
    wide = f32(rows, groups, LANES)
    params = pltpu.CompilerParams(vmem_limit_bytes=12 << 20)
    cost = pl.CostEstimate(flops=0, bytes_accessed=16 << 20, transcendentals=0)

    depth = min(DEPTH, width)
    left = {1: [(0, streams - 1), (1, streams - 1)], 2: [(1, streams - 1)]}

    def pieces(step):
        every = [(b, s) for s in range(streams) for b in range(len(loads(step)))]
        return [piece for piece in every if piece not in left.get(step, [])]

    total, weights = pl.pallas_call(
        functools.partial(first_kernel, order, loads(1), pieces(1)),
        out_shape=[sums, held(2)],
        in_specs=[VMEM, HBM],
        out_specs=[VMEM] * 2,
        scratch_shapes=[
            pltpu.VMEM((streams, width, chans), jnp.bfloat16),
            pltpu.SemaphoreType.DMA((width // depth,)),
            pltpu.SemaphoreType.DMA((len(pieces(1)),)),
        ],
        compiler_params=params,
        cost_estimate=cost,
        name="project_own",
    )(tokens, weight)
    fore, aft = tokens, tokens
    for step in range(1, half):
        fore = lax.ppermute(fore, "tp", ahead)
        aft = lax.ppermute(aft, "tp", back)
        fore, total, weights = lax.optimization_barrier((fore, total, weights))
        aft, total, weights = lax.optimization_barrier((aft, total, weights))
        coming = loads(step + 1)
        missing = left.get(step, [])
        extra = [filter_taps, decay_rate, residue] if step == 1 else []
        made = [f32(lags, streams, groups, LANES), f32(5, modes, groups, LANES)] if step == 1 else []
        total, weights, *made = pl.pallas_call(
            functools.partial(
                middle_kernel, order, loads(step), missing, coming, pieces(step + 1), len(extra)
            ),
            out_shape=[sums, held(len(coming))] + made,
            in_specs=[VMEM, VMEM, VMEM, HBM, VMEM] + [VMEM] * len(extra),
            out_specs=[VMEM] * (2 + len(made)),
            scratch_shapes=[
                pltpu.VMEM((max(len(missing), 1), width, chans), jnp.bfloat16),
                pltpu.SemaphoreType.DMA((max(len(missing), 1),)),
                pltpu.SemaphoreType.DMA((len(pieces(step + 1)),)),
            ],
            input_output_aliases={4: 0},
            compiler_params=params,
            cost_estimate=cost,
            name="project_pair",
        )(fore, aft, weights, weight, total, *extra)
        if made:
            taps, table = made
    fore = lax.ppermute(fore[:, : width // 2], "tp", ahead)
    aft = lax.ppermute(aft[:, width // 2 :], "tp", back)
    total = pl.pallas_call(
        half_kernel,
        out_shape=sums,
        in_specs=[VMEM] * 3,
        out_specs=VMEM,
        input_output_aliases={2: 0},
        compiler_params=params,
        cost_estimate=cost,
        name="project_half",
    )(fore, weights, total)
    total, source, local = pl.pallas_call(
        last_kernel,
        out_shape=[sums, wide, f32(modes + EDGE, groups, LANES)],
        in_specs=[VMEM] * 5,
        out_specs=[VMEM] * 3,
        scratch_shapes=[
            pltpu.VMEM((2, rows, groups, LANES), jnp.float32),
            pltpu.VMEM((8, groups, LANES), jnp.float32),
        ],
        input_output_aliases={4: 0},
        compiler_params=params,
        cost_estimate=cost,
        name="project_last",
    )(aft, weights, taps, table, total)

    partner = lax.ppermute(local, "ctx", [(j, j ^ 1) for j in range(ctx)])
    lone = ctx == 4
    chip = pl.pallas_call(
        functools.partial(chip_kernel, lone),
        out_shape=f32(modes + (6 if lone else EDGE), groups, LANES),
        in_specs=[VMEM] * 4,
        out_specs=VMEM,
        compiler_params=params,
        name="chip_state",
    )(local, partner, taps, table)
    sent = [
        lax.ppermute(chip, "ctx", [(j, (j + d) % ctx) for j in range(ctx)])
        for d in range(2, ctx, 2)
    ]
    query, response = pl.pallas_call(
        local_kernel,
        out_shape=[wide, wide],
        in_specs=[VMEM] * 4,
        out_specs=[VMEM] * 2,
        scratch_shapes=[pltpu.VMEM((rows, groups, LANES), jnp.float32)],
        compiler_params=params,
        cost_estimate=cost,
        name="local_response",
    )(total, source, taps, table)
    return pl.pallas_call(
        functools.partial(final_kernel, lone, len(sent)),
        out_shape=jax.ShapeDtypeStruct((rows, chans), jnp.bfloat16),
        in_specs=[VMEM] * (len(sent) + 6),
        out_specs=HBM,
        scratch_shapes=[
            pltpu.VMEM((rows, groups, LANES), jnp.float32),
            pltpu.VMEM((rows, chans), jnp.bfloat16),
            pltpu.SemaphoreType.DMA((rows // PIECE,)),
        ],
        compiler_params=params,
        name="carried_response",
    )(*sent, local, partner, query, response, taps, table)


def solution(mesh):
    return jax.shard_map(
        on_device,
        mesh=mesh,
        in_specs=(
            P("ctx", "tp"),
            P(None, None, "tp"),
            P(None, None, "tp"),
            P(None, "tp"),
            P(None, "tp"),
        ),
        out_specs=P("ctx", "tp"),
        check_vma=False,
    )
```

```python
import functools

import jax
import jax.numpy as jnp
from jax import lax
from jax.experimental import pallas as pl
from jax.experimental.pallas import tpu as pltpu
from jax.sharding import PartitionSpec as P

LANES = 128
COLS = 256
SOON = 2
GRID_ROWS = 4
EDGE = 10
UNROLL = 16
PIECE = 32
VMEM = pl.BlockSpec(memory_space=pltpu.VMEM)
HBM = pl.BlockSpec(memory_space=pltpu.HBM)


def ring_order(count):
    if count % (2 * GRID_ROWS):
        return list(range(count))
    cols = count // GRID_ROWS
    cells = [(0, c) for c in range(cols)]
    for r in range(1, GRID_ROWS):
        inner = list(range(1, cols))
        cells += [(r, c) for c in (reversed(inner) if r % 2 else inner)]
    cells += [(r, 0) for r in range(GRID_ROWS - 1, 0, -1)]
    return [r * cols + c for r, c in cells]


def owner_at(order, step):
    me = lax.axis_index("tp")
    owner = jnp.int32(0)
    for place, index in enumerate(order):
        owner = jnp.where(me == index, order[(place - step) % len(order)], owner)
    return owner


def piece_loads(order, steps, pieces, w_ref, target, sem):
    width = w_ref.shape[1] // len(order)
    starts = [pl.multiple_of(owner_at(order, step) * width, width) for step in steps]
    return [
        pltpu.make_async_copy(
            w_ref.at[s, pl.ds(starts[b], width), :], target(i, b, s), sem.at[i]
        )
        for i, (b, s) in enumerate(pieces)
    ]


def add_products(xs, weights, total, s, fresh=False):
    for c in range(0, total.shape[2], COLS):
        at = slice(c, c + COLS)
        terms = [
            jnp.dot(x, weights(b, at), preferred_element_type=jnp.float32) for b, x in enumerate(xs)
        ]
        total[s, :, at] = sum(terms) if fresh else total[s, :, at] + sum(terms)


def spread(out_ref, value):
    groups, lanes = out_ref.shape[-2:]
    for g in range(groups):
        out_ref[..., g, :] = value[..., g * lanes : (g + 1) * lanes]


def load_kernel(order, steps, pieces, w_ref, held, sem):
    copies = piece_loads(order, steps, pieces, w_ref, lambda i, b, s: held.at[b, s], sem)
    for copy in copies:
        copy.start()
    for copy in copies:
        copy.wait()


def middle_kernel(order, here, missing, steps, pieces, inputs_count, *refs):
    xs, (held, w_ref, *refs) = refs[: len(here)], refs[len(here) :]
    *refs, rest, rest_sem, sem = refs
    inputs, (total, next_held, *made) = refs[:inputs_count], refs[inputs_count:]
    fresh = bool(made)
    late = piece_loads(order, here, missing, w_ref, lambda i, b, s: rest.at[i], rest_sem)
    ahead = piece_loads(order, steps, pieces, w_ref, lambda i, b, s: next_held.at[b, s], sem)
    for copy in late + ahead[:SOON]:
        copy.start()
    if made:
        make_tables(*inputs, *made, total.shape[1])
    whole = min(s for _, s in missing)

    @pl.loop(0, whole)
    def _(s):
        add_products([x[...] for x in xs], lambda b, at: held[b, s, :, at], total, s, fresh)

    for copy in ahead[SOON:]:
        copy.start()
    for copy in late:
        copy.wait()

    for s in range(whole, held.shape[1]):

        def weights(b, at):
            if (b, s) in missing:
                return rest[missing.index((b, s)), :, at]
            return held[b, s, :, at]

        add_products([x[...] for x in xs], weights, total, s, fresh)

    for copy in ahead:
        copy.wait()


def half_kernel(x_ref, held, _, total):
    depth = x_ref.shape[1]
    for s in range(total.shape[0]):
        add_products([x_ref[...]], lambda b, at: held[0, s, :depth, at], total, s)


def make_tables(taps_in, decay, residue, taps, table, rows):
    rate = decay[...]
    for i, power in enumerate((1, rows, rows - 1, rows - 2)):
        spread(table.at[i], jnp.exp(-rate * power))
    spread(table.at[4], residue[...] * jnp.sqrt(1.0 - jnp.exp(-2.0 * rate)))
    spread(taps, taps_in[...])


def over_rows(step, start, stop, carry):
    aligned = -(-start // UNROLL) * UNROLL
    for t in range(start, aligned):
        carry = step(t, carry)

    def group(i, carry):
        for j in range(UNROLL):
            carry = step(i * UNROLL + j, carry)
        return carry

    return lax.fori_loop(aligned // UNROLL, stop // UNROLL, group, carry)


def filtered(taps, p_ref, s, t):
    return (
        taps[0, s] * p_ref[s - 1, t]
        + taps[1, s] * p_ref[s - 1, t - 1]
        + taps[2, s] * p_ref[s - 1, t - 2]
    )


def last_kernel(x_ref, held, taps, table, _, total, source, out_ref, p_ref, tail):
    depth = x_ref.shape[1]
    for s in range(total.shape[0]):
        add_products([x_ref[...]], lambda b, at: held[0, s, depth:, at], total, s)
    rows, groups, lanes = source.shape
    modes = table.shape[1]
    for s in (1, 2):
        spread(p_ref.at[s - 1], rounded(total[s]))
    spread(tail, rounded(total[0, rows - 8 :]))
    rate = [table[0, n] for n in range(modes)]

    def step_row(t, state):
        u = filtered(taps, p_ref, 1, t) * filtered(taps, p_ref, 2, t)
        source[t] = u
        return [r * s + u for r, s in zip(rate, state)]

    state = [jnp.zeros((groups, lanes), jnp.float32)] * modes
    state = over_rows(step_row, 2, rows, state)
    for n in range(modes):
        out_ref[n] = state[n]
    for s in (1, 2):
        for j in range(2):
            out_ref[modes + (s - 1) * 2 + j] = p_ref[s - 1, j]
            out_ref[modes + 4 + s * 2 + j] = p_ref[s - 1, rows - 2 + j]
    for j in range(2):
        out_ref[modes + 4 + j] = tail[6 + j]


def rounded(value):
    return value.astype(jnp.bfloat16).astype(jnp.float32)


def tree_sum(terms):
    while len(terms) > 1:
        terms = [a + b for a, b in zip(terms[::2], terms[1::2])] + terms[len(terms) & ~1 :]
    return terms[0]


def local_kernel(total, source, taps, table, query, response, p_ref):
    rows, groups, lanes = source.shape
    modes = table.shape[1]
    spread(p_ref, rounded(total[0]))
    for j in range(2):
        query[j] = p_ref[j]

    def step_row(t, state):
        query[t] = taps[0, 0] * p_ref[t] + taps[1, 0] * p_ref[t - 1] + taps[2, 0] * p_ref[t - 2]
        u = source[t]
        state = [table[0, n] * state[n] + u for n in range(modes)]
        response[t] = tree_sum([table[4, n] * state[n] for n in range(modes)])
        return state

    state = [jnp.zeros((groups, lanes), jnp.float32)] * modes
    over_rows(step_row, 2, rows, state)


def edge(taps, s, first, second, before, last):
    return (
        taps[0, s] * first + taps[1, s] * last + taps[2, s] * before,
        taps[0, s] * second + taps[1, s] * first + taps[2, s] * last,
    )


def lead_sources(taps, heads, rims):
    one = edge(taps, 1, heads[0], heads[1], rims[2], rims[3])
    two = edge(taps, 2, heads[2], heads[3], rims[4], rims[5])
    return one[0] * two[0], one[1] * two[1]


class Summary:
    def __init__(self, rows, modes):
        self.state = rows[:modes]
        self.heads = rows[modes : modes + 4]
        self.rims = rows[modes + 4 :]

    @classmethod
    def read(cls, ref, modes):
        return cls([ref[i] for i in range(ref.shape[0])], modes)

    @classmethod
    def chosen(cls, odd, when_odd, when_even, modes):
        pairs = zip(when_odd.rows(), when_even.rows())
        return cls([jnp.where(odd, a, b) for a, b in pairs], modes)

    def rows(self):
        return self.state + self.heads + self.rims

    def complete(self, taps, rims, by_first, by_second):
        u0, u1 = lead_sources(taps, self.heads, rims)
        return [x + f * u0 + g * u1 for x, f, g in zip(self.state, by_first, by_second)]


def powers(table):
    return [[table[i, n] for n in range(table.shape[1])] for i in range(table.shape[0])]


def chip_kernel(lone, local, partner, taps, table, out_ref):
    modes = table.shape[1]
    odd = lax.rem(lax.axis_index("ctx"), 2) == 1
    mine, other = Summary.read(local, modes), Summary.read(partner, modes)
    first = Summary.chosen(odd, other, mine, modes)
    second = Summary.chosen(odd, mine, other, modes)
    _, block, less_one, less_two, _ = powers(table)
    start, heads = first.state, first.heads
    if lone:
        start, heads = first.complete(taps, [jnp.zeros_like(heads[0])] * 6, less_one, less_two), []
    end = second.complete(taps, first.rims, less_one, less_two)
    joined = [d * x + y for d, x, y in zip(block, start, end)]
    for i, value in enumerate(joined + heads + second.rims):
        out_ref[i] = value


def final_kernel(lone, count, *refs):
    sent = refs[:count]
    local, partner, query, response, taps, table, out_ref, work, rounded_out, out_sem = refs[count:]
    rows, groups, lanes = query.shape
    modes = table.shape[1]
    zero = jnp.zeros((groups, lanes), jnp.float32)
    index = lax.axis_index("ctx")
    odd = lax.rem(index, 2) == 1
    _, block, less_one, less_two, _ = powers(table)
    values = [
        [jnp.where(index >= 2 * (d + 1), ref[i], zero) for i in range(ref.shape[0])]
        for d, ref in enumerate(sent)
    ]
    rims = [value[-6:] for value in values] + [[zero] * 6]
    state = [zero] * modes
    for d in reversed(range(count)):
        end = values[d][:modes]
        if not lone:
            end = Summary(values[d], modes).complete(
                taps,
                rims[d + 1],
                [a * b for a, b in zip(block, less_one)],
                [a * b for a, b in zip(block, less_two)],
            )
        state = [d * d * x + y for d, x, y in zip(block, state, end)]
    before = Summary.read(partner, modes)
    end = before.complete(taps, rims[0], less_one, less_two)
    state = [jnp.where(odd, d * x + y, x) for d, x, y in zip(block, state, end)]
    rim = [jnp.where(odd, a, b) for a, b in zip(before.rims, rims[0])]

    leads = lead_sources(taps, Summary.read(local, modes).heads, rim)
    heads = edge(taps, 0, query[0], query[1], rim[0], rim[1])
    for t, u in enumerate(leads):
        state = [table[0, n] * state[n] + u for n in range(modes)]
        work[t] = heads[t] * tree_sum([table[4, n] * state[n] for n in range(modes)])
    carried = [table[4, n] * state[n] for n in range(modes)]

    def row(t, carried):
        carried = [table[0, n] * carried[n] for n in range(modes)]
        work[t] = query[t] * (response[t] + tree_sum(carried))
        return carried

    copies = []
    for i in range(rows // PIECE):
        at = slice(i * PIECE, (i + 1) * PIECE)
        carried = over_rows(row, max(i * PIECE, 2), (i + 1) * PIECE, carried)
        for g in range(groups):
            rounded_out[at, g * lanes : (g + 1) * lanes] = work[at, g, :].astype(out_ref.dtype)
        copies.append(pltpu.make_async_copy(rounded_out.at[at], out_ref.at[at], out_sem.at[i]))
        copies[-1].start()
    for copy in copies:
        copy.wait()


def on_device(tokens, in_weight, filter_taps, decay_rate, residue):
    rows, width = tokens.shape
    streams, chans = in_weight.shape[1:]
    lags = filter_taps.shape[0]
    modes = decay_rate.shape[0]
    groups = chans // LANES
    tp, ctx = lax.axis_size("tp"), lax.axis_size("ctx")
    order = ring_order(tp)
    weight = jnp.transpose(in_weight, (1, 0, 2))
    half = tp // 2
    ahead = [(order[i], order[(i + 1) % tp]) for i in range(tp)]
    back = [(b, a) for a, b in ahead]

    def f32(*shape):
        return jax.ShapeDtypeStruct(shape, jnp.float32)

    def held(count):
        return jax.ShapeDtypeStruct((count, streams, width, chans), jnp.bfloat16)

    def loads(step):
        return [step, -step] if step < half else [step]

    sums = f32(streams, rows, chans)
    wide = f32(rows, groups, LANES)
    params = pltpu.CompilerParams(vmem_limit_bytes=12 << 20)
    cost = pl.CostEstimate(flops=0, bytes_accessed=16 << 20, transcendentals=0)

    def blocks(step):
        return [0] + loads(1) if step == 1 else loads(step)

    def left(step):
        return [(len(blocks(step)) - 1, streams - 1)] if step < half else []

    def pieces(step):
        every = [(b, s) for s in range(streams) for b in range(len(blocks(step)))]
        return [piece for piece in every if piece not in left(step)]

    weights = pl.pallas_call(
        functools.partial(load_kernel, order, blocks(1), pieces(1)),
        out_shape=held(len(blocks(1))),
        in_specs=[HBM],
        out_specs=VMEM,
        scratch_shapes=[pltpu.SemaphoreType.DMA((len(pieces(1)),))],
        compiler_params=params,
        cost_estimate=cost,
        name="load_first",
    )(weight)
    fore, aft, total = tokens, tokens, None
    for step in range(1, half):
        fore = lax.ppermute(fore, "tp", ahead)
        aft = lax.ppermute(aft, "tp", back)
        fore, total, weights = lax.optimization_barrier((fore, total, weights))
        aft, total, weights = lax.optimization_barrier((aft, total, weights))
        first = step == 1
        xs = [tokens, fore, aft] if first else [fore, aft]
        extra = [filter_taps, decay_rate, residue] if first else [total]
        made = [f32(lags, streams, groups, LANES), f32(5, modes, groups, LANES)] if first else []
        total, weights, *made = pl.pallas_call(
            functools.partial(
                middle_kernel, order, blocks(step), left(step), blocks(step + 1), pieces(step + 1),
                len(extra),
            ),
            out_shape=[sums, held(len(blocks(step + 1)))] + made,
            in_specs=[VMEM] * (len(xs) + 1) + [HBM] + [VMEM] * len(extra),
            out_specs=[VMEM] * (2 + len(made)),
            scratch_shapes=[
                pltpu.VMEM((len(left(step)), width, chans), jnp.bfloat16),
                pltpu.SemaphoreType.DMA((len(left(step)),)),
                pltpu.SemaphoreType.DMA((len(pieces(step + 1)),)),
            ],
            input_output_aliases={} if first else {len(xs) + 2: 0},
            compiler_params=params,
            cost_estimate=cost,
            name="project_blocks",
        )(*xs, weights, weight, *extra)
        if first:
            taps, table = made
    fore = lax.ppermute(fore[:, : width // 2], "tp", ahead)
    aft = lax.ppermute(aft[:, width // 2 :], "tp", back)
    total = pl.pallas_call(
        half_kernel,
        out_shape=sums,
        in_specs=[VMEM] * 3,
        out_specs=VMEM,
        input_output_aliases={2: 0},
        compiler_params=params,
        cost_estimate=cost,
        name="project_half",
    )(fore, weights, total)
    total, source, local = pl.pallas_call(
        last_kernel,
        out_shape=[sums, wide, f32(modes + EDGE, groups, LANES)],
        in_specs=[VMEM] * 5,
        out_specs=[VMEM] * 3,
        scratch_shapes=[
            pltpu.VMEM((2, rows, groups, LANES), jnp.float32),
            pltpu.VMEM((8, groups, LANES), jnp.float32),
        ],
        input_output_aliases={4: 0},
        compiler_params=params,
        cost_estimate=cost,
        name="project_last",
    )(aft, weights, taps, table, total)

    partner = lax.ppermute(local, "ctx", [(j, j ^ 1) for j in range(ctx)])
    lone = ctx == 4
    chip = pl.pallas_call(
        functools.partial(chip_kernel, lone),
        out_shape=f32(modes + (6 if lone else EDGE), groups, LANES),
        in_specs=[VMEM] * 4,
        out_specs=VMEM,
        compiler_params=params,
        name="chip_state",
    )(local, partner, taps, table)
    sent = [
        lax.ppermute(chip, "ctx", [(j, (j + d) % ctx) for j in range(ctx)])
        for d in range(2, ctx, 2)
    ]
    query, response = pl.pallas_call(
        local_kernel,
        out_shape=[wide, wide],
        in_specs=[VMEM] * 4,
        out_specs=[VMEM] * 2,
        scratch_shapes=[pltpu.VMEM((rows, groups, LANES), jnp.float32)],
        compiler_params=params,
        cost_estimate=cost,
        name="local_response",
    )(total, source, taps, table)
    return pl.pallas_call(
        functools.partial(final_kernel, lone, len(sent)),
        out_shape=jax.ShapeDtypeStruct((rows, chans), jnp.bfloat16),
        in_specs=[VMEM] * (len(sent) + 6),
        out_specs=HBM,
        scratch_shapes=[
            pltpu.VMEM((rows, groups, LANES), jnp.float32),
            pltpu.VMEM((rows, chans), jnp.bfloat16),
            pltpu.SemaphoreType.DMA((rows // PIECE,)),
        ],
        compiler_params=params,
        name="carried_response",
    )(*sent, local, partner, query, response, taps, table)


def solution(mesh):
    return jax.shard_map(
        on_device,
        mesh=mesh,
        in_specs=(
            P("ctx", "tp"),
            P(None, None, "tp"),
            P(None, None, "tp"),
            P(None, "tp"),
            P(None, "tp"),
        ),
        out_specs=P("ctx", "tp"),
        check_vma=False,
    )
```

```python
import functools

import jax
import jax.numpy as jnp
from jax import lax
from jax.experimental import pallas as pl
from jax.experimental.pallas import tpu as pltpu
from jax.sharding import PartitionSpec as P

LANES = 128
COLS = 256
SOON = 2
GRID_ROWS = 4
EDGE = 10
UNROLL = 16
VMEM = pl.BlockSpec(memory_space=pltpu.VMEM)
HBM = pl.BlockSpec(memory_space=pltpu.HBM)


def ring_order(count):
    if count % (2 * GRID_ROWS):
        return list(range(count))
    cols = count // GRID_ROWS
    cells = [(0, c) for c in range(cols)]
    for r in range(1, GRID_ROWS):
        inner = list(range(1, cols))
        cells += [(r, c) for c in (reversed(inner) if r % 2 else inner)]
    cells += [(r, 0) for r in range(GRID_ROWS - 1, 0, -1)]
    return [r * cols + c for r, c in cells]


def owner_at(order, step):
    me = lax.axis_index("tp")
    owner = jnp.int32(0)
    for place, index in enumerate(order):
        owner = jnp.where(me == index, order[(place - step) % len(order)], owner)
    return owner


def piece_loads(order, steps, pieces, w_ref, target, sem):
    width = w_ref.shape[1] // len(order)
    starts = [pl.multiple_of(owner_at(order, step) * width, width) for step in steps]
    return [
        pltpu.make_async_copy(
            w_ref.at[s, pl.ds(starts[b] + low, high - low), :], target(i, b, s, low, high), sem.at[i]
        )
        for i, (b, s, low, high) in enumerate(pieces)
    ]


def add_products(xs, weights, total, s, fresh=False):
    for c in range(0, total.shape[2], COLS):
        at = slice(c, c + COLS)
        terms = [
            jnp.dot(x, weights(b, at), preferred_element_type=jnp.float32) for b, x in enumerate(xs)
        ]
        total[s, :, at] = sum(terms) if fresh else total[s, :, at] + sum(terms)


def spread(out_ref, value):
    groups, lanes = out_ref.shape[-2:]
    for g in range(groups):
        out_ref[..., g, :] = value[..., g * lanes : (g + 1) * lanes]


def held_part(held):
    return lambda i, b, s, low, high: held.at[b, s, pl.ds(low, high - low), :]


def load_kernel(order, steps, pieces, w_ref, held, sem):
    copies = piece_loads(order, steps, pieces, w_ref, held_part(held), sem)
    for copy in copies:
        copy.start()
    for copy in copies:
        copy.wait()


def middle_kernel(order, here, missing, steps, pieces, inputs_count, *refs):
    xs, (held, w_ref, *refs) = refs[: len(here)], refs[len(here) :]
    *refs, rest, rest_sem, sem = refs
    inputs, (total, next_held, *made) = refs[:inputs_count], refs[inputs_count:]
    fresh = bool(made)
    late = piece_loads(order, here, missing, w_ref, lambda i, *_: rest.at[i], rest_sem)
    ahead = piece_loads(order, steps, pieces, w_ref, held_part(next_held), sem)
    for copy in late + ahead[:SOON]:
        copy.start()
    if made:
        make_tables(*inputs, *made, total.shape[1])
    whole = held.shape[1] - len(missing)

    @pl.loop(0, whole)
    def _(s):
        add_products([x[...] for x in xs], lambda b, at: held[b, s, :, at], total, s, fresh)

    for copy in ahead[SOON:]:
        copy.start()
    for copy in late:
        copy.wait()
    for i, (b, s, low, _) in enumerate(missing):
        parts = [(x[...], (lambda at, k=k: held[k, s, :, at])) for k, x in enumerate(xs) if k != b]
        parts.append((xs[b][:, :low], lambda at: held[b, s, :low, at]))
        parts.append((xs[b][:, low:], lambda at: rest[i, :, at]))
        values, weights = zip(*parts)
        add_products(values, lambda k, at: weights[k](at), total, s, fresh)
    for copy in ahead:
        copy.wait()


def half_kernel(x_ref, held, _, total):
    depth = x_ref.shape[1]
    for s in range(total.shape[0]):
        add_products([x_ref[...]], lambda b, at: held[0, s, :depth, at], total, s)


def make_tables(taps_in, decay, residue, taps, table, tile, tile_step, rows):
    rate = decay[...]
    coeffs = residue[...] * jnp.sqrt(1.0 - jnp.exp(-2.0 * rate))
    for i, power in enumerate((1, rows, rows - 1, rows - 2)):
        spread(table.at[i], jnp.exp(-rate * power))
    spread(table.at[4], coeffs)
    spread(taps, taps_in[...])
    for r in range(tile.shape[1]):
        tile[:, r, :] = coeffs * jnp.exp(-rate * (r - 1.0))
    tile_step[...] = jnp.exp(-rate * tile.shape[1])


def over_rows(step, start, stop, carry):
    aligned = -(-start // UNROLL) * UNROLL
    for t in range(start, aligned):
        carry = step(t, carry)

    def group(i, carry):
        for j in range(UNROLL):
            carry = step(i * UNROLL + j, carry)
        return carry

    return lax.fori_loop(aligned // UNROLL, stop // UNROLL, group, carry)


def filtered(taps, s, value, cols):
    one, two = pltpu.roll(value, 1, 0), pltpu.roll(value, 2, 0)
    lags = [taps[j, s : s + 1, cols] for j in range(3)]
    return lags[0] * value + lags[1] * one + lags[2] * two


def last_kernel(x_ref, held, taps, table, _, total, source, out_ref, low, high):
    depth = x_ref.shape[1]
    for s in range(total.shape[0]):
        add_products([x_ref[...]], lambda b, at: held[0, s, depth:, at], total, s)
    rows, groups, lanes = source.shape
    modes = table.shape[1]
    for g in range(groups):
        cols = slice(g * lanes, (g + 1) * lanes)
        one, two = rounded(total[1, :, cols]), rounded(total[2, :, cols])
        source[:, g, :] = filtered(taps, 1, one, cols) * filtered(taps, 2, two, cols)
        for s, value in ((1, one), (2, two)):
            low[s - 1, :, g, :] = value[:8]
            high[s, :, g, :] = value[rows - 8 :]
        high[0, :, g, :] = rounded(total[0, rows - 8 :, cols])
    rate = [table[0, n] for n in range(modes)]

    def step_row(t, state):
        u = source[t]
        return [r * s + u for r, s in zip(rate, state)]

    state = [jnp.zeros((groups, lanes), jnp.float32)] * modes
    state = over_rows(step_row, 2, rows, state)
    for n in range(modes):
        out_ref[n] = state[n]
    for j in range(2):
        for s in (1, 2):
            out_ref[modes + (s - 1) * 2 + j] = low[s - 1, j]
        for s in range(3):
            out_ref[modes + 4 + s * 2 + j] = high[s, 6 + j]


def rounded(value):
    return value.astype(jnp.bfloat16).astype(jnp.float32)


def tree_sum(terms):
    while len(terms) > 1:
        terms = [a + b for a, b in zip(terms[::2], terms[1::2])] + terms[len(terms) & ~1 :]
    return terms[0]


def local_kernel(total, source, taps, table, query, response, heads, work, low):
    rows, groups, lanes = source.shape
    modes = table.shape[1]
    for g in range(groups):
        cols = slice(g * lanes, (g + 1) * lanes)
        value = rounded(total[0, :, cols])
        query[:, cols] = filtered(taps, 0, value, cols)
        low[:, g, :] = value[:8]
    for j in range(2):
        heads[j] = low[j]
        work[j] = jnp.zeros((groups, lanes), jnp.float32)

    def step_row(t, state):
        u = source[t]
        state = [table[0, n] * state[n] + u for n in range(modes)]
        work[t] = tree_sum([table[4, n] * state[n] for n in range(modes)])
        return state

    over_rows(step_row, 2, rows, [jnp.zeros((groups, lanes), jnp.float32)] * modes)
    for g in range(groups):
        response[:, g * lanes : (g + 1) * lanes] = work[:, g, :]


def edge(taps, s, first, second, before, last):
    return (
        taps[0, s] * first + taps[1, s] * last + taps[2, s] * before,
        taps[0, s] * second + taps[1, s] * first + taps[2, s] * last,
    )


def lead_sources(taps, heads, rims):
    one = edge(taps, 1, heads[0], heads[1], rims[2], rims[3])
    two = edge(taps, 2, heads[2], heads[3], rims[4], rims[5])
    return one[0] * two[0], one[1] * two[1]


class Summary:
    def __init__(self, rows, modes):
        self.state = rows[:modes]
        self.heads = rows[modes : modes + 4]
        self.rims = rows[modes + 4 :]

    @classmethod
    def read(cls, ref, modes):
        return cls([ref[i] for i in range(ref.shape[0])], modes)

    @classmethod
    def chosen(cls, odd, when_odd, when_even, modes):
        pairs = zip(when_odd.rows(), when_even.rows())
        return cls([jnp.where(odd, a, b) for a, b in pairs], modes)

    def rows(self):
        return self.state + self.heads + self.rims

    def complete(self, taps, rims, by_first, by_second):
        u0, u1 = lead_sources(taps, self.heads, rims)
        return [x + f * u0 + g * u1 for x, f, g in zip(self.state, by_first, by_second)]


def powers(table):
    return [[table[i, n] for n in range(table.shape[1])] for i in range(table.shape[0])]


def chip_kernel(lone, local, partner, taps, table, out_ref):
    modes = table.shape[1]
    odd = lax.rem(lax.axis_index("ctx"), 2) == 1
    mine, other = Summary.read(local, modes), Summary.read(partner, modes)
    first = Summary.chosen(odd, other, mine, modes)
    second = Summary.chosen(odd, mine, other, modes)
    _, block, less_one, less_two, _ = powers(table)
    start, heads = first.state, first.heads
    if lone:
        start, heads = first.complete(taps, [jnp.zeros_like(heads[0])] * 6, less_one, less_two), []
    end = second.complete(taps, first.rims, less_one, less_two)
    joined = [d * x + y for d, x, y in zip(block, start, end)]
    for i, value in enumerate(joined + heads + second.rims):
        out_ref[i] = value


def final_kernel(lone, count, *refs):
    sent = refs[:count]
    local, partner, query, response, query_heads, taps, table, tile, tile_step, *refs = refs[count:]
    out_ref, states, firsts, rounded_out, out_sem = refs
    rows = query.shape[0]
    groups, lanes = local.shape[1:]
    modes = table.shape[1]
    zero = jnp.zeros((groups, lanes), jnp.float32)
    index = lax.axis_index("ctx")
    odd = lax.rem(index, 2) == 1
    _, block, less_one, less_two, _ = powers(table)
    values = [
        [jnp.where(index >= 2 * (d + 1), ref[i], zero) for i in range(ref.shape[0])]
        for d, ref in enumerate(sent)
    ]
    rims = [value[-6:] for value in values] + [[zero] * 6]
    state = [zero] * modes
    for d in reversed(range(count)):
        end = values[d][:modes]
        if not lone:
            end = Summary(values[d], modes).complete(
                taps,
                rims[d + 1],
                [a * b for a, b in zip(block, less_one)],
                [a * b for a, b in zip(block, less_two)],
            )
        state = [d * d * x + y for d, x, y in zip(block, state, end)]
    before = Summary.read(partner, modes)
    end = before.complete(taps, rims[0], less_one, less_two)
    state = [jnp.where(odd, d * x + y, x) for d, x, y in zip(block, state, end)]
    rim = [jnp.where(odd, a, b) for a, b in zip(before.rims, rims[0])]

    leads = lead_sources(taps, Summary.read(local, modes).heads, rim)
    heads = edge(taps, 0, query_heads[0], query_heads[1], rim[0], rim[1])
    for t, u in enumerate(leads):
        state = [table[0, n] * state[n] + u for n in range(modes)]
        firsts[t] = heads[t] * tree_sum([table[4, n] * state[n] for n in range(modes)])
    for n in range(modes):
        states[n] = state[n]

    tall = tile.shape[1]
    row = lax.broadcasted_iota(jnp.int32, (tall, lanes), 0)
    copies = []
    for g in range(groups):
        cols = slice(g * lanes, (g + 1) * lanes)
        carried = [tile[n, :, cols] * states[n, g : g + 1, :] for n in range(modes)]
        step = [jnp.broadcast_to(tile_step[n : n + 1, cols], (tall, lanes)) for n in range(modes)]
        for i in range(0, rows, 2 * tall):
            pair = []
            for at in (slice(i, i + tall), slice(i + tall, i + 2 * tall)):
                value = query[at, cols] * (response[at, cols] + tree_sum(carried))
                if at.start == 0:
                    value = jnp.where(row == 0, firsts[0, g : g + 1, :], value)
                    value = jnp.where(row == 1, firsts[1, g : g + 1, :], value)
                pair.append(value)
                carried = [a * b for a, b in zip(carried, step)]
            rounded_out[i : i + 2 * tall, cols] = jnp.concatenate(pair, axis=0).astype(out_ref.dtype)
        if g % 2:
            wide = slice((g - 1) * lanes, (g + 1) * lanes)
            k = g // 2
            copies.append(
                pltpu.make_async_copy(rounded_out.at[:, wide], out_ref.at[:, wide], out_sem.at[k])
            )
            copies[-1].start()
    for copy in copies:
        copy.wait()


def on_device(tokens, in_weight, filter_taps, decay_rate, residue):
    rows, width = tokens.shape
    streams, chans = in_weight.shape[1:]
    lags = filter_taps.shape[0]
    modes = decay_rate.shape[0]
    groups = chans // LANES
    tp, ctx = lax.axis_size("tp"), lax.axis_size("ctx")
    order = ring_order(tp)
    weight = jnp.transpose(in_weight, (1, 0, 2))
    half = tp // 2
    ahead = [(order[i], order[(i + 1) % tp]) for i in range(tp)]
    back = [(b, a) for a, b in ahead]

    def f32(*shape):
        return jax.ShapeDtypeStruct(shape, jnp.float32)

    def held(count):
        return jax.ShapeDtypeStruct((count, streams, width, chans), jnp.bfloat16)

    def loads(step):
        return [step, -step] if step < half else [step]

    sums = f32(streams, rows, chans)
    wide = f32(rows, groups, LANES)
    params = pltpu.CompilerParams(vmem_limit_bytes=12 << 20)
    cost = pl.CostEstimate(flops=0, bytes_accessed=16 << 20, transcendentals=0)

    def blocks(step):
        return [0] + loads(1) if step == 1 else loads(step)

    def left(step):
        rows_left = (width // 2, width)
        return [(len(blocks(step)) - 1, streams - 1, *rows_left)] if step % 2 and step < half else []

    def pieces(step):
        lacking = {(b, s): low for b, s, low, _ in left(step)}
        every = [(b, s) for s in range(streams) for b in range(len(blocks(step)))]
        return [(b, s, 0, lacking.get((b, s), width)) for b, s in every]

    weights = pl.pallas_call(
        functools.partial(load_kernel, order, blocks(1), pieces(1)),
        out_shape=held(len(blocks(1))),
        in_specs=[HBM],
        out_specs=VMEM,
        scratch_shapes=[pltpu.SemaphoreType.DMA((len(pieces(1)),))],
        compiler_params=params,
        cost_estimate=cost,
        name="load_first",
    )(weight)
    fore, aft, total = tokens, tokens, None
    for step in range(1, half):
        fore = lax.ppermute(fore, "tp", ahead)
        aft = lax.ppermute(aft, "tp", back)
        fore, total, weights = lax.optimization_barrier((fore, total, weights))
        aft, total, weights = lax.optimization_barrier((aft, total, weights))
        first = step == 1
        xs = [tokens, fore, aft] if first else [fore, aft]
        extra = [filter_taps, decay_rate, residue] if first else [total]
        made = []
        if first:
            made = [f32(lags, streams, groups, LANES), f32(5, modes, groups, LANES)]
            made += [f32(modes, 8, chans), f32(modes, chans)]
        total, weights, *made = pl.pallas_call(
            functools.partial(
                middle_kernel, order, blocks(step), left(step), blocks(step + 1), pieces(step + 1),
                len(extra),
            ),
            out_shape=[sums, held(len(blocks(step + 1)))] + made,
            in_specs=[VMEM] * (len(xs) + 1) + [HBM] + [VMEM] * len(extra),
            out_specs=[VMEM] * (2 + len(made)),
            scratch_shapes=[
                pltpu.VMEM((1, width // 2, chans), jnp.bfloat16),
                pltpu.SemaphoreType.DMA((1,)),
                pltpu.SemaphoreType.DMA((len(pieces(step + 1)),)),
            ],
            input_output_aliases={} if first else {len(xs) + 2: 0},
            compiler_params=params,
            cost_estimate=cost,
            name="project_blocks",
        )(*xs, weights, weight, *extra)
        if first:
            taps, table, *tiles = made
    fore = lax.ppermute(fore[:, : width // 2], "tp", ahead)
    aft = lax.ppermute(aft[:, width // 2 :], "tp", back)
    total = pl.pallas_call(
        half_kernel,
        out_shape=sums,
        in_specs=[VMEM] * 3,
        out_specs=VMEM,
        input_output_aliases={2: 0},
        compiler_params=params,
        cost_estimate=cost,
        name="project_half",
    )(fore, weights, total)
    total, source, local = pl.pallas_call(
        last_kernel,
        out_shape=[sums, wide, f32(modes + EDGE, groups, LANES)],
        in_specs=[VMEM] * 5,
        out_specs=[VMEM] * 3,
        scratch_shapes=[
            pltpu.VMEM((streams - 1, 8, groups, LANES), jnp.float32),
            pltpu.VMEM((streams, 8, groups, LANES), jnp.float32),
        ],
        input_output_aliases={4: 0},
        compiler_params=params,
        cost_estimate=cost,
        name="project_last",
    )(aft, weights, filter_taps, table, total)

    partner = lax.ppermute(local, "ctx", [(j, j ^ 1) for j in range(ctx)])
    lone = ctx == 4
    chip = pl.pallas_call(
        functools.partial(chip_kernel, lone),
        out_shape=f32(modes + (6 if lone else EDGE), groups, LANES),
        in_specs=[VMEM] * 4,
        out_specs=VMEM,
        compiler_params=params,
        name="chip_state",
    )(local, partner, taps, table)
    sent = [
        lax.ppermute(chip, "ctx", [(j, (j + d) % ctx) for j in range(ctx)])
        for d in range(2, ctx, 2)
    ]
    query, response, heads = pl.pallas_call(
        local_kernel,
        out_shape=[f32(rows, chans), f32(rows, chans), f32(2, groups, LANES)],
        in_specs=[VMEM] * 4,
        out_specs=[VMEM] * 3,
        scratch_shapes=[
            pltpu.VMEM((rows, groups, LANES), jnp.float32),
            pltpu.VMEM((8, groups, LANES), jnp.float32),
        ],
        compiler_params=params,
        cost_estimate=cost,
        name="local_response",
    )(total, source, filter_taps, table)
    return pl.pallas_call(
        functools.partial(final_kernel, lone, len(sent)),
        out_shape=jax.ShapeDtypeStruct((rows, chans), jnp.bfloat16),
        in_specs=[VMEM] * (len(sent) + 9),
        out_specs=HBM,
        scratch_shapes=[
            pltpu.VMEM((modes, groups, LANES), jnp.float32),
            pltpu.VMEM((2, groups, LANES), jnp.float32),
            pltpu.VMEM((rows, chans), jnp.bfloat16),
            pltpu.SemaphoreType.DMA((groups // 2,)),
        ],
        compiler_params=params,
        name="carried_response",
    )(*sent, local, partner, query, response, heads, taps, table, *tiles)


def solution(mesh):
    return jax.shard_map(
        on_device,
        mesh=mesh,
        in_specs=(
            P("ctx", "tp"),
            P(None, None, "tp"),
            P(None, None, "tp"),
            P(None, "tp"),
            P(None, "tp"),
        ),
        out_specs=P("ctx", "tp"),
        check_vma=False,
    )
```

```python
import functools

import jax
import jax.numpy as jnp
from jax import lax
from jax.experimental import pallas as pl
from jax.experimental.pallas import tpu as pltpu
from jax.sharding import PartitionSpec as P

LANES = 128
COLS = 256
WIDE = 512
SOON = 4
GRID_ROWS = 4
EDGE = 10
UNROLL = 16
VMEM = pl.BlockSpec(memory_space=pltpu.VMEM)
HBM = pl.BlockSpec(memory_space=pltpu.HBM)


def ring_order(count):
    if count % (2 * GRID_ROWS):
        return list(range(count))
    cols = count // GRID_ROWS
    cells = [(0, c) for c in range(cols)]
    for r in range(1, GRID_ROWS):
        inner = list(range(1, cols))
        cells += [(r, c) for c in (reversed(inner) if r % 2 else inner)]
    cells += [(r, 0) for r in range(GRID_ROWS - 1, 0, -1)]
    return [r * cols + c for r, c in cells]


def owner_at(order, step):
    me = lax.axis_index("tp")
    owner = jnp.int32(0)
    for place, index in enumerate(order):
        owner = jnp.where(me == index, order[(place - step) % len(order)], owner)
    return owner


def piece_loads(order, steps, pieces, w_ref, target, sem):
    width = w_ref.shape[1] // len(order)
    starts = [pl.multiple_of(owner_at(order, step) * width, width) for step in steps]
    return [
        pltpu.make_async_copy(
            w_ref.at[s, pl.ds(starts[b] + low, high - low), :], target(i, b, s, low, high), sem.at[i]
        )
        for i, (b, s, low, high) in enumerate(pieces)
    ]


def add_products(xs, weights, total, s, fresh=False, cols=COLS):
    cols = min(cols, total.shape[2])
    for c in range(0, total.shape[2], cols):
        at = slice(c, c + cols)
        terms = [
            jnp.dot(x, weights(b, at), preferred_element_type=jnp.float32) for b, x in enumerate(xs)
        ]
        total[s, :, at] = sum(terms) if fresh else total[s, :, at] + sum(terms)


def spread(out_ref, value):
    groups, lanes = out_ref.shape[-2:]
    for g in range(groups):
        out_ref[..., g, :] = value[..., g * lanes : (g + 1) * lanes]


def held_part(held):
    return lambda i, b, s, low, high: held.at[b, s, pl.ds(low, high - low), :]


def load_kernel(order, steps, pieces, w_ref, held, sem):
    copies = piece_loads(order, steps, pieces, w_ref, held_part(held), sem)
    for copy in copies:
        copy.start()
    for copy in copies:
        copy.wait()


def middle_kernel(order, here, missing, steps, pieces, inputs_count, *refs):
    xs, (held, w_ref, *refs) = refs[: len(here)], refs[len(here) :]
    *refs, rest, rest_sem, sem = refs
    inputs, (total, next_held, *made) = refs[:inputs_count], refs[inputs_count:]
    fresh = bool(made)
    late = piece_loads(order, here, missing, w_ref, lambda i, *_: rest.at[i], rest_sem)
    ahead = piece_loads(order, steps, pieces, w_ref, held_part(next_held), sem)
    for copy in late + ahead[:SOON]:
        copy.start()
    if made:
        make_tables(*inputs, *made, total.shape[1])
    whole = held.shape[1] - len(missing)

    @pl.loop(0, whole)
    def _(s):
        add_products([x[...] for x in xs], lambda b, at: held[b, s, :, at], total, s, fresh)

    for copy in ahead[SOON:]:
        copy.start()
    for copy in late:
        copy.wait()
    for i, (b, s, low, _) in enumerate(missing):
        parts = [(x[...], (lambda at, k=k: held[k, s, :, at])) for k, x in enumerate(xs) if k != b]
        parts.append((xs[b][:, :low], lambda at: held[b, s, :low, at]))
        parts.append((xs[b][:, low:], lambda at: rest[i, :, at]))
        values, weights = zip(*parts)
        add_products(values, lambda k, at: weights[k](at), total, s, fresh)
    for copy in ahead:
        copy.wait()


def half_kernel(x_ref, held, _, total):
    depth = x_ref.shape[1]
    for s in range(total.shape[0]):
        add_products([x_ref[...]], lambda b, at: held[0, s, :depth, at], total, s, cols=WIDE)


def make_tables(taps_in, decay, residue, taps, table, tile, tile_step, rows):
    rate = decay[...]
    coeffs = residue[...] * jnp.sqrt(1.0 - jnp.exp(-2.0 * rate))
    for i, power in enumerate((1, rows, rows - 1, rows - 2)):
        spread(table.at[i], jnp.exp(-rate * power))
    spread(table.at[4], coeffs)
    spread(taps, taps_in[...])
    for r in range(tile.shape[1]):
        tile[:, r, :] = coeffs * jnp.exp(-rate * (r - 1.0))
    tile_step[...] = jnp.exp(-rate * tile.shape[1])


def over_rows(step, start, stop, carry):
    aligned = -(-start // UNROLL) * UNROLL
    for t in range(start, aligned):
        carry = step(t, carry)

    def group(i, carry):
        for j in range(UNROLL):
            carry = step(i * UNROLL + j, carry)
        return carry

    return lax.fori_loop(aligned // UNROLL, stop // UNROLL, group, carry)


def filtered(taps, s, value, cols):
    one, two = pltpu.roll(value, 1, 0), pltpu.roll(value, 2, 0)
    lags = [taps[j, s : s + 1, cols] for j in range(3)]
    return lags[0] * value + lags[1] * one + lags[2] * two


def last_kernel(x_ref, held, taps, table, _, total, source, out_ref, low, high):
    depth = x_ref.shape[1]
    for s in range(total.shape[0]):
        add_products([x_ref[...]], lambda b, at: held[0, s, depth:, at], total, s, cols=WIDE)
    rows, groups, lanes = source.shape
    modes = table.shape[1]
    for g in range(groups):
        cols = slice(g * lanes, (g + 1) * lanes)
        one, two = rounded(total[1, :, cols]), rounded(total[2, :, cols])
        source[:, g, :] = filtered(taps, 1, one, cols) * filtered(taps, 2, two, cols)
        for s, value in ((1, one), (2, two)):
            low[s - 1, :, g, :] = value[:8]
            high[s, :, g, :] = value[rows - 8 :]
        high[0, :, g, :] = rounded(total[0, rows - 8 :, cols])
    rate = [table[0, n] for n in range(modes)]

    def step_row(t, state):
        u = source[t]
        return [r * s + u for r, s in zip(rate, state)]

    state = [jnp.zeros((groups, lanes), jnp.float32)] * modes
    state = over_rows(step_row, 2, rows, state)
    for n in range(modes):
        out_ref[n] = state[n]
    for j in range(2):
        for s in (1, 2):
            out_ref[modes + (s - 1) * 2 + j] = low[s - 1, j]
        for s in range(3):
            out_ref[modes + 4 + s * 2 + j] = high[s, 6 + j]


def rounded(value):
    return value.astype(jnp.bfloat16).astype(jnp.float32)


def tree_sum(terms):
    while len(terms) > 1:
        terms = [a + b for a, b in zip(terms[::2], terms[1::2])] + terms[len(terms) & ~1 :]
    return terms[0]


def local_kernel(total, source, taps, table, query, response, heads, work, low):
    rows, groups, lanes = source.shape
    modes = table.shape[1]
    for g in range(groups):
        cols = slice(g * lanes, (g + 1) * lanes)
        value = rounded(total[0, :, cols])
        query[:, cols] = filtered(taps, 0, value, cols)
        low[:, g, :] = value[:8]
    for j in range(2):
        heads[j] = low[j]
        work[j] = jnp.zeros((groups, lanes), jnp.float32)

    def step_row(t, state):
        u = source[t]
        state = [table[0, n] * state[n] + u for n in range(modes)]
        work[t] = tree_sum([table[4, n] * state[n] for n in range(modes)])
        return state

    over_rows(step_row, 2, rows, [jnp.zeros((groups, lanes), jnp.float32)] * modes)
    for g in range(groups):
        response[:, g * lanes : (g + 1) * lanes] = work[:, g, :]


def edge(taps, s, first, second, before, last):
    return (
        taps[0, s] * first + taps[1, s] * last + taps[2, s] * before,
        taps[0, s] * second + taps[1, s] * first + taps[2, s] * last,
    )


def lead_sources(taps, heads, rims):
    one = edge(taps, 1, heads[0], heads[1], rims[2], rims[3])
    two = edge(taps, 2, heads[2], heads[3], rims[4], rims[5])
    return one[0] * two[0], one[1] * two[1]


class Summary:
    def __init__(self, rows, modes):
        self.state = rows[:modes]
        self.heads = rows[modes : modes + 4]
        self.rims = rows[modes + 4 :]

    @classmethod
    def read(cls, ref, modes):
        return cls([ref[i] for i in range(ref.shape[0])], modes)

    @classmethod
    def chosen(cls, odd, when_odd, when_even, modes):
        pairs = zip(when_odd.rows(), when_even.rows())
        return cls([jnp.where(odd, a, b) for a, b in pairs], modes)

    def rows(self):
        return self.state + self.heads + self.rims

    def complete(self, taps, rims, by_first, by_second):
        u0, u1 = lead_sources(taps, self.heads, rims)
        return [x + f * u0 + g * u1 for x, f, g in zip(self.state, by_first, by_second)]


def powers(table):
    return [[table[i, n] for n in range(table.shape[1])] for i in range(table.shape[0])]


def chip_kernel(lone, local, partner, taps, table, out_ref):
    modes = table.shape[1]
    odd = lax.rem(lax.axis_index("ctx"), 2) == 1
    mine, other = Summary.read(local, modes), Summary.read(partner, modes)
    first = Summary.chosen(odd, other, mine, modes)
    second = Summary.chosen(odd, mine, other, modes)
    _, block, less_one, less_two, _ = powers(table)
    start, heads = first.state, first.heads
    if lone:
        start, heads = first.complete(taps, [jnp.zeros_like(heads[0])] * 6, less_one, less_two), []
    end = second.complete(taps, first.rims, less_one, less_two)
    joined = [d * x + y for d, x, y in zip(block, start, end)]
    for i, value in enumerate(joined + heads + second.rims):
        out_ref[i] = value


def final_kernel(lone, count, *refs):
    sent = refs[:count]
    local, partner, query, response, query_heads, taps, table, tile, tile_step, *refs = refs[count:]
    out_ref, states, firsts, rounded_out, out_sem = refs
    rows = query.shape[0]
    groups, lanes = local.shape[1:]
    modes = table.shape[1]
    zero = jnp.zeros((groups, lanes), jnp.float32)
    index = lax.axis_index("ctx")
    odd = lax.rem(index, 2) == 1
    _, block, less_one, less_two, _ = powers(table)
    values = [
        [jnp.where(index >= 2 * (d + 1), ref[i], zero) for i in range(ref.shape[0])]
        for d, ref in enumerate(sent)
    ]
    rims = [value[-6:] for value in values] + [[zero] * 6]
    state = [zero] * modes
    for d in reversed(range(count)):
        end = values[d][:modes]
        if not lone:
            end = Summary(values[d], modes).complete(
                taps,
                rims[d + 1],
                [a * b for a, b in zip(block, less_one)],
                [a * b for a, b in zip(block, less_two)],
            )
        state = [d * d * x + y for d, x, y in zip(block, state, end)]
    before = Summary.read(partner, modes)
    end = before.complete(taps, rims[0], less_one, less_two)
    state = [jnp.where(odd, d * x + y, x) for d, x, y in zip(block, state, end)]
    rim = [jnp.where(odd, a, b) for a, b in zip(before.rims, rims[0])]

    leads = lead_sources(taps, Summary.read(local, modes).heads, rim)
    heads = edge(taps, 0, query_heads[0], query_heads[1], rim[0], rim[1])
    for t, u in enumerate(leads):
        state = [table[0, n] * state[n] + u for n in range(modes)]
        firsts[t] = heads[t] * tree_sum([table[4, n] * state[n] for n in range(modes)])
    for n in range(modes):
        states[n] = state[n]

    tall = tile.shape[1]
    row = lax.broadcasted_iota(jnp.int32, (tall, lanes), 0)
    copies = []
    for g in range(groups):
        cols = slice(g * lanes, (g + 1) * lanes)
        carried = [tile[n, :, cols] * states[n, g : g + 1, :] for n in range(modes)]
        step = [jnp.broadcast_to(tile_step[n : n + 1, cols], (tall, lanes)) for n in range(modes)]
        for i in range(0, rows, 2 * tall):
            pair = []
            for at in (slice(i, i + tall), slice(i + tall, i + 2 * tall)):
                value = query[at, cols] * (response[at, cols] + tree_sum(carried))
                if at.start == 0:
                    value = jnp.where(row == 0, firsts[0, g : g + 1, :], value)
                    value = jnp.where(row == 1, firsts[1, g : g + 1, :], value)
                pair.append(value)
                carried = [a * b for a, b in zip(carried, step)]
            rounded_out[i : i + 2 * tall, cols] = jnp.concatenate(pair, axis=0).astype(out_ref.dtype)
        if g % 2:
            wide = slice((g - 1) * lanes, (g + 1) * lanes)
            k = g // 2
            copies.append(
                pltpu.make_async_copy(rounded_out.at[:, wide], out_ref.at[:, wide], out_sem.at[k])
            )
            copies[-1].start()
    for copy in copies:
        copy.wait()


def on_device(tokens, in_weight, filter_taps, decay_rate, residue):
    rows, width = tokens.shape
    streams, chans = in_weight.shape[1:]
    lags = filter_taps.shape[0]
    modes = decay_rate.shape[0]
    groups = chans // LANES
    tp, ctx = lax.axis_size("tp"), lax.axis_size("ctx")
    order = ring_order(tp)
    weight = jnp.transpose(in_weight, (1, 0, 2))
    half = tp // 2
    ahead = [(order[i], order[(i + 1) % tp]) for i in range(tp)]
    back = [(b, a) for a, b in ahead]

    def f32(*shape):
        return jax.ShapeDtypeStruct(shape, jnp.float32)

    def held(count):
        return jax.ShapeDtypeStruct((count, streams, width, chans), jnp.bfloat16)

    def loads(step):
        return [step, -step] if step < half else [step]

    sums = f32(streams, rows, chans)
    wide = f32(rows, groups, LANES)
    params = pltpu.CompilerParams(vmem_limit_bytes=12 << 20)
    cost = pl.CostEstimate(flops=0, bytes_accessed=16 << 20, transcendentals=0)

    def blocks(step):
        return [0] + loads(1) if step == 1 else loads(step)

    def left(step):
        rows_left = (width // 2, width)
        return [(len(blocks(step)) - 1, streams - 1, *rows_left)] if step % 2 and step < half else []

    def pieces(step):
        lacking = {(b, s): low for b, s, low, _ in left(step)}
        every = [(b, s) for s in range(streams) for b in range(len(blocks(step)))]
        return [(b, s, 0, lacking.get((b, s), width)) for b, s in every]

    weights = pl.pallas_call(
        functools.partial(load_kernel, order, blocks(1), pieces(1)),
        out_shape=held(len(blocks(1))),
        in_specs=[HBM],
        out_specs=VMEM,
        scratch_shapes=[pltpu.SemaphoreType.DMA((len(pieces(1)),))],
        compiler_params=params,
        cost_estimate=cost,
        name="load_first",
    )(weight)
    fore, aft, total = tokens, tokens, None
    for step in range(1, half):
        fore = lax.ppermute(fore, "tp", ahead)
        aft = lax.ppermute(aft, "tp", back)
        fore, total, weights = lax.optimization_barrier((fore, total, weights))
        aft, total, weights = lax.optimization_barrier((aft, total, weights))
        first = step == 1
        xs = [tokens, fore, aft] if first else [fore, aft]
        extra = [filter_taps, decay_rate, residue] if first else [total]
        made = []
        if first:
            made = [f32(lags, streams, groups, LANES), f32(5, modes, groups, LANES)]
            made += [f32(modes, 8, chans), f32(modes, chans)]
        total, weights, *made = pl.pallas_call(
            functools.partial(
                middle_kernel, order, blocks(step), left(step), blocks(step + 1), pieces(step + 1),
                len(extra),
            ),
            out_shape=[sums, held(len(blocks(step + 1)))] + made,
            in_specs=[VMEM] * (len(xs) + 1) + [HBM] + [VMEM] * len(extra),
            out_specs=[VMEM] * (2 + len(made)),
            scratch_shapes=[
                pltpu.VMEM((1, width // 2, chans), jnp.bfloat16),
                pltpu.SemaphoreType.DMA((1,)),
                pltpu.SemaphoreType.DMA((len(pieces(step + 1)),)),
            ],
            input_output_aliases={} if first else {len(xs) + 2: 0},
            compiler_params=params,
            cost_estimate=cost,
            name="project_blocks",
        )(*xs, weights, weight, *extra)
        if first:
            taps, table, *tiles = made
    fore = lax.ppermute(fore[:, : width // 2], "tp", ahead)
    aft = lax.ppermute(aft[:, width // 2 :], "tp", back)
    total = pl.pallas_call(
        half_kernel,
        out_shape=sums,
        in_specs=[VMEM] * 3,
        out_specs=VMEM,
        input_output_aliases={2: 0},
        compiler_params=params,
        cost_estimate=cost,
        name="project_half",
    )(fore, weights, total)
    total, source, local = pl.pallas_call(
        last_kernel,
        out_shape=[sums, wide, f32(modes + EDGE, groups, LANES)],
        in_specs=[VMEM] * 5,
        out_specs=[VMEM] * 3,
        scratch_shapes=[
            pltpu.VMEM((streams - 1, 8, groups, LANES), jnp.float32),
            pltpu.VMEM((streams, 8, groups, LANES), jnp.float32),
        ],
        input_output_aliases={4: 0},
        compiler_params=params,
        cost_estimate=cost,
        name="project_last",
    )(aft, weights, filter_taps, table, total)

    partner = lax.ppermute(local, "ctx", [(j, j ^ 1) for j in range(ctx)])
    lone = ctx == 4
    chip = pl.pallas_call(
        functools.partial(chip_kernel, lone),
        out_shape=f32(modes + (6 if lone else EDGE), groups, LANES),
        in_specs=[VMEM] * 4,
        out_specs=VMEM,
        compiler_params=params,
        name="chip_state",
    )(local, partner, taps, table)
    sent = [
        lax.ppermute(chip, "ctx", [(j, (j + d) % ctx) for j in range(ctx)])
        for d in range(2, ctx, 2)
    ]
    query, response, heads = pl.pallas_call(
        local_kernel,
        out_shape=[f32(rows, chans), f32(rows, chans), f32(2, groups, LANES)],
        in_specs=[VMEM] * 4,
        out_specs=[VMEM] * 3,
        scratch_shapes=[
            pltpu.VMEM((rows, groups, LANES), jnp.float32),
            pltpu.VMEM((8, groups, LANES), jnp.float32),
        ],
        compiler_params=params,
        cost_estimate=cost,
        name="local_response",
    )(total, source, filter_taps, table)
    return pl.pallas_call(
        functools.partial(final_kernel, lone, len(sent)),
        out_shape=jax.ShapeDtypeStruct((rows, chans), jnp.bfloat16),
        in_specs=[VMEM] * (len(sent) + 9),
        out_specs=HBM,
        scratch_shapes=[
            pltpu.VMEM((modes, groups, LANES), jnp.float32),
            pltpu.VMEM((2, groups, LANES), jnp.float32),
            pltpu.VMEM((rows, chans), jnp.bfloat16),
            pltpu.SemaphoreType.DMA((groups // 2,)),
        ],
        compiler_params=params,
        name="carried_response",
    )(*sent, local, partner, query, response, heads, taps, table, *tiles)


def solution(mesh):
    return jax.shard_map(
        on_device,
        mesh=mesh,
        in_specs=(
            P("ctx", "tp"),
            P(None, None, "tp"),
            P(None, None, "tp"),
            P(None, "tp"),
            P(None, "tp"),
        ),
        out_specs=P("ctx", "tp"),
        check_vma=False,
    )
```

```python
import functools

import jax
import jax.numpy as jnp
from jax import lax
from jax.experimental import pallas as pl
from jax.experimental.pallas import tpu as pltpu
from jax.sharding import PartitionSpec as P

LANES = 128
COLS = 256
WIDE = 512
SOON = 4
GRID_ROWS = 4
EDGE = 10
UNROLL = 16
VMEM = pl.BlockSpec(memory_space=pltpu.VMEM)
HBM = pl.BlockSpec(memory_space=pltpu.HBM)


def ring_order(count):
    if count % (2 * GRID_ROWS):
        return list(range(count))
    cols = count // GRID_ROWS
    cells = [(0, c) for c in range(cols)]
    for r in range(1, GRID_ROWS):
        inner = list(range(1, cols))
        cells += [(r, c) for c in (reversed(inner) if r % 2 else inner)]
    cells += [(r, 0) for r in range(GRID_ROWS - 1, 0, -1)]
    return [r * cols + c for r, c in cells]


def owner_at(order, step):
    me = lax.axis_index("tp")
    owner = jnp.int32(0)
    for place, index in enumerate(order):
        owner = jnp.where(me == index, order[(place - step) % len(order)], owner)
    return owner


def piece_loads(order, steps, pieces, w_ref, target, sem):
    width = w_ref.shape[1] // len(order)
    starts = [pl.multiple_of(owner_at(order, step) * width, width) for step in steps]
    return [
        pltpu.make_async_copy(
            w_ref.at[s, pl.ds(starts[b] + low, high - low), :], target(i, b, s, low, high), sem.at[i]
        )
        for i, (b, s, low, high) in enumerate(pieces)
    ]


def add_products(xs, weights, total, s, fresh=False, cols=COLS):
    cols = min(cols, total.shape[2])
    for c in range(0, total.shape[2], cols):
        at = slice(c, c + cols)
        terms = [
            jnp.dot(x, weights(b, at), preferred_element_type=jnp.float32) for b, x in enumerate(xs)
        ]
        total[s, :, at] = sum(terms) if fresh else total[s, :, at] + sum(terms)


def spread(out_ref, value):
    groups, lanes = out_ref.shape[-2:]
    for g in range(groups):
        out_ref[..., g, :] = value[..., g * lanes : (g + 1) * lanes]


def held_part(held):
    return lambda i, b, s, low, high: held.at[b, s, pl.ds(low, high - low), :]


def load_kernel(order, steps, pieces, w_ref, held, sem):
    copies = piece_loads(order, steps, pieces, w_ref, held_part(held), sem)
    for copy in copies:
        copy.start()
    for copy in copies:
        copy.wait()


def middle_kernel(order, here, missing, steps, pieces, inputs_count, *refs):
    xs, (held, w_ref, *refs) = refs[: len(here)], refs[len(here) :]
    *refs, rest, rest_sem, sem = refs
    inputs, (total, next_held, *made) = refs[:inputs_count], refs[inputs_count:]
    fresh = bool(made)
    late = piece_loads(order, here, missing, w_ref, lambda i, *_: rest.at[i], rest_sem)
    ahead = piece_loads(order, steps, pieces, w_ref, held_part(next_held), sem)
    for copy in late + ahead[:SOON]:
        copy.start()
    if made:
        make_tables(*inputs, *made, total.shape[1])
    whole = held.shape[1] - len(missing)

    @pl.loop(0, whole)
    def _(s):
        add_products([x[...] for x in xs], lambda b, at: held[b, s, :, at], total, s, fresh)

    for copy in ahead[SOON:]:
        copy.start()
    for copy in late:
        copy.wait()
    for i, (b, s, low, _) in enumerate(missing):
        parts = [(x[...], (lambda at, k=k: held[k, s, :, at])) for k, x in enumerate(xs) if k != b]
        parts.append((xs[b][:, :low], lambda at: held[b, s, :low, at]))
        parts.append((xs[b][:, low:], lambda at: rest[i, :, at]))
        values, weights = zip(*parts)
        add_products(values, lambda k, at: weights[k](at), total, s, fresh)
    for copy in ahead:
        copy.wait()


def half_kernel(x_ref, held, _, total):
    depth = x_ref.shape[1]
    for s in range(total.shape[0]):
        add_products([x_ref[...]], lambda b, at: held[0, s, :depth, at], total, s, cols=WIDE)


def make_tables(taps_in, decay, residue, taps, table, tile, tile_step, rows):
    rate = decay[...]
    coeffs = residue[...] * jnp.sqrt(1.0 - jnp.exp(-2.0 * rate))
    for i, power in enumerate((1, rows, rows - 1, rows - 2)):
        spread(table.at[i], jnp.exp(-rate * power))
    spread(table.at[4], coeffs)
    spread(taps, taps_in[...])
    for r in range(tile.shape[1]):
        tile[:, r, :] = coeffs * jnp.exp(-rate * (r - 1.0))
    tile_step[...] = jnp.exp(-rate * tile.shape[1])


def over_rows(step, start, stop, carry):
    aligned = -(-start // UNROLL) * UNROLL
    for t in range(start, aligned):
        carry = step(t, carry)

    def group(i, carry):
        for j in range(UNROLL):
            carry = step(i * UNROLL + j, carry)
        return carry

    return lax.fori_loop(aligned // UNROLL, stop // UNROLL, group, carry)


def filtered(taps, s, value, cols):
    one, two = pltpu.roll(value, 1, 0), pltpu.roll(value, 2, 0)
    lags = [taps[j, s : s + 1, cols] for j in range(3)]
    return lags[0] * value + lags[1] * one + lags[2] * two


def last_kernel(x_ref, held, taps, table, _, total, source, states, edges, low, high):
    depth = x_ref.shape[1]
    for s in range(total.shape[0]):
        add_products([x_ref[...]], lambda b, at: held[0, s, depth:, at], total, s, cols=WIDE)
    rows, groups, lanes = source.shape
    modes = table.shape[1]
    for g in range(groups):
        cols = slice(g * lanes, (g + 1) * lanes)
        one, two = rounded(total[1, :, cols]), rounded(total[2, :, cols])
        source[:, g, :] = filtered(taps, 1, one, cols) * filtered(taps, 2, two, cols)
        for s, value in ((1, one), (2, two)):
            low[s - 1, :, g, :] = value[:8]
            high[s, :, g, :] = value[rows - 8 :]
        high[0, :, g, :] = rounded(total[0, rows - 8 :, cols])
    rate = [table[0, n] for n in range(modes)]

    def step_row(t, state):
        u = source[t]
        return [r * s + u for r, s in zip(rate, state)]

    state = [jnp.zeros((groups, lanes), jnp.float32)] * modes
    state = over_rows(step_row, 2, rows, state)
    for n in range(modes):
        states[n] = state[n]
    for j in range(2):
        for s in (1, 2):
            edges[(s - 1) * 2 + j] = low[s - 1, j]
        for s in range(3):
            edges[4 + s * 2 + j] = high[s, 6 + j]


def rounded(value):
    return value.astype(jnp.bfloat16).astype(jnp.float32)


def tree_sum(terms):
    while len(terms) > 1:
        terms = [a + b for a, b in zip(terms[::2], terms[1::2])] + terms[len(terms) & ~1 :]
    return terms[0]


def local_kernel(total, source, taps, table, query, response, heads, work, low):
    rows, groups, lanes = source.shape
    modes = table.shape[1]
    for g in range(groups):
        cols = slice(g * lanes, (g + 1) * lanes)
        value = rounded(total[0, :, cols])
        query[:, cols] = filtered(taps, 0, value, cols)
        low[:, g, :] = value[:8]
    for j in range(2):
        heads[j] = low[j]
        work[j] = jnp.zeros((groups, lanes), jnp.float32)

    def step_row(t, state):
        u = source[t]
        state = [table[0, n] * state[n] + u for n in range(modes)]
        work[t] = tree_sum([table[4, n] * state[n] for n in range(modes)])
        return state

    over_rows(step_row, 2, rows, [jnp.zeros((groups, lanes), jnp.float32)] * modes)
    for g in range(groups):
        response[:, g * lanes : (g + 1) * lanes] = work[:, g, :]


def edge(taps, s, first, second, before, last):
    return (
        taps[0, s] * first + taps[1, s] * last + taps[2, s] * before,
        taps[0, s] * second + taps[1, s] * first + taps[2, s] * last,
    )


def lead_sources(taps, heads, rims):
    one = edge(taps, 1, heads[0], heads[1], rims[2], rims[3])
    two = edge(taps, 2, heads[2], heads[3], rims[4], rims[5])
    return one[0] * two[0], one[1] * two[1]


class Summary:
    def __init__(self, rows, modes):
        self.state = rows[:modes]
        self.heads = rows[modes : modes + 4]
        self.rims = rows[modes + 4 :]

    @classmethod
    def read(cls, states, edges):
        return cls([ref[i] for ref in (states, edges) for i in range(ref.shape[0])], states.shape[0])

    @classmethod
    def chosen(cls, odd, when_odd, when_even, modes):
        pairs = zip(when_odd.rows(), when_even.rows())
        return cls([jnp.where(odd, a, b) for a, b in pairs], modes)

    def rows(self):
        return self.state + self.heads + self.rims

    def complete(self, taps, rims, by_first, by_second):
        u0, u1 = lead_sources(taps, self.heads, rims)
        return [x + f * u0 + g * u1 for x, f, g in zip(self.state, by_first, by_second)]


def powers(table):
    return [[table[i, n] for n in range(table.shape[1])] for i in range(table.shape[0])]


def chip_kernel(lone, states, edges, other_states, other_edges, taps, table, out_states, out_edges):
    modes = table.shape[1]
    odd = lax.rem(lax.axis_index("ctx"), 2) == 1
    mine, other = Summary.read(states, edges), Summary.read(other_states, other_edges)
    first = Summary.chosen(odd, other, mine, modes)
    second = Summary.chosen(odd, mine, other, modes)
    _, block, less_one, less_two, _ = powers(table)
    start, heads = first.state, first.heads
    if lone:
        start, heads = first.complete(taps, [jnp.zeros_like(heads[0])] * 6, less_one, less_two), []
    end = second.complete(taps, first.rims, less_one, less_two)
    joined = [d * x + y for d, x, y in zip(block, start, end)]
    for i, value in enumerate(joined):
        out_states[i] = value
    for i, value in enumerate(heads + second.rims):
        out_edges[i] = value


def final_kernel(lone, count, *refs):
    sent, sent_edges = refs[:count], refs[count : 2 * count]
    own_edges, other_states, other_edges, query, response, *refs = refs[2 * count :]
    query_heads, taps, table, tile, tile_step, out_ref, states, firsts, rounded_out, out_sem = refs
    rows = query.shape[0]
    groups, lanes = own_edges.shape[1:]
    modes = table.shape[1]
    zero = jnp.zeros((groups, lanes), jnp.float32)
    index = lax.axis_index("ctx")
    odd = lax.rem(index, 2) == 1
    _, block, less_one, less_two, _ = powers(table)
    values = [
        [
            jnp.where(index >= 2 * (d + 1), ref[i], zero)
            for ref in (sent[d], sent_edges[d])
            for i in range(ref.shape[0])
        ]
        for d in range(count)
    ]
    rims = [value[-6:] for value in values] + [[zero] * 6]
    state = [zero] * modes
    for d in reversed(range(count)):
        end = values[d][:modes]
        if not lone:
            end = Summary(values[d], modes).complete(
                taps,
                rims[d + 1],
                [a * b for a, b in zip(block, less_one)],
                [a * b for a, b in zip(block, less_two)],
            )
        state = [d * d * x + y for d, x, y in zip(block, state, end)]
    before = Summary.read(other_states, other_edges)
    end = before.complete(taps, rims[0], less_one, less_two)
    state = [jnp.where(odd, d * x + y, x) for d, x, y in zip(block, state, end)]
    rim = [jnp.where(odd, a, b) for a, b in zip(before.rims, rims[0])]

    leads = lead_sources(taps, [own_edges[i] for i in range(4)], rim)
    heads = edge(taps, 0, query_heads[0], query_heads[1], rim[0], rim[1])
    for t, u in enumerate(leads):
        state = [table[0, n] * state[n] + u for n in range(modes)]
        firsts[t] = heads[t] * tree_sum([table[4, n] * state[n] for n in range(modes)])
    for n in range(modes):
        states[n] = state[n]

    tall = tile.shape[1]
    row = lax.broadcasted_iota(jnp.int32, (tall, lanes), 0)
    copies = []
    for g in range(groups):
        cols = slice(g * lanes, (g + 1) * lanes)
        carried = [tile[n, :, cols] * states[n, g : g + 1, :] for n in range(modes)]
        step = [jnp.broadcast_to(tile_step[n : n + 1, cols], (tall, lanes)) for n in range(modes)]
        for i in range(0, rows, 2 * tall):
            pair = []
            for at in (slice(i, i + tall), slice(i + tall, i + 2 * tall)):
                value = query[at, cols] * (response[at, cols] + tree_sum(carried))
                if at.start == 0:
                    value = jnp.where(row == 0, firsts[0, g : g + 1, :], value)
                    value = jnp.where(row == 1, firsts[1, g : g + 1, :], value)
                pair.append(value)
                carried = [a * b for a, b in zip(carried, step)]
            rounded_out[i : i + 2 * tall, cols] = jnp.concatenate(pair, axis=0).astype(out_ref.dtype)
        if g % 2:
            wide = slice((g - 1) * lanes, (g + 1) * lanes)
            k = g // 2
            copies.append(
                pltpu.make_async_copy(rounded_out.at[:, wide], out_ref.at[:, wide], out_sem.at[k])
            )
            copies[-1].start()
    for copy in copies:
        copy.wait()


def on_device(tokens, in_weight, filter_taps, decay_rate, residue):
    rows, width = tokens.shape
    streams, chans = in_weight.shape[1:]
    lags = filter_taps.shape[0]
    modes = decay_rate.shape[0]
    groups = chans // LANES
    tp, ctx = lax.axis_size("tp"), lax.axis_size("ctx")
    order = ring_order(tp)
    weight = jnp.transpose(in_weight, (1, 0, 2))
    half = tp // 2
    ahead = [(order[i], order[(i + 1) % tp]) for i in range(tp)]
    back = [(b, a) for a, b in ahead]

    def f32(*shape):
        return jax.ShapeDtypeStruct(shape, jnp.float32)

    def held(count):
        return jax.ShapeDtypeStruct((count, streams, width, chans), jnp.bfloat16)

    def loads(step):
        return [step, -step] if step < half else [step]

    sums = f32(streams, rows, chans)
    wide = f32(rows, groups, LANES)
    params = pltpu.CompilerParams(vmem_limit_bytes=12 << 20)
    cost = pl.CostEstimate(flops=0, bytes_accessed=16 << 20, transcendentals=0)

    def blocks(step):
        return [0] + loads(1) if step == 1 else loads(step)

    def left(step):
        rows_left = (width // 2, width)
        return [(len(blocks(step)) - 1, streams - 1, *rows_left)] if step % 2 and step < half else []

    def pieces(step):
        lacking = {(b, s): low for b, s, low, _ in left(step)}
        every = [(b, s) for s in range(streams) for b in range(len(blocks(step)))]
        return [(b, s, 0, lacking.get((b, s), width)) for b, s in every]

    weights = pl.pallas_call(
        functools.partial(load_kernel, order, blocks(1), pieces(1)),
        out_shape=held(len(blocks(1))),
        in_specs=[HBM],
        out_specs=VMEM,
        scratch_shapes=[pltpu.SemaphoreType.DMA((len(pieces(1)),))],
        compiler_params=params,
        cost_estimate=cost,
        name="load_first",
    )(weight)
    fore, aft, total = tokens, tokens, None
    for step in range(1, half):
        fore = lax.ppermute(fore, "tp", ahead)
        aft = lax.ppermute(aft, "tp", back)
        fore, total, weights = lax.optimization_barrier((fore, total, weights))
        aft, total, weights = lax.optimization_barrier((aft, total, weights))
        first = step == 1
        xs = [tokens, fore, aft] if first else [fore, aft]
        extra = [filter_taps, decay_rate, residue] if first else [total]
        made = []
        if first:
            made = [f32(lags, streams, groups, LANES), f32(5, modes, groups, LANES)]
            made += [f32(modes, 8, chans), f32(modes, chans)]
        total, weights, *made = pl.pallas_call(
            functools.partial(
                middle_kernel, order, blocks(step), left(step), blocks(step + 1), pieces(step + 1),
                len(extra),
            ),
            out_shape=[sums, held(len(blocks(step + 1)))] + made,
            in_specs=[VMEM] * (len(xs) + 1) + [HBM] + [VMEM] * len(extra),
            out_specs=[VMEM] * (2 + len(made)),
            scratch_shapes=[
                pltpu.VMEM((1, width // 2, chans), jnp.bfloat16),
                pltpu.SemaphoreType.DMA((1,)),
                pltpu.SemaphoreType.DMA((len(pieces(step + 1)),)),
            ],
            input_output_aliases={} if first else {len(xs) + 2: 0},
            compiler_params=params,
            cost_estimate=cost,
            name="project_blocks",
        )(*xs, weights, weight, *extra)
        if first:
            taps, table, *tiles = made
    fore = lax.ppermute(fore[:, : width // 2], "tp", ahead)
    aft = lax.ppermute(aft[:, width // 2 :], "tp", back)
    states, edges = f32(modes, groups, LANES), f32(EDGE, groups, LANES)
    total = pl.pallas_call(
        half_kernel,
        out_shape=sums,
        in_specs=[VMEM] * 3,
        out_specs=VMEM,
        input_output_aliases={2: 0},
        compiler_params=params,
        cost_estimate=cost,
        name="project_half",
    )(fore, weights, total)
    total, source, *local = pl.pallas_call(
        last_kernel,
        out_shape=[sums, wide, states, edges],
        in_specs=[VMEM] * 5,
        out_specs=[VMEM] * 4,
        scratch_shapes=[
            pltpu.VMEM((streams - 1, 8, groups, LANES), jnp.float32),
            pltpu.VMEM((streams, 8, groups, LANES), jnp.float32),
        ],
        input_output_aliases={4: 0},
        compiler_params=params,
        cost_estimate=cost,
        name="project_last",
    )(aft, weights, filter_taps, table, total)

    partner = [lax.ppermute(part, "ctx", [(j, j ^ 1) for j in range(ctx)]) for part in local]
    lone = ctx == 4
    chip = pl.pallas_call(
        functools.partial(chip_kernel, lone),
        out_shape=[states, f32(6, groups, LANES) if lone else edges],
        in_specs=[VMEM] * 6,
        out_specs=[VMEM] * 2,
        compiler_params=params,
        name="chip_state",
    )(*local, *partner, taps, table)
    sent = [
        lax.ppermute(part, "ctx", [(j, (j + d) % ctx) for j in range(ctx)])
        for part in chip
        for d in range(2, ctx, 2)
    ]
    query, response, heads = pl.pallas_call(
        local_kernel,
        out_shape=[f32(rows, chans), f32(rows, chans), f32(2, groups, LANES)],
        in_specs=[VMEM] * 4,
        out_specs=[VMEM] * 3,
        scratch_shapes=[
            pltpu.VMEM((rows, groups, LANES), jnp.float32),
            pltpu.VMEM((8, groups, LANES), jnp.float32),
        ],
        compiler_params=params,
        cost_estimate=cost,
        name="local_response",
    )(total, source, filter_taps, table)
    return pl.pallas_call(
        functools.partial(final_kernel, lone, len(sent) // 2),
        out_shape=jax.ShapeDtypeStruct((rows, chans), jnp.bfloat16),
        in_specs=[VMEM] * (len(sent) + 10),
        out_specs=HBM,
        scratch_shapes=[
            pltpu.VMEM((modes, groups, LANES), jnp.float32),
            pltpu.VMEM((2, groups, LANES), jnp.float32),
            pltpu.VMEM((rows, chans), jnp.bfloat16),
            pltpu.SemaphoreType.DMA((groups // 2,)),
        ],
        compiler_params=params,
        name="carried_response",
    )(*sent, local[1], *partner, query, response, heads, taps, table, *tiles)


def solution(mesh):
    return jax.shard_map(
        on_device,
        mesh=mesh,
        in_specs=(
            P("ctx", "tp"),
            P(None, None, "tp"),
            P(None, None, "tp"),
            P(None, "tp"),
            P(None, "tp"),
        ),
        out_specs=P("ctx", "tp"),
        check_vma=False,
    )
```

```python
import functools

import jax
import jax.numpy as jnp
from jax import lax
from jax.experimental import pallas as pl
from jax.experimental.pallas import tpu as pltpu
from jax.sharding import PartitionSpec as P

LANES = 128
COLS = 256
WIDE = 512
SOON = 4
GRID_ROWS = 4
EDGE = 10
UNROLL = 16
VMEM = pl.BlockSpec(memory_space=pltpu.VMEM)
HBM = pl.BlockSpec(memory_space=pltpu.HBM)


def ring_order(count):
    if count % (2 * GRID_ROWS):
        return list(range(count))
    cols = count // GRID_ROWS
    cells = [(0, c) for c in range(cols)]
    for r in range(1, GRID_ROWS):
        inner = list(range(1, cols))
        cells += [(r, c) for c in (reversed(inner) if r % 2 else inner)]
    cells += [(r, 0) for r in range(GRID_ROWS - 1, 0, -1)]
    return [r * cols + c for r, c in cells]


def owner_at(order, step):
    me = lax.axis_index("tp")
    owner = jnp.int32(0)
    for place, index in enumerate(order):
        owner = jnp.where(me == index, order[(place - step) % len(order)], owner)
    return owner


def piece_loads(order, steps, pieces, w_ref, target, sem):
    width = w_ref.shape[1] // len(order)
    starts = [pl.multiple_of(owner_at(order, step) * width, width) for step in steps]
    return [
        pltpu.make_async_copy(
            w_ref.at[s, pl.ds(starts[b] + low, high - low), :], target(i, b, s, low, high), sem.at[i]
        )
        for i, (b, s, low, high) in enumerate(pieces)
    ]


def add_products(xs, weights, total, s, fresh=False, cols=COLS):
    cols = min(cols, total.shape[2])
    for c in range(0, total.shape[2], cols):
        at = slice(c, c + cols)
        terms = [
            jnp.dot(x, weights(b, at), preferred_element_type=jnp.float32) for b, x in enumerate(xs)
        ]
        total[s, :, at] = sum(terms) if fresh else total[s, :, at] + sum(terms)


def spread(out_ref, value):
    groups, lanes = out_ref.shape[-2:]
    for g in range(groups):
        out_ref[..., g, :] = value[..., g * lanes : (g + 1) * lanes]


def held_part(held):
    return lambda i, b, s, low, high: held.at[b, s, pl.ds(low, high - low), :]


def load_kernel(order, steps, pieces, w_ref, held, sem):
    copies = piece_loads(order, steps, pieces, w_ref, held_part(held), sem)
    for copy in copies:
        copy.start()
    for copy in copies:
        copy.wait()


def middle_kernel(order, here, missing, steps, pieces, inputs_count, *refs):
    xs, (held, w_ref, *refs) = refs[: len(here)], refs[len(here) :]
    *refs, rest, rest_sem, sem = refs
    inputs, (total, next_held, *made) = refs[:inputs_count], refs[inputs_count:]
    fresh = bool(made)
    late = piece_loads(order, here, missing, w_ref, lambda i, *_: rest.at[i], rest_sem)
    ahead = piece_loads(order, steps, pieces, w_ref, held_part(next_held), sem)
    for copy in late + ahead[:SOON]:
        copy.start()
    if made:
        make_tables(*inputs, *made, total.shape[1])
    whole = held.shape[1] - len(missing)

    @pl.loop(0, whole)
    def _(s):
        add_products([x[...] for x in xs], lambda b, at: held[b, s, :, at], total, s, fresh)

    for copy in ahead[SOON:]:
        copy.start()
    for copy in late:
        copy.wait()
    for i, (b, s, low, _) in enumerate(missing):
        parts = [(x[...], (lambda at, k=k: held[k, s, :, at])) for k, x in enumerate(xs) if k != b]
        parts.append((xs[b][:, :low], lambda at: held[b, s, :low, at]))
        parts.append((xs[b][:, low:], lambda at: rest[i, :, at]))
        values, weights = zip(*parts)
        add_products(values, lambda k, at: weights[k](at), total, s, fresh)
    for copy in ahead:
        copy.wait()


def half_kernel(x_ref, held, _, total):
    depth = x_ref.shape[1]
    for s in range(total.shape[0]):
        add_products([x_ref[...]], lambda b, at: held[0, s, :depth, at], total, s, cols=WIDE)


def make_tables(taps_in, decay, residue, taps, table, tile, tile_step, rows):
    rate = decay[...]
    coeffs = residue[...] * jnp.sqrt(1.0 - jnp.exp(-2.0 * rate))
    for i, power in enumerate((1, rows, rows - 1, rows - 2)):
        spread(table.at[i], jnp.exp(-rate * power))
    spread(table.at[4], coeffs)
    spread(taps, taps_in[...])
    for r in range(tile.shape[1]):
        tile[:, r, :] = coeffs * jnp.exp(-rate * (r - 1.0))
    tile_step[...] = jnp.exp(-rate * tile.shape[1])


def over_rows(step, start, stop, carry):
    aligned = -(-start // UNROLL) * UNROLL
    for t in range(start, aligned):
        carry = step(t, carry)

    def group(i, carry):
        for j in range(UNROLL):
            carry = step(i * UNROLL + j, carry)
        return carry

    return lax.fori_loop(aligned // UNROLL, stop // UNROLL, group, carry)


def filtered(taps, s, value, cols):
    one, two = pltpu.roll(value, 1, 0), pltpu.roll(value, 2, 0)
    lags = [taps[j, s : s + 1, cols] for j in range(3)]
    return lags[0] * value + lags[1] * one + lags[2] * two


def last_kernel(x_ref, held, taps, table, _, total, source, out_ref, low, high):
    depth = x_ref.shape[1]
    rows, groups, lanes = source.shape
    modes = table.shape[1]
    for c in range(0, total.shape[2], COLS):
        at = slice(c, c + COLS)
        sums = [
            total[s, :, at]
            + jnp.dot(x_ref[...], held[0, s, depth:, at], preferred_element_type=jnp.float32)
            for s in range(3)
        ]
        total[0, :, at] = sums[0]
        projected = [rounded(value) for value in sums[1:]]
        for g in range(c // lanes, (c + COLS) // lanes):
            cols = slice(g * lanes, (g + 1) * lanes)
            one, two = [value[:, g * lanes - c : (g + 1) * lanes - c] for value in projected]
            source[:, g, :] = filtered(taps, 1, one, cols) * filtered(taps, 2, two, cols)
            for s, value in ((1, one), (2, two)):
                low[s - 1, :, g, :] = value[:8]
                high[s, :, g, :] = value[rows - 8 :]
            high[0, :, g, :] = rounded(sums[0][rows - 8 :, g * lanes - c : (g + 1) * lanes - c])
    rate = [table[0, n] for n in range(modes)]

    def step_row(t, state):
        u = source[t]
        return [r * s + u for r, s in zip(rate, state)]

    state = [jnp.zeros((groups, lanes), jnp.float32)] * modes
    state = over_rows(step_row, 2, rows, state)
    for n in range(modes):
        out_ref[n] = state[n]
    for j in range(2):
        for s in (1, 2):
            out_ref[modes + (s - 1) * 2 + j] = low[s - 1, j]
        for s in range(3):
            out_ref[modes + 4 + s * 2 + j] = high[s, 6 + j]


def rounded(value):
    return value.astype(jnp.bfloat16).astype(jnp.float32)


def tree_sum(terms):
    while len(terms) > 1:
        terms = [a + b for a, b in zip(terms[::2], terms[1::2])] + terms[len(terms) & ~1 :]
    return terms[0]


def local_kernel(total, source, taps, table, query, response, heads, work, low):
    rows, groups, lanes = source.shape
    modes = table.shape[1]
    for g in range(groups):
        cols = slice(g * lanes, (g + 1) * lanes)
        value = rounded(total[0, :, cols])
        query[:, cols] = filtered(taps, 0, value, cols)
        low[:, g, :] = value[:8]
    for j in range(2):
        heads[j] = low[j]
        work[j] = jnp.zeros((groups, lanes), jnp.float32)

    def step_row(t, state):
        u = source[t]
        state = [table[0, n] * state[n] + u for n in range(modes)]
        work[t] = tree_sum([table[4, n] * state[n] for n in range(modes)])
        return state

    over_rows(step_row, 2, rows, [jnp.zeros((groups, lanes), jnp.float32)] * modes)
    for g in range(groups):
        response[:, g * lanes : (g + 1) * lanes] = work[:, g, :]


def edge(taps, s, first, second, before, last):
    return (
        taps[0, s] * first + taps[1, s] * last + taps[2, s] * before,
        taps[0, s] * second + taps[1, s] * first + taps[2, s] * last,
    )


def lead_sources(taps, heads, rims):
    one = edge(taps, 1, heads[0], heads[1], rims[2], rims[3])
    two = edge(taps, 2, heads[2], heads[3], rims[4], rims[5])
    return one[0] * two[0], one[1] * two[1]


class Summary:
    def __init__(self, rows, modes):
        self.state = rows[:modes]
        self.heads = rows[modes : modes + 4]
        self.rims = rows[modes + 4 :]

    @classmethod
    def read(cls, ref, modes):
        return cls([ref[i] for i in range(ref.shape[0])], modes)

    @classmethod
    def chosen(cls, odd, when_odd, when_even, modes):
        pairs = zip(when_odd.rows(), when_even.rows())
        return cls([jnp.where(odd, a, b) for a, b in pairs], modes)

    def rows(self):
        return self.state + self.heads + self.rims

    def complete(self, taps, rims, by_first, by_second):
        u0, u1 = lead_sources(taps, self.heads, rims)
        return [x + f * u0 + g * u1 for x, f, g in zip(self.state, by_first, by_second)]


def powers(table):
    return [[table[i, n] for n in range(table.shape[1])] for i in range(table.shape[0])]


def chip_kernel(lone, local, partner, taps, table, out_ref):
    modes = table.shape[1]
    odd = lax.rem(lax.axis_index("ctx"), 2) == 1
    mine, other = Summary.read(local, modes), Summary.read(partner, modes)
    first = Summary.chosen(odd, other, mine, modes)
    second = Summary.chosen(odd, mine, other, modes)
    _, block, less_one, less_two, _ = powers(table)
    start, heads = first.state, first.heads
    if lone:
        start, heads = first.complete(taps, [jnp.zeros_like(heads[0])] * 6, less_one, less_two), []
    end = second.complete(taps, first.rims, less_one, less_two)
    joined = [d * x + y for d, x, y in zip(block, start, end)]
    for i, value in enumerate(joined + heads + second.rims):
        out_ref[i] = value


def final_kernel(lone, count, *refs):
    sent = refs[:count]
    local, partner, query, response, query_heads, taps, table, tile, tile_step, *refs = refs[count:]
    out_ref, states, firsts, rounded_out, out_sem = refs
    rows = query.shape[0]
    groups, lanes = local.shape[1:]
    modes = table.shape[1]
    zero = jnp.zeros((groups, lanes), jnp.float32)
    index = lax.axis_index("ctx")
    odd = lax.rem(index, 2) == 1
    _, block, less_one, less_two, _ = powers(table)
    values = [
        [jnp.where(index >= 2 * (d + 1), ref[i], zero) for i in range(ref.shape[0])]
        for d, ref in enumerate(sent)
    ]
    rims = [value[-6:] for value in values] + [[zero] * 6]
    state = [zero] * modes
    for d in reversed(range(count)):
        end = values[d][:modes]
        if not lone:
            end = Summary(values[d], modes).complete(
                taps,
                rims[d + 1],
                [a * b for a, b in zip(block, less_one)],
                [a * b for a, b in zip(block, less_two)],
            )
        state = [d * d * x + y for d, x, y in zip(block, state, end)]
    before = Summary.read(partner, modes)
    end = before.complete(taps, rims[0], less_one, less_two)
    state = [jnp.where(odd, d * x + y, x) for d, x, y in zip(block, state, end)]
    rim = [jnp.where(odd, a, b) for a, b in zip(before.rims, rims[0])]

    leads = lead_sources(taps, Summary.read(local, modes).heads, rim)
    heads = edge(taps, 0, query_heads[0], query_heads[1], rim[0], rim[1])
    for t, u in enumerate(leads):
        state = [table[0, n] * state[n] + u for n in range(modes)]
        firsts[t] = heads[t] * tree_sum([table[4, n] * state[n] for n in range(modes)])
    for n in range(modes):
        states[n] = state[n]

    tall = tile.shape[1]
    row = lax.broadcasted_iota(jnp.int32, (tall, lanes), 0)
    copies = []
    for g in range(groups):
        cols = slice(g * lanes, (g + 1) * lanes)
        carried = [tile[n, :, cols] * states[n, g : g + 1, :] for n in range(modes)]
        step = [jnp.broadcast_to(tile_step[n : n + 1, cols], (tall, lanes)) for n in range(modes)]
        for i in range(0, rows, 2 * tall):
            pair = []
            for at in (slice(i, i + tall), slice(i + tall, i + 2 * tall)):
                value = query[at, cols] * (response[at, cols] + tree_sum(carried))
                if at.start == 0:
                    value = jnp.where(row == 0, firsts[0, g : g + 1, :], value)
                    value = jnp.where(row == 1, firsts[1, g : g + 1, :], value)
                pair.append(value)
                carried = [a * b for a, b in zip(carried, step)]
            rounded_out[i : i + 2 * tall, cols] = jnp.concatenate(pair, axis=0).astype(out_ref.dtype)
        if g % 2:
            wide = slice((g - 1) * lanes, (g + 1) * lanes)
            k = g // 2
            copies.append(
                pltpu.make_async_copy(rounded_out.at[:, wide], out_ref.at[:, wide], out_sem.at[k])
            )
            copies[-1].start()
    for copy in copies:
        copy.wait()


def on_device(tokens, in_weight, filter_taps, decay_rate, residue):
    rows, width = tokens.shape
    streams, chans = in_weight.shape[1:]
    lags = filter_taps.shape[0]
    modes = decay_rate.shape[0]
    groups = chans // LANES
    tp, ctx = lax.axis_size("tp"), lax.axis_size("ctx")
    order = ring_order(tp)
    weight = jnp.transpose(in_weight, (1, 0, 2))
    half = tp // 2
    ahead = [(order[i], order[(i + 1) % tp]) for i in range(tp)]
    back = [(b, a) for a, b in ahead]

    def f32(*shape):
        return jax.ShapeDtypeStruct(shape, jnp.float32)

    def held(count):
        return jax.ShapeDtypeStruct((count, streams, width, chans), jnp.bfloat16)

    def loads(step):
        return [step, -step] if step < half else [step]

    sums = f32(streams, rows, chans)
    wide = f32(rows, groups, LANES)
    params = pltpu.CompilerParams(vmem_limit_bytes=12 << 20)
    cost = pl.CostEstimate(flops=0, bytes_accessed=16 << 20, transcendentals=0)

    def blocks(step):
        return [0] + loads(1) if step == 1 else loads(step)

    def left(step):
        rows_left = (width // 2, width)
        return [(len(blocks(step)) - 1, streams - 1, *rows_left)] if step % 2 and step < half else []

    def pieces(step):
        lacking = {(b, s): low for b, s, low, _ in left(step)}
        every = [(b, s) for s in range(streams) for b in range(len(blocks(step)))]
        return [(b, s, 0, lacking.get((b, s), width)) for b, s in every]

    weights = pl.pallas_call(
        functools.partial(load_kernel, order, blocks(1), pieces(1)),
        out_shape=held(len(blocks(1))),
        in_specs=[HBM],
        out_specs=VMEM,
        scratch_shapes=[pltpu.SemaphoreType.DMA((len(pieces(1)),))],
        compiler_params=params,
        cost_estimate=cost,
        name="load_first",
    )(weight)
    fore, aft, total = tokens, tokens, None
    for step in range(1, half):
        fore = lax.ppermute(fore, "tp", ahead)
        aft = lax.ppermute(aft, "tp", back)
        fore, total, weights = lax.optimization_barrier((fore, total, weights))
        aft, total, weights = lax.optimization_barrier((aft, total, weights))
        first = step == 1
        xs = [tokens, fore, aft] if first else [fore, aft]
        extra = [filter_taps, decay_rate, residue] if first else [total]
        made = []
        if first:
            made = [f32(lags, streams, groups, LANES), f32(5, modes, groups, LANES)]
            made += [f32(modes, 8, chans), f32(modes, chans)]
        total, weights, *made = pl.pallas_call(
            functools.partial(
                middle_kernel, order, blocks(step), left(step), blocks(step + 1), pieces(step + 1),
                len(extra),
            ),
            out_shape=[sums, held(len(blocks(step + 1)))] + made,
            in_specs=[VMEM] * (len(xs) + 1) + [HBM] + [VMEM] * len(extra),
            out_specs=[VMEM] * (2 + len(made)),
            scratch_shapes=[
                pltpu.VMEM((1, width // 2, chans), jnp.bfloat16),
                pltpu.SemaphoreType.DMA((1,)),
                pltpu.SemaphoreType.DMA((len(pieces(step + 1)),)),
            ],
            input_output_aliases={} if first else {len(xs) + 2: 0},
            compiler_params=params,
            cost_estimate=cost,
            name="project_blocks",
        )(*xs, weights, weight, *extra)
        if first:
            taps, table, *tiles = made
    fore = lax.ppermute(fore[:, : width // 2], "tp", ahead)
    aft = lax.ppermute(aft[:, width // 2 :], "tp", back)
    total = pl.pallas_call(
        half_kernel,
        out_shape=sums,
        in_specs=[VMEM] * 3,
        out_specs=VMEM,
        input_output_aliases={2: 0},
        compiler_params=params,
        cost_estimate=cost,
        name="project_half",
    )(fore, weights, total)
    total, source, local = pl.pallas_call(
        last_kernel,
        out_shape=[sums, wide, f32(modes + EDGE, groups, LANES)],
        in_specs=[VMEM] * 5,
        out_specs=[VMEM] * 3,
        scratch_shapes=[
            pltpu.VMEM((streams - 1, 8, groups, LANES), jnp.float32),
            pltpu.VMEM((streams, 8, groups, LANES), jnp.float32),
        ],
        input_output_aliases={4: 0},
        compiler_params=params,
        cost_estimate=cost,
        name="project_last",
    )(aft, weights, filter_taps, table, total)

    partner = lax.ppermute(local, "ctx", [(j, j ^ 1) for j in range(ctx)])
    lone = ctx == 4
    chip = pl.pallas_call(
        functools.partial(chip_kernel, lone),
        out_shape=f32(modes + (6 if lone else EDGE), groups, LANES),
        in_specs=[VMEM] * 4,
        out_specs=VMEM,
        compiler_params=params,
        name="chip_state",
    )(local, partner, taps, table)
    sent = [
        lax.ppermute(chip, "ctx", [(j, (j + d) % ctx) for j in range(ctx)])
        for d in range(2, ctx, 2)
    ]
    query, response, heads = pl.pallas_call(
        local_kernel,
        out_shape=[f32(rows, chans), f32(rows, chans), f32(2, groups, LANES)],
        in_specs=[VMEM] * 4,
        out_specs=[VMEM] * 3,
        scratch_shapes=[
            pltpu.VMEM((rows, groups, LANES), jnp.float32),
            pltpu.VMEM((8, groups, LANES), jnp.float32),
        ],
        compiler_params=params,
        cost_estimate=cost,
        name="local_response",
    )(total, source, filter_taps, table)
    return pl.pallas_call(
        functools.partial(final_kernel, lone, len(sent)),
        out_shape=jax.ShapeDtypeStruct((rows, chans), jnp.bfloat16),
        in_specs=[VMEM] * (len(sent) + 9),
        out_specs=HBM,
        scratch_shapes=[
            pltpu.VMEM((modes, groups, LANES), jnp.float32),
            pltpu.VMEM((2, groups, LANES), jnp.float32),
            pltpu.VMEM((rows, chans), jnp.bfloat16),
            pltpu.SemaphoreType.DMA((groups // 2,)),
        ],
        compiler_params=params,
        name="carried_response",
    )(*sent, local, partner, query, response, heads, taps, table, *tiles)


def solution(mesh):
    return jax.shard_map(
        on_device,
        mesh=mesh,
        in_specs=(
            P("ctx", "tp"),
            P(None, None, "tp"),
            P(None, None, "tp"),
            P(None, "tp"),
            P(None, "tp"),
        ),
        out_specs=P("ctx", "tp"),
        check_vma=False,
    )
```

```python
import functools

import jax
import jax.numpy as jnp
from jax import lax
from jax.experimental import pallas as pl
from jax.experimental.pallas import tpu as pltpu
from jax.sharding import PartitionSpec as P

LANES = 128
COLS = 256
WIDE = 512
SOON = 4
GRID_ROWS = 4
EDGE = 10
UNROLL = 16
VMEM = pl.BlockSpec(memory_space=pltpu.VMEM)
HBM = pl.BlockSpec(memory_space=pltpu.HBM)


def ring_order(count):
    if count % (2 * GRID_ROWS):
        return list(range(count))
    cols = count // GRID_ROWS
    cells = [(0, c) for c in range(cols)]
    for r in range(1, GRID_ROWS):
        inner = list(range(1, cols))
        cells += [(r, c) for c in (reversed(inner) if r % 2 else inner)]
    cells += [(r, 0) for r in range(GRID_ROWS - 1, 0, -1)]
    return [r * cols + c for r, c in cells]


def owner_at(order, step):
    me = lax.axis_index("tp")
    owner = jnp.int32(0)
    for place, index in enumerate(order):
        owner = jnp.where(me == index, order[(place - step) % len(order)], owner)
    return owner


def piece_loads(order, steps, pieces, w_ref, target, sem):
    width = w_ref.shape[1] // len(order)
    starts = [pl.multiple_of(owner_at(order, step) * width, width) for step in steps]
    return [
        pltpu.make_async_copy(
            w_ref.at[s, pl.ds(starts[b] + low, high - low), :], target(i, b, s, low, high), sem.at[i]
        )
        for i, (b, s, low, high) in enumerate(pieces)
    ]


def add_products(xs, weights, total, s, fresh=False, cols=COLS):
    cols = min(cols, total.shape[2])
    for c in range(0, total.shape[2], cols):
        at = slice(c, c + cols)
        terms = [
            jnp.dot(x, weights(b, at), preferred_element_type=jnp.float32) for b, x in enumerate(xs)
        ]
        total[s, :, at] = sum(terms) if fresh else total[s, :, at] + sum(terms)


def spread(out_ref, value):
    groups, lanes = out_ref.shape[-2:]
    for g in range(groups):
        out_ref[..., g, :] = value[..., g * lanes : (g + 1) * lanes]


def held_part(held):
    return lambda i, b, s, low, high: held.at[b, s, pl.ds(low, high - low), :]


def load_kernel(order, steps, pieces, w_ref, held, sem):
    copies = piece_loads(order, steps, pieces, w_ref, held_part(held), sem)
    for copy in copies:
        copy.start()
    for copy in copies:
        copy.wait()


def middle_kernel(order, here, missing, steps, pieces, inputs_count, *refs):
    xs, (held, w_ref, *refs) = refs[: len(here)], refs[len(here) :]
    *refs, rest, rest_sem, sem = refs
    inputs, (total, next_held, *made) = refs[:inputs_count], refs[inputs_count:]
    fresh = bool(made)
    late = piece_loads(
        order, here, missing, w_ref,
        lambda i, b, s, low, high: rest.at[i, pl.ds(0, high - low), :], rest_sem,
    )
    ahead = piece_loads(order, steps, pieces, w_ref, held_part(next_held), sem)
    soon = max(SOON - len(late), 0)
    for copy in late + ahead[:soon]:
        copy.start()
    if made:
        make_tables(*inputs, *made, total.shape[1])
    whole = min(s for _, s, _, _ in missing) if missing else held.shape[1]

    @pl.loop(0, whole)
    def _(s):
        add_products([x[...] for x in xs], lambda b, at: held[b, s, :, at], total, s, fresh)

    for copy in ahead[soon:]:
        copy.start()
    for copy in late:
        copy.wait()
    for s in range(whole, held.shape[1]):
        gaps = {b: (i, low, high) for i, (b, k, low, high) in enumerate(missing) if k == s}
        parts = []
        for b, x in enumerate(xs):
            i, low, high = gaps.get(b, (0, x.shape[1], x.shape[1]))
            if low:
                parts.append((x[:, :low], lambda at, b=b, low=low: held[b, s, :low, at]))
            if low < high:
                parts.append((x[:, low:], lambda at, i=i, n=high - low: rest[i, :n, at]))
        values, weights = zip(*parts)
        add_products(values, lambda k, at: weights[k](at), total, s, fresh)
    for copy in ahead:
        copy.wait()


def half_kernel(x_ref, held, _, total):
    depth = x_ref.shape[1]
    for s in range(total.shape[0]):
        add_products([x_ref[...]], lambda b, at: held[0, s, :depth, at], total, s, cols=WIDE)


def make_tables(taps_in, decay, residue, taps, table, tile, tile_step, rows):
    rate = decay[...]
    coeffs = residue[...] * jnp.sqrt(1.0 - jnp.exp(-2.0 * rate))
    for i, power in enumerate((1, rows, rows - 1, rows - 2)):
        spread(table.at[i], jnp.exp(-rate * power))
    spread(table.at[4], coeffs)
    spread(taps, taps_in[...])
    for r in range(tile.shape[1]):
        tile[:, r, :] = coeffs * jnp.exp(-rate * (r - 1.0))
    tile_step[...] = jnp.exp(-rate * tile.shape[1])


def over_rows(step, start, stop, carry):
    aligned = -(-start // UNROLL) * UNROLL
    for t in range(start, aligned):
        carry = step(t, carry)

    def group(i, carry):
        for j in range(UNROLL):
            carry = step(i * UNROLL + j, carry)
        return carry

    return lax.fori_loop(aligned // UNROLL, stop // UNROLL, group, carry)


def filtered(taps, s, value, cols):
    one, two = pltpu.roll(value, 1, 0), pltpu.roll(value, 2, 0)
    lags = [taps[j, s : s + 1, cols] for j in range(3)]
    return lags[0] * value + lags[1] * one + lags[2] * two


def last_kernel(x_ref, held, taps, table, _, total, source, out_ref, low, high):
    depth = x_ref.shape[1]
    for s in range(total.shape[0]):
        add_products([x_ref[...]], lambda b, at: held[0, s, depth:, at], total, s, cols=WIDE)
    rows, groups, lanes = source.shape
    modes = table.shape[1]
    for g in range(groups):
        cols = slice(g * lanes, (g + 1) * lanes)
        one, two = rounded(total[1, :, cols]), rounded(total[2, :, cols])
        source[:, g, :] = filtered(taps, 1, one, cols) * filtered(taps, 2, two, cols)
        for s, value in ((1, one), (2, two)):
            low[s - 1, :, g, :] = value[:8]
            high[s, :, g, :] = value[rows - 8 :]
        high[0, :, g, :] = rounded(total[0, rows - 8 :, cols])
    rate = [table[0, n] for n in range(modes)]

    def step_row(t, state):
        u = source[t]
        return [r * s + u for r, s in zip(rate, state)]

    state = [jnp.zeros((groups, lanes), jnp.float32)] * modes
    state = over_rows(step_row, 2, rows, state)
    for n in range(modes):
        out_ref[n] = state[n]
    for j in range(2):
        for s in (1, 2):
            out_ref[modes + (s - 1) * 2 + j] = low[s - 1, j]
        for s in range(3):
            out_ref[modes + 4 + s * 2 + j] = high[s, 6 + j]


def rounded(value):
    return value.astype(jnp.bfloat16).astype(jnp.float32)


def tree_sum(terms):
    while len(terms) > 1:
        terms = [a + b for a, b in zip(terms[::2], terms[1::2])] + terms[len(terms) & ~1 :]
    return terms[0]


def local_kernel(total, source, taps, table, query, response, heads, work, low):
    rows, groups, lanes = source.shape
    modes = table.shape[1]
    for g in range(groups):
        cols = slice(g * lanes, (g + 1) * lanes)
        value = rounded(total[0, :, cols])
        query[:, cols] = filtered(taps, 0, value, cols)
        low[:, g, :] = value[:8]
    for j in range(2):
        heads[j] = low[j]
        work[j] = jnp.zeros((groups, lanes), jnp.float32)

    def step_row(t, state):
        u = source[t]
        state = [table[0, n] * state[n] + u for n in range(modes)]
        work[t] = tree_sum([table[4, n] * state[n] for n in range(modes)])
        return state

    over_rows(step_row, 2, rows, [jnp.zeros((groups, lanes), jnp.float32)] * modes)
    for g in range(groups):
        response[:, g * lanes : (g + 1) * lanes] = work[:, g, :]


def edge(taps, s, first, second, before, last):
    return (
        taps[0, s] * first + taps[1, s] * last + taps[2, s] * before,
        taps[0, s] * second + taps[1, s] * first + taps[2, s] * last,
    )


def lead_sources(taps, heads, rims):
    one = edge(taps, 1, heads[0], heads[1], rims[2], rims[3])
    two = edge(taps, 2, heads[2], heads[3], rims[4], rims[5])
    return one[0] * two[0], one[1] * two[1]


class Summary:
    def __init__(self, rows, modes):
        self.state = rows[:modes]
        self.heads = rows[modes : modes + 4]
        self.rims = rows[modes + 4 :]

    @classmethod
    def read(cls, ref, modes):
        return cls([ref[i] for i in range(ref.shape[0])], modes)

    @classmethod
    def chosen(cls, odd, when_odd, when_even, modes):
        pairs = zip(when_odd.rows(), when_even.rows())
        return cls([jnp.where(odd, a, b) for a, b in pairs], modes)

    def rows(self):
        return self.state + self.heads + self.rims

    def complete(self, taps, rims, by_first, by_second):
        u0, u1 = lead_sources(taps, self.heads, rims)
        return [x + f * u0 + g * u1 for x, f, g in zip(self.state, by_first, by_second)]


def powers(table):
    return [[table[i, n] for n in range(table.shape[1])] for i in range(table.shape[0])]


def chip_kernel(lone, local, partner, taps, table, out_ref):
    modes = table.shape[1]
    odd = lax.rem(lax.axis_index("ctx"), 2) == 1
    mine, other = Summary.read(local, modes), Summary.read(partner, modes)
    first = Summary.chosen(odd, other, mine, modes)
    second = Summary.chosen(odd, mine, other, modes)
    _, block, less_one, less_two, _ = powers(table)
    start, heads = first.state, first.heads
    if lone:
        start, heads = first.complete(taps, [jnp.zeros_like(heads[0])] * 6, less_one, less_two), []
    end = second.complete(taps, first.rims, less_one, less_two)
    joined = [d * x + y for d, x, y in zip(block, start, end)]
    for i, value in enumerate(joined + heads + second.rims):
        out_ref[i] = value


def final_kernel(lone, count, *refs):
    sent = refs[:count]
    local, partner, query, response, query_heads, taps, table, tile, tile_step, *refs = refs[count:]
    out_ref, states, firsts, rounded_out, out_sem = refs
    rows = query.shape[0]
    groups, lanes = local.shape[1:]
    modes = table.shape[1]
    zero = jnp.zeros((groups, lanes), jnp.float32)
    index = lax.axis_index("ctx")
    odd = lax.rem(index, 2) == 1
    _, block, less_one, less_two, _ = powers(table)
    values = [
        [jnp.where(index >= 2 * (d + 1), ref[i], zero) for i in range(ref.shape[0])]
        for d, ref in enumerate(sent)
    ]
    rims = [value[-6:] for value in values] + [[zero] * 6]
    state = [zero] * modes
    for d in reversed(range(count)):
        end = values[d][:modes]
        if not lone:
            end = Summary(values[d], modes).complete(
                taps,
                rims[d + 1],
                [a * b for a, b in zip(block, less_one)],
                [a * b for a, b in zip(block, less_two)],
            )
        state = [d * d * x + y for d, x, y in zip(block, state, end)]
    before = Summary.read(partner, modes)
    end = before.complete(taps, rims[0], less_one, less_two)
    state = [jnp.where(odd, d * x + y, x) for d, x, y in zip(block, state, end)]
    rim = [jnp.where(odd, a, b) for a, b in zip(before.rims, rims[0])]

    leads = lead_sources(taps, Summary.read(local, modes).heads, rim)
    heads = edge(taps, 0, query_heads[0], query_heads[1], rim[0], rim[1])
    for t, u in enumerate(leads):
        state = [table[0, n] * state[n] + u for n in range(modes)]
        firsts[t] = heads[t] * tree_sum([table[4, n] * state[n] for n in range(modes)])
    for n in range(modes):
        states[n] = state[n]

    tall = tile.shape[1]
    row = lax.broadcasted_iota(jnp.int32, (tall, lanes), 0)
    copies = []
    for g in range(groups):
        cols = slice(g * lanes, (g + 1) * lanes)
        carried = [tile[n, :, cols] * states[n, g : g + 1, :] for n in range(modes)]
        step = [jnp.broadcast_to(tile_step[n : n + 1, cols], (tall, lanes)) for n in range(modes)]
        for i in range(0, rows, 2 * tall):
            pair = []
            for at in (slice(i, i + tall), slice(i + tall, i + 2 * tall)):
                value = query[at, cols] * (response[at, cols] + tree_sum(carried))
                if at.start == 0:
                    value = jnp.where(row == 0, firsts[0, g : g + 1, :], value)
                    value = jnp.where(row == 1, firsts[1, g : g + 1, :], value)
                pair.append(value)
                carried = [a * b for a, b in zip(carried, step)]
            rounded_out[i : i + 2 * tall, cols] = jnp.concatenate(pair, axis=0).astype(out_ref.dtype)
        if g % 2:
            wide = slice((g - 1) * lanes, (g + 1) * lanes)
            k = g // 2
            copies.append(
                pltpu.make_async_copy(rounded_out.at[:, wide], out_ref.at[:, wide], out_sem.at[k])
            )
            copies[-1].start()
    for copy in copies:
        copy.wait()


def on_device(tokens, in_weight, filter_taps, decay_rate, residue):
    rows, width = tokens.shape
    streams, chans = in_weight.shape[1:]
    lags = filter_taps.shape[0]
    modes = decay_rate.shape[0]
    groups = chans // LANES
    tp, ctx = lax.axis_size("tp"), lax.axis_size("ctx")
    order = ring_order(tp)
    weight = jnp.transpose(in_weight, (1, 0, 2))
    half = tp // 2
    ahead = [(order[i], order[(i + 1) % tp]) for i in range(tp)]
    back = [(b, a) for a, b in ahead]

    def f32(*shape):
        return jax.ShapeDtypeStruct(shape, jnp.float32)

    def held(count):
        return jax.ShapeDtypeStruct((count, streams, width, chans), jnp.bfloat16)

    def loads(step):
        return [step, -step] if step < half else [step]

    sums = f32(streams, rows, chans)
    wide = f32(rows, groups, LANES)
    params = pltpu.CompilerParams(vmem_limit_bytes=12 << 20)
    cost = pl.CostEstimate(flops=0, bytes_accessed=16 << 20, transcendentals=0)

    def blocks(step):
        return [0] + loads(1) if step == 1 else loads(step)

    def left(step):
        if step >= half:
            return []
        last, halfway = len(blocks(step)) - 1, (width // 2, width)
        if step == 1:
            return [(last, streams - 1, *halfway)]
        return [(last, streams - 1, 0, width)] + [(0, streams - 1, *halfway)] * (step == half - 1)

    def pieces(step):
        lacking = {(b, s): low for b, s, low, _ in left(step)}
        every = [(b, s) for s in range(streams) for b in range(len(blocks(step)))]
        found = [(b, s, 0, lacking.get((b, s), width)) for b, s in every]
        return [piece for piece in found if piece[3]]

    weights = pl.pallas_call(
        functools.partial(load_kernel, order, blocks(1), pieces(1)),
        out_shape=held(len(blocks(1))),
        in_specs=[HBM],
        out_specs=VMEM,
        scratch_shapes=[pltpu.SemaphoreType.DMA((len(pieces(1)),))],
        compiler_params=params,
        cost_estimate=cost,
        name="load_first",
    )(weight)
    fore, aft, total = tokens, tokens, None
    for step in range(1, half):
        fore = lax.ppermute(fore, "tp", ahead)
        aft = lax.ppermute(aft, "tp", back)
        fore, total, weights = lax.optimization_barrier((fore, total, weights))
        aft, total, weights = lax.optimization_barrier((aft, total, weights))
        first = step == 1
        xs = [tokens, fore, aft] if first else [fore, aft]
        extra = [filter_taps, decay_rate, residue] if first else [total]
        made = []
        if first:
            made = [f32(lags, streams, groups, LANES), f32(5, modes, groups, LANES)]
            made += [f32(modes, 8, chans), f32(modes, chans)]
        total, weights, *made = pl.pallas_call(
            functools.partial(
                middle_kernel, order, blocks(step), left(step), blocks(step + 1), pieces(step + 1),
                len(extra),
            ),
            out_shape=[sums, held(len(blocks(step + 1)))] + made,
            in_specs=[VMEM] * (len(xs) + 1) + [HBM] + [VMEM] * len(extra),
            out_specs=[VMEM] * (2 + len(made)),
            scratch_shapes=[
                pltpu.VMEM((2, width, chans), jnp.bfloat16),
                pltpu.SemaphoreType.DMA((2,)),
                pltpu.SemaphoreType.DMA((len(pieces(step + 1)),)),
            ],
            input_output_aliases={} if first else {len(xs) + 2: 0},
            compiler_params=params,
            cost_estimate=cost,
            name="project_blocks",
        )(*xs, weights, weight, *extra)
        if first:
            taps, table, *tiles = made
    fore = lax.ppermute(fore[:, : width // 2], "tp", ahead)
    aft = lax.ppermute(aft[:, width // 2 :], "tp", back)
    total = pl.pallas_call(
        half_kernel,
        out_shape=sums,
        in_specs=[VMEM] * 3,
        out_specs=VMEM,
        input_output_aliases={2: 0},
        compiler_params=params,
        cost_estimate=cost,
        name="project_half",
    )(fore, weights, total)
    total, source, local = pl.pallas_call(
        last_kernel,
        out_shape=[sums, wide, f32(modes + EDGE, groups, LANES)],
        in_specs=[VMEM] * 5,
        out_specs=[VMEM] * 3,
        scratch_shapes=[
            pltpu.VMEM((streams - 1, 8, groups, LANES), jnp.float32),
            pltpu.VMEM((streams, 8, groups, LANES), jnp.float32),
        ],
        input_output_aliases={4: 0},
        compiler_params=params,
        cost_estimate=cost,
        name="project_last",
    )(aft, weights, filter_taps, table, total)

    partner = lax.ppermute(local, "ctx", [(j, j ^ 1) for j in range(ctx)])
    lone = ctx == 4
    chip = pl.pallas_call(
        functools.partial(chip_kernel, lone),
        out_shape=f32(modes + (6 if lone else EDGE), groups, LANES),
        in_specs=[VMEM] * 4,
        out_specs=VMEM,
        compiler_params=params,
        name="chip_state",
    )(local, partner, taps, table)
    sent = [
        lax.ppermute(chip, "ctx", [(j, (j + d) % ctx) for j in range(ctx)])
        for d in range(2, ctx, 2)
    ]
    query, response, heads = pl.pallas_call(
        local_kernel,
        out_shape=[f32(rows, chans), f32(rows, chans), f32(2, groups, LANES)],
        in_specs=[VMEM] * 4,
        out_specs=[VMEM] * 3,
        scratch_shapes=[
            pltpu.VMEM((rows, groups, LANES), jnp.float32),
            pltpu.VMEM((8, groups, LANES), jnp.float32),
        ],
        compiler_params=params,
        cost_estimate=cost,
        name="local_response",
    )(total, source, filter_taps, table)
    return pl.pallas_call(
        functools.partial(final_kernel, lone, len(sent)),
        out_shape=jax.ShapeDtypeStruct((rows, chans), jnp.bfloat16),
        in_specs=[VMEM] * (len(sent) + 9),
        out_specs=HBM,
        scratch_shapes=[
            pltpu.VMEM((modes, groups, LANES), jnp.float32),
            pltpu.VMEM((2, groups, LANES), jnp.float32),
            pltpu.VMEM((rows, chans), jnp.bfloat16),
            pltpu.SemaphoreType.DMA((groups // 2,)),
        ],
        compiler_params=params,
        name="carried_response",
    )(*sent, local, partner, query, response, heads, taps, table, *tiles)


def solution(mesh):
    return jax.shard_map(
        on_device,
        mesh=mesh,
        in_specs=(
            P("ctx", "tp"),
            P(None, None, "tp"),
            P(None, None, "tp"),
            P(None, "tp"),
            P(None, "tp"),
        ),
        out_specs=P("ctx", "tp"),
        check_vma=False,
    )
```

```python
import functools

import jax
import jax.numpy as jnp
from jax import lax
from jax.experimental import pallas as pl
from jax.experimental.pallas import tpu as pltpu
from jax.sharding import PartitionSpec as P

LANES = 128
COLS = 256
WIDE = 512
SOON = 4
GRID_ROWS = 4
EDGE = 10
UNROLL = 16
VMEM = pl.BlockSpec(memory_space=pltpu.VMEM)
HBM = pl.BlockSpec(memory_space=pltpu.HBM)


def ring_order(count):
    if count % (2 * GRID_ROWS):
        return list(range(count))
    cols = count // GRID_ROWS
    cells = [(0, c) for c in range(cols)]
    for r in range(1, GRID_ROWS):
        inner = list(range(1, cols))
        cells += [(r, c) for c in (reversed(inner) if r % 2 else inner)]
    cells += [(r, 0) for r in range(GRID_ROWS - 1, 0, -1)]
    return [r * cols + c for r, c in cells]


def owner_at(order, step):
    me = lax.axis_index("tp")
    owner = jnp.int32(0)
    for place, index in enumerate(order):
        owner = jnp.where(me == index, order[(place - step) % len(order)], owner)
    return owner


def piece_loads(order, steps, pieces, w_ref, target, sem):
    width = w_ref.shape[1] // len(order)
    starts = [pl.multiple_of(owner_at(order, step) * width, width) for step in steps]
    return [
        pltpu.make_async_copy(
            w_ref.at[s, pl.ds(starts[b] + low, high - low), :], target(i, b, s, low, high), sem.at[i]
        )
        for i, (b, s, low, high) in enumerate(pieces)
    ]


def add_products(xs, weights, total, s, fresh=False, cols=COLS):
    cols = min(cols, total.shape[2])
    for c in range(0, total.shape[2], cols):
        at = slice(c, c + cols)
        terms = [
            jnp.dot(x, weights(b, at), preferred_element_type=jnp.float32) for b, x in enumerate(xs)
        ]
        total[s, :, at] = sum(terms) if fresh else total[s, :, at] + sum(terms)


def spread(out_ref, value):
    groups, lanes = out_ref.shape[-2:]
    for g in range(groups):
        out_ref[..., g, :] = value[..., g * lanes : (g + 1) * lanes]


def held_part(held):
    return lambda i, b, s, low, high: held.at[b, s, pl.ds(low, high - low), :]


def load_kernel(order, steps, pieces, w_ref, held, sem):
    copies = piece_loads(order, steps, pieces, w_ref, held_part(held), sem)
    for copy in copies:
        copy.start()
    for copy in copies:
        copy.wait()


def middle_kernel(order, here, missing, steps, pieces, inputs_count, *refs):
    xs, (held, w_ref, *refs) = refs[: len(here)], refs[len(here) :]
    *refs, rest, rest_sem, sem = refs
    inputs, (total, next_held, *made) = refs[:inputs_count], refs[inputs_count:]
    fresh = bool(made)
    late = piece_loads(
        order, here, missing, w_ref,
        lambda i, b, s, low, high: rest.at[i, pl.ds(0, high - low), :], rest_sem,
    )
    ahead = piece_loads(order, steps, pieces, w_ref, held_part(next_held), sem)
    soon = max(SOON - len(late), 0)
    for copy in late + ahead[:soon]:
        copy.start()
    if made:
        make_tables(*inputs, *made, total.shape[1])
    whole = min(s for _, s, _, _ in missing) if missing else held.shape[1]

    @pl.loop(0, whole)
    def _(s):
        add_products([x[...] for x in xs], lambda b, at: held[b, s, :, at], total, s, fresh)

    for copy in ahead[soon:]:
        copy.start()
    for copy in late:
        copy.wait()
    for s in range(whole, held.shape[1]):
        gaps = {b: (i, low, high) for i, (b, k, low, high) in enumerate(missing) if k == s}
        parts = []
        for b, x in enumerate(xs):
            i, low, high = gaps.get(b, (0, x.shape[1], x.shape[1]))
            if low:
                parts.append((x[:, :low], lambda at, b=b, low=low: held[b, s, :low, at]))
            if low < high:
                parts.append((x[:, low:], lambda at, i=i, n=high - low: rest[i, :n, at]))
        values, weights = zip(*parts)
        add_products(values, lambda k, at: weights[k](at), total, s, fresh)
    for copy in ahead:
        copy.wait()


def half_kernel(x_ref, held, _, total):
    depth = x_ref.shape[1]
    for s in range(total.shape[0]):
        add_products([x_ref[...]], lambda b, at: held[0, s, :depth, at], total, s, cols=WIDE)


def make_tables(taps_in, decay, residue, taps, table, tile, tile_step, rows):
    rate = decay[...]
    coeffs = residue[...] * jnp.sqrt(1.0 - jnp.exp(-2.0 * rate))
    for i, power in enumerate((1, rows, rows - 1, rows - 2)):
        spread(table.at[i], jnp.exp(-rate * power))
    spread(table.at[4], coeffs)
    spread(taps, taps_in[...])
    for r in range(tile.shape[1]):
        tile[:, r, :] = coeffs * jnp.exp(-rate * (r - 1.0))
    tile_step[...] = jnp.exp(-rate * tile.shape[1])


def over_rows(step, start, stop, carry):
    aligned = -(-start // UNROLL) * UNROLL
    for t in range(start, aligned):
        carry = step(t, carry)

    def group(i, carry):
        for j in range(UNROLL):
            carry = step(i * UNROLL + j, carry)
        return carry

    return lax.fori_loop(aligned // UNROLL, stop // UNROLL, group, carry)


def filtered(taps, s, value, cols):
    one, two = pltpu.roll(value, 1, 0), pltpu.roll(value, 2, 0)
    lags = [taps[j, s : s + 1, cols] for j in range(3)]
    return lags[0] * value + lags[1] * one + lags[2] * two


def last_kernel(x_ref, held, taps, table, _, total, source, out_ref, low, high):
    depth = x_ref.shape[1]
    for s in range(total.shape[0]):
        add_products([x_ref[...]], lambda b, at: held[0, s, depth:, at], total, s, cols=WIDE)
    rows, groups, lanes = source.shape
    modes = table.shape[1]
    for g in range(groups):
        cols = slice(g * lanes, (g + 1) * lanes)
        one, two = rounded(total[1, :, cols]), rounded(total[2, :, cols])
        source[:, g, :] = filtered(taps, 1, one, cols) * filtered(taps, 2, two, cols)
        for s, value in ((1, one), (2, two)):
            low[s - 1, :, g, :] = value[:8]
            high[s, :, g, :] = value[rows - 8 :]
        high[0, :, g, :] = rounded(total[0, rows - 8 :, cols])
    rate = [table[0, n] for n in range(modes)]

    def step_row(t, state):
        u = source[t]
        return [r * s + u for r, s in zip(rate, state)]

    state = [jnp.zeros((groups, lanes), jnp.float32)] * modes
    state = over_rows(step_row, 2, rows, state)
    for n in range(modes):
        out_ref[n] = state[n]
    for j in range(2):
        for s in (1, 2):
            out_ref[modes + (s - 1) * 2 + j] = low[s - 1, j]
        for s in range(3):
            out_ref[modes + 4 + s * 2 + j] = high[s, 6 + j]


def rounded(value):
    return value.astype(jnp.bfloat16).astype(jnp.float32)


def tree_sum(terms):
    while len(terms) > 1:
        terms = [a + b for a, b in zip(terms[::2], terms[1::2])] + terms[len(terms) & ~1 :]
    return terms[0]


def local_kernel(total, source, taps, table, query, response, heads, work, low):
    rows, groups, lanes = source.shape
    modes = table.shape[1]
    for g in range(groups):
        cols = slice(g * lanes, (g + 1) * lanes)
        value = rounded(total[0, :, cols])
        query[:, cols] = filtered(taps, 0, value, cols)
        low[:, g, :] = value[:8]
    for j in range(2):
        heads[j] = low[j]
        work[j] = jnp.zeros((groups, lanes), jnp.float32)

    def step_row(t, state):
        u = source[t]
        state = [table[0, n] * state[n] + u for n in range(modes)]
        work[t] = tree_sum([table[4, n] * state[n] for n in range(modes)])
        return state

    over_rows(step_row, 2, rows, [jnp.zeros((groups, lanes), jnp.float32)] * modes)
    for g in range(groups):
        response[:, g * lanes : (g + 1) * lanes] = work[:, g, :]


def edge(taps, s, first, second, before, last):
    return (
        taps[0, s] * first + taps[1, s] * last + taps[2, s] * before,
        taps[0, s] * second + taps[1, s] * first + taps[2, s] * last,
    )


def lead_sources(taps, heads, rims):
    one = edge(taps, 1, heads[0], heads[1], rims[2], rims[3])
    two = edge(taps, 2, heads[2], heads[3], rims[4], rims[5])
    return one[0] * two[0], one[1] * two[1]


class Summary:
    def __init__(self, rows, modes):
        self.state = rows[:modes]
        self.heads = rows[modes : modes + 4]
        self.rims = rows[modes + 4 :]

    @classmethod
    def read(cls, ref, modes):
        return cls([ref[i] for i in range(ref.shape[0])], modes)

    @classmethod
    def chosen(cls, odd, when_odd, when_even, modes):
        pairs = zip(when_odd.rows(), when_even.rows())
        return cls([jnp.where(odd, a, b) for a, b in pairs], modes)

    def rows(self):
        return self.state + self.heads + self.rims

    def complete(self, taps, rims, by_first, by_second):
        u0, u1 = lead_sources(taps, self.heads, rims)
        return [x + f * u0 + g * u1 for x, f, g in zip(self.state, by_first, by_second)]


def powers(table):
    return [[table[i, n] for n in range(table.shape[1])] for i in range(table.shape[0])]


def chip_kernel(lone, local, partner, taps, table, out_ref):
    modes = table.shape[1]
    odd = lax.rem(lax.axis_index("ctx"), 2) == 1
    mine, other = Summary.read(local, modes), Summary.read(partner, modes)
    first = Summary.chosen(odd, other, mine, modes)
    second = Summary.chosen(odd, mine, other, modes)
    _, block, less_one, less_two, _ = powers(table)
    start, heads = first.state, first.heads
    if lone:
        start, heads = first.complete(taps, [jnp.zeros_like(heads[0])] * 6, less_one, less_two), []
    end = second.complete(taps, first.rims, less_one, less_two)
    joined = [d * x + y for d, x, y in zip(block, start, end)]
    for i, value in enumerate(joined + heads + second.rims):
        out_ref[i] = value


def final_kernel(lone, count, *refs):
    sent = refs[:count]
    local, partner, query, response, query_heads, taps, table, tile, tile_step, *refs = refs[count:]
    out_ref, states, firsts, rounded_out, out_sem = refs
    rows = query.shape[0]
    groups, lanes = local.shape[1:]
    modes = table.shape[1]
    zero = jnp.zeros((groups, lanes), jnp.float32)
    index = lax.axis_index("ctx")
    odd = lax.rem(index, 2) == 1
    _, block, less_one, less_two, _ = powers(table)
    values = [
        [jnp.where(index >= 2 * (d + 1), ref[i], zero) for i in range(ref.shape[0])]
        for d, ref in enumerate(sent)
    ]
    rims = [value[-6:] for value in values] + [[zero] * 6]
    state = [zero] * modes
    for d in reversed(range(count)):
        end = values[d][:modes]
        if not lone:
            end = Summary(values[d], modes).complete(
                taps,
                rims[d + 1],
                [a * b for a, b in zip(block, less_one)],
                [a * b for a, b in zip(block, less_two)],
            )
        state = [d * d * x + y for d, x, y in zip(block, state, end)]
    before = Summary.read(partner, modes)
    end = before.complete(taps, rims[0], less_one, less_two)
    state = [jnp.where(odd, d * x + y, x) for d, x, y in zip(block, state, end)]
    rim = [jnp.where(odd, a, b) for a, b in zip(before.rims, rims[0])]

    leads = lead_sources(taps, Summary.read(local, modes).heads, rim)
    heads = edge(taps, 0, query_heads[0], query_heads[1], rim[0], rim[1])
    for t, u in enumerate(leads):
        state = [table[0, n] * state[n] + u for n in range(modes)]
        firsts[t] = heads[t] * tree_sum([table[4, n] * state[n] for n in range(modes)])
    for n in range(modes):
        states[n] = state[n]

    tall = tile.shape[1]
    row = lax.broadcasted_iota(jnp.int32, (tall, lanes), 0)
    copies = []
    for g in range(groups):
        cols = slice(g * lanes, (g + 1) * lanes)
        carried = [tile[n, :, cols] * states[n, g : g + 1, :] for n in range(modes)]
        step = [jnp.broadcast_to(tile_step[n : n + 1, cols], (tall, lanes)) for n in range(modes)]
        for i in range(0, rows, 2 * tall):
            pair = []
            for at in (slice(i, i + tall), slice(i + tall, i + 2 * tall)):
                value = query[at, cols] * (response[at, cols] + tree_sum(carried))
                if at.start == 0:
                    value = jnp.where(row == 0, firsts[0, g : g + 1, :], value)
                    value = jnp.where(row == 1, firsts[1, g : g + 1, :], value)
                pair.append(value)
                carried = [a * b for a, b in zip(carried, step)]
            rounded_out[i : i + 2 * tall, cols] = jnp.concatenate(pair, axis=0).astype(out_ref.dtype)
        if g % 2:
            wide = slice((g - 1) * lanes, (g + 1) * lanes)
            k = g // 2
            copies.append(
                pltpu.make_async_copy(rounded_out.at[:, wide], out_ref.at[:, wide], out_sem.at[k])
            )
            copies[-1].start()
    for copy in copies:
        copy.wait()


def on_device(tokens, in_weight, filter_taps, decay_rate, residue):
    rows, width = tokens.shape
    streams, chans = in_weight.shape[1:]
    lags = filter_taps.shape[0]
    modes = decay_rate.shape[0]
    groups = chans // LANES
    tp, ctx = lax.axis_size("tp"), lax.axis_size("ctx")
    order = ring_order(tp)
    weight = jnp.transpose(in_weight, (1, 0, 2))
    half = tp // 2
    ahead = [(order[i], order[(i + 1) % tp]) for i in range(tp)]
    back = [(b, a) for a, b in ahead]

    def f32(*shape):
        return jax.ShapeDtypeStruct(shape, jnp.float32)

    def held(count):
        return jax.ShapeDtypeStruct((count, streams, width, chans), jnp.bfloat16)

    def loads(step):
        return [step, -step] if step < half else [step]

    sums = f32(streams, rows, chans)
    wide = f32(rows, groups, LANES)
    params = pltpu.CompilerParams(vmem_limit_bytes=12 << 20)
    cost = pl.CostEstimate(flops=0, bytes_accessed=16 << 20, transcendentals=0)

    def blocks(step):
        return [0] + loads(1) if step == 1 else loads(step)

    def left(step):
        if step >= half:
            return []
        last, halfway = len(blocks(step)) - 1, (width // 2, width)
        return [(last, streams - 1, *halfway) if step < half - 1 else (last, streams - 1, 0, width)]

    def pieces(step):
        lacking = {(b, s): low for b, s, low, _ in left(step)}
        every = [(b, s) for s in range(streams) for b in range(len(blocks(step)))]
        found = [(b, s, 0, lacking.get((b, s), width)) for b, s in every]
        return [piece for piece in found if piece[3]]

    weights = pl.pallas_call(
        functools.partial(load_kernel, order, blocks(1), pieces(1)),
        out_shape=held(len(blocks(1))),
        in_specs=[HBM],
        out_specs=VMEM,
        scratch_shapes=[pltpu.SemaphoreType.DMA((len(pieces(1)),))],
        compiler_params=params,
        cost_estimate=cost,
        name="load_first",
    )(weight)
    fore, aft, total = tokens, tokens, None
    for step in range(1, half):
        fore = lax.ppermute(fore, "tp", ahead)
        aft = lax.ppermute(aft, "tp", back)
        fore, total, weights = lax.optimization_barrier((fore, total, weights))
        aft, total, weights = lax.optimization_barrier((aft, total, weights))
        first = step == 1
        xs = [tokens, fore, aft] if first else [fore, aft]
        extra = [filter_taps, decay_rate, residue] if first else [total]
        made = []
        if first:
            made = [f32(lags, streams, groups, LANES), f32(5, modes, groups, LANES)]
            made += [f32(modes, 8, chans), f32(modes, chans)]
        total, weights, *made = pl.pallas_call(
            functools.partial(
                middle_kernel, order, blocks(step), left(step), blocks(step + 1), pieces(step + 1),
                len(extra),
            ),
            out_shape=[sums, held(len(blocks(step + 1)))] + made,
            in_specs=[VMEM] * (len(xs) + 1) + [HBM] + [VMEM] * len(extra),
            out_specs=[VMEM] * (2 + len(made)),
            scratch_shapes=[
                pltpu.VMEM((2, width, chans), jnp.bfloat16),
                pltpu.SemaphoreType.DMA((2,)),
                pltpu.SemaphoreType.DMA((len(pieces(step + 1)),)),
            ],
            input_output_aliases={} if first else {len(xs) + 2: 0},
            compiler_params=params,
            cost_estimate=cost,
            name="project_blocks",
        )(*xs, weights, weight, *extra)
        if first:
            taps, table, *tiles = made
    fore = lax.ppermute(fore[:, : width // 2], "tp", ahead)
    aft = lax.ppermute(aft[:, width // 2 :], "tp", back)
    total = pl.pallas_call(
        half_kernel,
        out_shape=sums,
        in_specs=[VMEM] * 3,
        out_specs=VMEM,
        input_output_aliases={2: 0},
        compiler_params=params,
        cost_estimate=cost,
        name="project_half",
    )(fore, weights, total)
    total, source, local = pl.pallas_call(
        last_kernel,
        out_shape=[sums, wide, f32(modes + EDGE, groups, LANES)],
        in_specs=[VMEM] * 5,
        out_specs=[VMEM] * 3,
        scratch_shapes=[
            pltpu.VMEM((streams - 1, 8, groups, LANES), jnp.float32),
            pltpu.VMEM((streams, 8, groups, LANES), jnp.float32),
        ],
        input_output_aliases={4: 0},
        compiler_params=params,
        cost_estimate=cost,
        name="project_last",
    )(aft, weights, filter_taps, table, total)

    partner = lax.ppermute(local, "ctx", [(j, j ^ 1) for j in range(ctx)])
    lone = ctx == 4
    chip = pl.pallas_call(
        functools.partial(chip_kernel, lone),
        out_shape=f32(modes + (6 if lone else EDGE), groups, LANES),
        in_specs=[VMEM] * 4,
        out_specs=VMEM,
        compiler_params=params,
        name="chip_state",
    )(local, partner, taps, table)
    sent = [
        lax.ppermute(chip, "ctx", [(j, (j + d) % ctx) for j in range(ctx)])
        for d in range(2, ctx, 2)
    ]
    query, response, heads = pl.pallas_call(
        local_kernel,
        out_shape=[f32(rows, chans), f32(rows, chans), f32(2, groups, LANES)],
        in_specs=[VMEM] * 4,
        out_specs=[VMEM] * 3,
        scratch_shapes=[
            pltpu.VMEM((rows, groups, LANES), jnp.float32),
            pltpu.VMEM((8, groups, LANES), jnp.float32),
        ],
        compiler_params=params,
        cost_estimate=cost,
        name="local_response",
    )(total, source, filter_taps, table)
    return pl.pallas_call(
        functools.partial(final_kernel, lone, len(sent)),
        out_shape=jax.ShapeDtypeStruct((rows, chans), jnp.bfloat16),
        in_specs=[VMEM] * (len(sent) + 9),
        out_specs=HBM,
        scratch_shapes=[
            pltpu.VMEM((modes, groups, LANES), jnp.float32),
            pltpu.VMEM((2, groups, LANES), jnp.float32),
            pltpu.VMEM((rows, chans), jnp.bfloat16),
            pltpu.SemaphoreType.DMA((groups // 2,)),
        ],
        compiler_params=params,
        name="carried_response",
    )(*sent, local, partner, query, response, heads, taps, table, *tiles)


def solution(mesh):
    return jax.shard_map(
        on_device,
        mesh=mesh,
        in_specs=(
            P("ctx", "tp"),
            P(None, None, "tp"),
            P(None, None, "tp"),
            P(None, "tp"),
            P(None, "tp"),
        ),
        out_specs=P("ctx", "tp"),
        check_vma=False,
    )
```

```python
import functools

import jax
import jax.numpy as jnp
from jax import lax
from jax.experimental import pallas as pl
from jax.experimental.pallas import tpu as pltpu
from jax.sharding import PartitionSpec as P

LANES = 128
COLS = 256
WIDE = 512
SOON = 4
GRID_ROWS = 4
EDGE = 10
UNROLL = 16
VMEM = pl.BlockSpec(memory_space=pltpu.VMEM)
HBM = pl.BlockSpec(memory_space=pltpu.HBM)


def ring_order(count):
    if count % (2 * GRID_ROWS):
        return list(range(count))
    cols = count // GRID_ROWS
    cells = [(0, c) for c in range(cols)]
    for r in range(1, GRID_ROWS):
        inner = list(range(1, cols))
        cells += [(r, c) for c in (reversed(inner) if r % 2 else inner)]
    cells += [(r, 0) for r in range(GRID_ROWS - 1, 0, -1)]
    return [r * cols + c for r, c in cells]


def owner_at(order, step):
    me = lax.axis_index("tp")
    owner = jnp.int32(0)
    for place, index in enumerate(order):
        owner = jnp.where(me == index, order[(place - step) % len(order)], owner)
    return owner


def piece_loads(order, steps, pieces, w_ref, target, sem):
    width = w_ref.shape[1] // len(order)
    starts = [pl.multiple_of(owner_at(order, step) * width, width) for step in steps]
    return [
        pltpu.make_async_copy(
            w_ref.at[s, pl.ds(starts[b] + low, high - low), :], target(i, b, s, low, high), sem.at[i]
        )
        for i, (b, s, low, high) in enumerate(pieces)
    ]


def add_products(xs, weights, total, s, fresh=False, cols=COLS):
    cols = min(cols, total.shape[2])
    for c in range(0, total.shape[2], cols):
        at = slice(c, c + cols)
        terms = [
            jnp.dot(x, weights(b, at), preferred_element_type=jnp.float32) for b, x in enumerate(xs)
        ]
        total[s, :, at] = sum(terms) if fresh else total[s, :, at] + sum(terms)


def spread(out_ref, value):
    groups, lanes = out_ref.shape[-2:]
    for g in range(groups):
        out_ref[..., g, :] = value[..., g * lanes : (g + 1) * lanes]


def held_part(held):
    return lambda i, b, s, low, high: held.at[b, s, pl.ds(low, high - low), :]


def load_kernel(order, steps, pieces, w_ref, held, sem):
    copies = piece_loads(order, steps, pieces, w_ref, held_part(held), sem)
    for copy in copies:
        copy.start()
    for copy in copies:
        copy.wait()


def middle_kernel(order, here, missing, steps, pieces, inputs_count, *refs):
    xs, (held, w_ref, *refs) = refs[: len(here)], refs[len(here) :]
    *refs, rest, rest_sem, sem = refs
    inputs, (total, next_held, *made) = refs[:inputs_count], refs[inputs_count:]
    fresh = bool(made)
    late = piece_loads(
        order, here, missing, w_ref,
        lambda i, b, s, low, high: rest.at[i, pl.ds(0, high - low), :], rest_sem,
    )
    ahead = piece_loads(order, steps, pieces, w_ref, held_part(next_held), sem)
    soon = max(SOON - len(late), 0)
    for copy in late + ahead[:soon]:
        copy.start()
    if made:
        make_tables(*inputs, *made, total.shape[1])
    whole = min(s for _, s, _, _ in missing) if missing else held.shape[1]

    @pl.loop(0, whole)
    def _(s):
        add_products([x[...] for x in xs], lambda b, at: held[b, s, :, at], total, s, fresh)

    for copy in ahead[soon:]:
        copy.start()
    for copy in late:
        copy.wait()
    for s in range(whole, held.shape[1]):
        gaps = {b: (i, low, high) for i, (b, k, low, high) in enumerate(missing) if k == s}
        parts = []
        for b, x in enumerate(xs):
            i, low, high = gaps.get(b, (0, x.shape[1], x.shape[1]))
            if low:
                parts.append((x[:, :low], lambda at, b=b, low=low: held[b, s, :low, at]))
            if low < high:
                parts.append((x[:, low:], lambda at, i=i, n=high - low: rest[i, :n, at]))
        values, weights = zip(*parts)
        add_products(values, lambda k, at: weights[k](at), total, s, fresh)
    for copy in ahead:
        copy.wait()


def half_kernel(x_ref, held, _, total):
    depth = x_ref.shape[1]
    for s in range(total.shape[0]):
        add_products([x_ref[...]], lambda b, at: held[0, s, :depth, at], total, s, cols=WIDE)


def make_tables(taps_in, decay, residue, taps, table, tile, tile_step, fade, rows):
    rate = decay[...]
    coeffs = residue[...] * jnp.sqrt(1.0 - jnp.exp(-2.0 * rate))
    for i, power in enumerate((1, rows, rows - 1, rows - 2)):
        spread(table.at[i], jnp.exp(-rate * power))
    spread(table.at[4], coeffs)
    spread(taps, taps_in[...])
    for r in range(tile.shape[1]):
        tile[:, r, :] = coeffs * jnp.exp(-rate * (r - 1.0))
        fade[:, r, :] = jnp.exp(-rate * (fade.shape[1] - 1.0 - r))
    tile_step[...] = jnp.exp(-rate * tile.shape[1])


def over_rows(step, start, stop, carry):
    aligned = -(-start // UNROLL) * UNROLL
    for t in range(start, aligned):
        carry = step(t, carry)

    def group(i, carry):
        for j in range(UNROLL):
            carry = step(i * UNROLL + j, carry)
        return carry

    return lax.fori_loop(aligned // UNROLL, stop // UNROLL, group, carry)


def filtered(taps, s, value, cols):
    one, two = pltpu.roll(value, 1, 0), pltpu.roll(value, 2, 0)
    lags = [taps[j, s : s + 1, cols] for j in range(3)]
    return lags[0] * value + lags[1] * one + lags[2] * two


def last_kernel(x_ref, held, taps, tile_step, fade, _, total, source, out_ref):
    depth = x_ref.shape[1]
    for s in range(total.shape[0]):
        add_products([x_ref[...]], lambda b, at: held[0, s, depth:, at], total, s, cols=WIDE)
    rows = source.shape[0]
    modes, tall, _ = fade.shape
    groups, lanes = out_ref.shape[1:]
    row = lax.broadcasted_iota(jnp.int32, (tall, lanes), 0)
    for g in range(groups):
        cols = slice(g * lanes, (g + 1) * lanes)
        one, two = rounded(total[1, :, cols]), rounded(total[2, :, cols])
        value = filtered(taps, 1, one, cols) * filtered(taps, 2, two, cols)
        source[:, cols] = value
        step = [jnp.broadcast_to(tile_step[n : n + 1, cols], (tall, lanes)) for n in range(modes)]
        first = jnp.where(row < 2, 0.0, value[:tall])
        state = [first] * modes
        for i in range(tall, rows, tall):
            state = [a * b + value[i : i + tall] for a, b in zip(state, step)]
        for n in range(modes):
            out_ref[n, g : g + 1, :] = jnp.sum(state[n] * fade[n, :, cols], axis=0, keepdims=True)
        query = rounded(total[0, rows - tall :, cols])
        for s, ends in ((1, one), (2, two)):
            out_ref[modes + s * 2 - 2 : modes + s * 2, g, :] = ends[:2]
        for s, ends in ((0, query), (1, one), (2, two)):
            low = modes + 4 + s * 2
            out_ref[low : low + 2, g, :] = ends[-2:]


def rounded(value):
    return value.astype(jnp.bfloat16).astype(jnp.float32)


def tree_sum(terms):
    while len(terms) > 1:
        terms = [a + b for a, b in zip(terms[::2], terms[1::2])] + terms[len(terms) & ~1 :]
    return terms[0]


def local_kernel(total, natural, taps, table, query, response, heads, work, low, source):
    rows, groups, lanes = source.shape
    modes = table.shape[1]
    for g in range(groups):
        cols = slice(g * lanes, (g + 1) * lanes)
        value = rounded(total[0, :, cols])
        query[:, cols] = filtered(taps, 0, value, cols)
        low[:, g, :] = value[:8]
        source[:, g, :] = natural[:, cols]
    for j in range(2):
        heads[j] = low[j]
        work[j] = jnp.zeros((groups, lanes), jnp.float32)

    def step_row(t, state):
        u = source[t]
        state = [table[0, n] * state[n] + u for n in range(modes)]
        work[t] = tree_sum([table[4, n] * state[n] for n in range(modes)])
        return state

    over_rows(step_row, 2, rows, [jnp.zeros((groups, lanes), jnp.float32)] * modes)
    for g in range(groups):
        response[:, g * lanes : (g + 1) * lanes] = work[:, g, :]


def edge(taps, s, first, second, before, last):
    return (
        taps[0, s] * first + taps[1, s] * last + taps[2, s] * before,
        taps[0, s] * second + taps[1, s] * first + taps[2, s] * last,
    )


def lead_sources(taps, heads, rims):
    one = edge(taps, 1, heads[0], heads[1], rims[2], rims[3])
    two = edge(taps, 2, heads[2], heads[3], rims[4], rims[5])
    return one[0] * two[0], one[1] * two[1]


class Summary:
    def __init__(self, rows, modes):
        self.state = rows[:modes]
        self.heads = rows[modes : modes + 4]
        self.rims = rows[modes + 4 :]

    @classmethod
    def read(cls, ref, modes):
        return cls([ref[i] for i in range(ref.shape[0])], modes)

    @classmethod
    def chosen(cls, odd, when_odd, when_even, modes):
        pairs = zip(when_odd.rows(), when_even.rows())
        return cls([jnp.where(odd, a, b) for a, b in pairs], modes)

    def rows(self):
        return self.state + self.heads + self.rims

    def complete(self, taps, rims, by_first, by_second):
        u0, u1 = lead_sources(taps, self.heads, rims)
        return [x + f * u0 + g * u1 for x, f, g in zip(self.state, by_first, by_second)]


def powers(table):
    return [[table[i, n] for n in range(table.shape[1])] for i in range(table.shape[0])]


def chip_kernel(lone, local, partner, taps, table, out_ref):
    modes = table.shape[1]
    odd = lax.rem(lax.axis_index("ctx"), 2) == 1
    mine, other = Summary.read(local, modes), Summary.read(partner, modes)
    first = Summary.chosen(odd, other, mine, modes)
    second = Summary.chosen(odd, mine, other, modes)
    _, block, less_one, less_two, _ = powers(table)
    start, heads = first.state, first.heads
    if lone:
        start, heads = first.complete(taps, [jnp.zeros_like(heads[0])] * 6, less_one, less_two), []
    end = second.complete(taps, first.rims, less_one, less_two)
    joined = [d * x + y for d, x, y in zip(block, start, end)]
    for i, value in enumerate(joined + heads + second.rims):
        out_ref[i] = value


def final_kernel(lone, count, *refs):
    sent = refs[:count]
    local, partner, query, response, query_heads, taps, table, tile, tile_step, *refs = refs[count:]
    out_ref, states, firsts, rounded_out, out_sem = refs
    rows = query.shape[0]
    groups, lanes = local.shape[1:]
    modes = table.shape[1]
    zero = jnp.zeros((groups, lanes), jnp.float32)
    index = lax.axis_index("ctx")
    odd = lax.rem(index, 2) == 1
    _, block, less_one, less_two, _ = powers(table)
    values = [
        [jnp.where(index >= 2 * (d + 1), ref[i], zero) for i in range(ref.shape[0])]
        for d, ref in enumerate(sent)
    ]
    rims = [value[-6:] for value in values] + [[zero] * 6]
    state = [zero] * modes
    for d in reversed(range(count)):
        end = values[d][:modes]
        if not lone:
            end = Summary(values[d], modes).complete(
                taps,
                rims[d + 1],
                [a * b for a, b in zip(block, less_one)],
                [a * b for a, b in zip(block, less_two)],
            )
        state = [d * d * x + y for d, x, y in zip(block, state, end)]
    before = Summary.read(partner, modes)
    end = before.complete(taps, rims[0], less_one, less_two)
    state = [jnp.where(odd, d * x + y, x) for d, x, y in zip(block, state, end)]
    rim = [jnp.where(odd, a, b) for a, b in zip(before.rims, rims[0])]

    leads = lead_sources(taps, Summary.read(local, modes).heads, rim)
    heads = edge(taps, 0, query_heads[0], query_heads[1], rim[0], rim[1])
    for t, u in enumerate(leads):
        state = [table[0, n] * state[n] + u for n in range(modes)]
        firsts[t] = heads[t] * tree_sum([table[4, n] * state[n] for n in range(modes)])
    for n in range(modes):
        states[n] = state[n]

    tall = tile.shape[1]
    row = lax.broadcasted_iota(jnp.int32, (tall, lanes), 0)
    copies = []
    for g in range(groups):
        cols = slice(g * lanes, (g + 1) * lanes)
        carried = [tile[n, :, cols] * states[n, g : g + 1, :] for n in range(modes)]
        step = [jnp.broadcast_to(tile_step[n : n + 1, cols], (tall, lanes)) for n in range(modes)]
        for i in range(0, rows, 2 * tall):
            pair = []
            for at in (slice(i, i + tall), slice(i + tall, i + 2 * tall)):
                value = query[at, cols] * (response[at, cols] + tree_sum(carried))
                if at.start == 0:
                    value = jnp.where(row == 0, firsts[0, g : g + 1, :], value)
                    value = jnp.where(row == 1, firsts[1, g : g + 1, :], value)
                pair.append(value)
                carried = [a * b for a, b in zip(carried, step)]
            rounded_out[i : i + 2 * tall, cols] = jnp.concatenate(pair, axis=0).astype(out_ref.dtype)
        if g % 2:
            wide = slice((g - 1) * lanes, (g + 1) * lanes)
            k = g // 2
            copies.append(
                pltpu.make_async_copy(rounded_out.at[:, wide], out_ref.at[:, wide], out_sem.at[k])
            )
            copies[-1].start()
    for copy in copies:
        copy.wait()


def on_device(tokens, in_weight, filter_taps, decay_rate, residue):
    rows, width = tokens.shape
    streams, chans = in_weight.shape[1:]
    lags = filter_taps.shape[0]
    modes = decay_rate.shape[0]
    groups = chans // LANES
    tp, ctx = lax.axis_size("tp"), lax.axis_size("ctx")
    order = ring_order(tp)
    weight = jnp.transpose(in_weight, (1, 0, 2))
    half = tp // 2
    ahead = [(order[i], order[(i + 1) % tp]) for i in range(tp)]
    back = [(b, a) for a, b in ahead]

    def f32(*shape):
        return jax.ShapeDtypeStruct(shape, jnp.float32)

    def held(count):
        return jax.ShapeDtypeStruct((count, streams, width, chans), jnp.bfloat16)

    def loads(step):
        return [step, -step] if step < half else [step]

    sums = f32(streams, rows, chans)
    params = pltpu.CompilerParams(vmem_limit_bytes=12 << 20)
    cost = pl.CostEstimate(flops=0, bytes_accessed=16 << 20, transcendentals=0)

    def blocks(step):
        return [0] + loads(1) if step == 1 else loads(step)

    def left(step):
        if step >= half:
            return []
        last, halfway = len(blocks(step)) - 1, (width // 2, width)
        return [(last, streams - 1, *halfway) if step < half - 1 else (last, streams - 1, 0, width)]

    def pieces(step):
        lacking = {(b, s): low for b, s, low, _ in left(step)}
        every = [(b, s) for s in range(streams) for b in range(len(blocks(step)))]
        found = [(b, s, 0, lacking.get((b, s), width)) for b, s in every]
        return [piece for piece in found if piece[3]]

    weights = pl.pallas_call(
        functools.partial(load_kernel, order, blocks(1), pieces(1)),
        out_shape=held(len(blocks(1))),
        in_specs=[HBM],
        out_specs=VMEM,
        scratch_shapes=[pltpu.SemaphoreType.DMA((len(pieces(1)),))],
        compiler_params=params,
        cost_estimate=cost,
        name="load_first",
    )(weight)
    fore, aft, total = tokens, tokens, None
    for step in range(1, half):
        fore = lax.ppermute(fore, "tp", ahead)
        aft = lax.ppermute(aft, "tp", back)
        fore, total, weights = lax.optimization_barrier((fore, total, weights))
        aft, total, weights = lax.optimization_barrier((aft, total, weights))
        first = step == 1
        xs = [tokens, fore, aft] if first else [fore, aft]
        extra = [filter_taps, decay_rate, residue] if first else [total]
        made = []
        if first:
            made = [f32(lags, streams, groups, LANES), f32(5, modes, groups, LANES)]
            made += [f32(modes, 8, chans), f32(modes, chans), f32(modes, 8, chans)]
        total, weights, *made = pl.pallas_call(
            functools.partial(
                middle_kernel, order, blocks(step), left(step), blocks(step + 1), pieces(step + 1),
                len(extra),
            ),
            out_shape=[sums, held(len(blocks(step + 1)))] + made,
            in_specs=[VMEM] * (len(xs) + 1) + [HBM] + [VMEM] * len(extra),
            out_specs=[VMEM] * (2 + len(made)),
            scratch_shapes=[
                pltpu.VMEM((2, width, chans), jnp.bfloat16),
                pltpu.SemaphoreType.DMA((2,)),
                pltpu.SemaphoreType.DMA((len(pieces(step + 1)),)),
            ],
            input_output_aliases={} if first else {len(xs) + 2: 0},
            compiler_params=params,
            cost_estimate=cost,
            name="project_blocks",
        )(*xs, weights, weight, *extra)
        if first:
            taps, table, tile, tile_step, fade = made
    fore = lax.ppermute(fore[:, : width // 2], "tp", ahead)
    aft = lax.ppermute(aft[:, width // 2 :], "tp", back)
    total = pl.pallas_call(
        half_kernel,
        out_shape=sums,
        in_specs=[VMEM] * 3,
        out_specs=VMEM,
        input_output_aliases={2: 0},
        compiler_params=params,
        cost_estimate=cost,
        name="project_half",
    )(fore, weights, total)
    total, source, local = pl.pallas_call(
        last_kernel,
        out_shape=[sums, f32(rows, chans), f32(modes + EDGE, groups, LANES)],
        in_specs=[VMEM] * 6,
        out_specs=[VMEM] * 3,
        input_output_aliases={5: 0},
        compiler_params=params,
        cost_estimate=cost,
        name="project_last",
    )(aft, weights, filter_taps, tile_step, fade, total)

    partner = lax.ppermute(local, "ctx", [(j, j ^ 1) for j in range(ctx)])
    lone = ctx == 4
    chip = pl.pallas_call(
        functools.partial(chip_kernel, lone),
        out_shape=f32(modes + (6 if lone else EDGE), groups, LANES),
        in_specs=[VMEM] * 4,
        out_specs=VMEM,
        compiler_params=params,
        name="chip_state",
    )(local, partner, taps, table)
    sent = [
        lax.ppermute(chip, "ctx", [(j, (j + d) % ctx) for j in range(ctx)])
        for d in range(2, ctx, 2)
    ]
    query, response, heads = pl.pallas_call(
        local_kernel,
        out_shape=[f32(rows, chans), f32(rows, chans), f32(2, groups, LANES)],
        in_specs=[VMEM] * 4,
        out_specs=[VMEM] * 3,
        scratch_shapes=[
            pltpu.VMEM((rows, groups, LANES), jnp.float32),
            pltpu.VMEM((8, groups, LANES), jnp.float32),
            pltpu.VMEM((rows, groups, LANES), jnp.float32),
        ],
        compiler_params=params,
        cost_estimate=cost,
        name="local_response",
    )(total, source, filter_taps, table)
    return pl.pallas_call(
        functools.partial(final_kernel, lone, len(sent)),
        out_shape=jax.ShapeDtypeStruct((rows, chans), jnp.bfloat16),
        in_specs=[VMEM] * (len(sent) + 9),
        out_specs=HBM,
        scratch_shapes=[
            pltpu.VMEM((modes, groups, LANES), jnp.float32),
            pltpu.VMEM((2, groups, LANES), jnp.float32),
            pltpu.VMEM((rows, chans), jnp.bfloat16),
            pltpu.SemaphoreType.DMA((groups // 2,)),
        ],
        compiler_params=params,
        name="carried_response",
    )(*sent, local, partner, query, response, heads, taps, table, tile, tile_step)


def solution(mesh):
    return jax.shard_map(
        on_device,
        mesh=mesh,
        in_specs=(
            P("ctx", "tp"),
            P(None, None, "tp"),
            P(None, None, "tp"),
            P(None, "tp"),
            P(None, "tp"),
        ),
        out_specs=P("ctx", "tp"),
        check_vma=False,
    )
```

```python
import functools

import jax
import jax.numpy as jnp
from jax import lax
from jax.experimental import pallas as pl
from jax.experimental.pallas import tpu as pltpu
from jax.sharding import PartitionSpec as P

LANES = 128
COLS = 256
WIDE = 512
SOON = 4
GRID_ROWS = 4
EDGE = 10
UNROLL = 16
VMEM = pl.BlockSpec(memory_space=pltpu.VMEM)
HBM = pl.BlockSpec(memory_space=pltpu.HBM)


def ring_order(count):
    if count % (2 * GRID_ROWS):
        return list(range(count))
    cols = count // GRID_ROWS
    cells = [(0, c) for c in range(cols)]
    for r in range(1, GRID_ROWS):
        inner = list(range(1, cols))
        cells += [(r, c) for c in (reversed(inner) if r % 2 else inner)]
    cells += [(r, 0) for r in range(GRID_ROWS - 1, 0, -1)]
    return [r * cols + c for r, c in cells]


def owner_at(order, step):
    me = lax.axis_index("tp")
    owner = jnp.int32(0)
    for place, index in enumerate(order):
        owner = jnp.where(me == index, order[(place - step) % len(order)], owner)
    return owner


def piece_loads(order, steps, pieces, w_ref, target, sem):
    width = w_ref.shape[1] // len(order)
    starts = [pl.multiple_of(owner_at(order, step) * width, width) for step in steps]
    return [
        pltpu.make_async_copy(
            w_ref.at[s, pl.ds(starts[b] + low, high - low), :], target(i, b, s, low, high), sem.at[i]
        )
        for i, (b, s, low, high) in enumerate(pieces)
    ]


def add_products(xs, weights, total, s, fresh=False, cols=COLS):
    cols = min(cols, total.shape[2])
    for c in range(0, total.shape[2], cols):
        at = slice(c, c + cols)
        terms = [
            jnp.dot(x, weights(b, at), preferred_element_type=jnp.float32) for b, x in enumerate(xs)
        ]
        total[s, :, at] = sum(terms) if fresh else total[s, :, at] + sum(terms)


def spread(out_ref, value):
    groups, lanes = out_ref.shape[-2:]
    for g in range(groups):
        out_ref[..., g, :] = value[..., g * lanes : (g + 1) * lanes]


def held_part(held):
    return lambda i, b, s, low, high: held.at[b, s, pl.ds(low, high - low), :]


def load_kernel(order, steps, pieces, w_ref, held, sem):
    copies = piece_loads(order, steps, pieces, w_ref, held_part(held), sem)
    for copy in copies:
        copy.start()
    for copy in copies:
        copy.wait()


def middle_kernel(order, here, missing, steps, pieces, inputs_count, *refs):
    xs, (held, w_ref, *refs) = refs[: len(here)], refs[len(here) :]
    *refs, rest, rest_sem, sem = refs
    inputs, (total, next_held, *made) = refs[:inputs_count], refs[inputs_count:]
    fresh = bool(made)
    late = piece_loads(
        order, here, missing, w_ref,
        lambda i, b, s, low, high: rest.at[i, pl.ds(0, high - low), :], rest_sem,
    )
    ahead = piece_loads(order, steps, pieces, w_ref, held_part(next_held), sem)
    soon = max(SOON - len(late), 0)
    for copy in late + ahead[:soon]:
        copy.start()
    if made:
        make_tables(*inputs, *made, total.shape[1])
    whole = min(s for _, s, _, _ in missing) if missing else held.shape[1]

    @pl.loop(0, whole)
    def _(s):
        add_products([x[...] for x in xs], lambda b, at: held[b, s, :, at], total, s, fresh)

    for copy in ahead[soon:]:
        copy.start()
    for copy in late:
        copy.wait()
    for s in range(whole, held.shape[1]):
        gaps = {b: (i, low, high) for i, (b, k, low, high) in enumerate(missing) if k == s}
        parts = []
        for b, x in enumerate(xs):
            i, low, high = gaps.get(b, (0, x.shape[1], x.shape[1]))
            if low:
                parts.append((x[:, :low], lambda at, b=b, low=low: held[b, s, :low, at]))
            if low < high:
                parts.append((x[:, low:], lambda at, i=i, n=high - low: rest[i, :n, at]))
        values, weights = zip(*parts)
        add_products(values, lambda k, at: weights[k](at), total, s, fresh)
    for copy in ahead:
        copy.wait()


def half_kernel(x_ref, held, _, total):
    depth = x_ref.shape[1]
    for s in range(total.shape[0]):
        add_products([x_ref[...]], lambda b, at: held[0, s, :depth, at], total, s, cols=WIDE)


def make_tables(taps_in, decay, residue, taps, table, tile, tile_step, fade, rows):
    rate = decay[...]
    coeffs = residue[...] * jnp.sqrt(1.0 - jnp.exp(-2.0 * rate))
    for i, power in enumerate((1, rows, rows - 1, rows - 2)):
        spread(table.at[i], jnp.exp(-rate * power))
    spread(table.at[4], coeffs)
    spread(taps, taps_in[...])
    for r in range(tile.shape[1]):
        tile[:, r, :] = coeffs * jnp.exp(-rate * (r - 1.0))
        fade[:, r, :] = jnp.exp(-rate * (fade.shape[1] - 1.0 - r))
    tile_step[...] = jnp.exp(-rate * tile.shape[1])


def over_rows(step, start, stop, carry):
    aligned = -(-start // UNROLL) * UNROLL
    for t in range(start, aligned):
        carry = step(t, carry)

    def group(i, carry):
        for j in range(UNROLL):
            carry = step(i * UNROLL + j, carry)
        return carry

    return lax.fori_loop(aligned // UNROLL, stop // UNROLL, group, carry)


def filtered(taps, s, value, cols):
    one, two = pltpu.roll(value, 1, 0), pltpu.roll(value, 2, 0)
    lags = [taps[j, s : s + 1, cols] for j in range(3)]
    return lags[0] * value + lags[1] * one + lags[2] * two


def last_kernel(x_ref, held, taps, tile_step, fade, _, total, source, out_ref):
    depth = x_ref.shape[1]
    for s in range(total.shape[0]):
        add_products([x_ref[...]], lambda b, at: held[0, s, depth:, at], total, s, cols=WIDE)
    rows = source.shape[0]
    modes, tall, _ = fade.shape
    groups, lanes = out_ref.shape[1:]
    row = lax.broadcasted_iota(jnp.int32, (tall, lanes), 0)
    for g in range(groups):
        cols = slice(g * lanes, (g + 1) * lanes)
        one, two = total[1, :, cols], total[2, :, cols]
        value = filtered(taps, 1, one, cols) * filtered(taps, 2, two, cols)
        source[:, cols] = value
        step = [jnp.broadcast_to(tile_step[n : n + 1, cols], (tall, lanes)) for n in range(modes)]
        first = jnp.where(row < 2, 0.0, value[:tall])
        state = [first] * modes
        for i in range(tall, rows, tall):
            state = [a * b + value[i : i + tall] for a, b in zip(state, step)]
        for n in range(modes):
            out_ref[n, g : g + 1, :] = jnp.sum(state[n] * fade[n, :, cols], axis=0, keepdims=True)
        query = total[0, rows - tall :, cols]
        for s, ends in ((1, one), (2, two)):
            out_ref[modes + s * 2 - 2 : modes + s * 2, g, :] = ends[:2]
        for s, ends in ((0, query), (1, one), (2, two)):
            low = modes + 4 + s * 2
            out_ref[low : low + 2, g, :] = ends[-2:]


def tree_sum(terms):
    while len(terms) > 1:
        terms = [a + b for a, b in zip(terms[::2], terms[1::2])] + terms[len(terms) & ~1 :]
    return terms[0]


def local_kernel(total, natural, taps, table, query, response, heads, work, low, source):
    rows, groups, lanes = source.shape
    modes = table.shape[1]
    for g in range(groups):
        cols = slice(g * lanes, (g + 1) * lanes)
        value = total[0, :, cols]
        query[:, cols] = filtered(taps, 0, value, cols)
        low[:, g, :] = value[:8]
        source[:, g, :] = natural[:, cols]
    for j in range(2):
        heads[j] = low[j]
        work[j] = jnp.zeros((groups, lanes), jnp.float32)

    def step_row(t, state):
        u = source[t]
        state = [table[0, n] * state[n] + u for n in range(modes)]
        work[t] = tree_sum([table[4, n] * state[n] for n in range(modes)])
        return state

    over_rows(step_row, 2, rows, [jnp.zeros((groups, lanes), jnp.float32)] * modes)
    for g in range(groups):
        response[:, g * lanes : (g + 1) * lanes] = work[:, g, :]


def edge(taps, s, first, second, before, last):
    return (
        taps[0, s] * first + taps[1, s] * last + taps[2, s] * before,
        taps[0, s] * second + taps[1, s] * first + taps[2, s] * last,
    )


def lead_sources(taps, heads, rims):
    one = edge(taps, 1, heads[0], heads[1], rims[2], rims[3])
    two = edge(taps, 2, heads[2], heads[3], rims[4], rims[5])
    return one[0] * two[0], one[1] * two[1]


class Summary:
    def __init__(self, rows, modes):
        self.state = rows[:modes]
        self.heads = rows[modes : modes + 4]
        self.rims = rows[modes + 4 :]

    @classmethod
    def read(cls, ref, modes):
        return cls([ref[i] for i in range(ref.shape[0])], modes)

    @classmethod
    def chosen(cls, odd, when_odd, when_even, modes):
        pairs = zip(when_odd.rows(), when_even.rows())
        return cls([jnp.where(odd, a, b) for a, b in pairs], modes)

    def rows(self):
        return self.state + self.heads + self.rims

    def complete(self, taps, rims, by_first, by_second):
        u0, u1 = lead_sources(taps, self.heads, rims)
        return [x + f * u0 + g * u1 for x, f, g in zip(self.state, by_first, by_second)]


def powers(table):
    return [[table[i, n] for n in range(table.shape[1])] for i in range(table.shape[0])]


def chip_kernel(lone, local, partner, taps, table, out_ref):
    modes = table.shape[1]
    odd = lax.rem(lax.axis_index("ctx"), 2) == 1
    mine, other = Summary.read(local, modes), Summary.read(partner, modes)
    first = Summary.chosen(odd, other, mine, modes)
    second = Summary.chosen(odd, mine, other, modes)
    _, block, less_one, less_two, _ = powers(table)
    start, heads = first.state, first.heads
    if lone:
        start, heads = first.complete(taps, [jnp.zeros_like(heads[0])] * 6, less_one, less_two), []
    end = second.complete(taps, first.rims, less_one, less_two)
    joined = [d * x + y for d, x, y in zip(block, start, end)]
    for i, value in enumerate(joined + heads + second.rims):
        out_ref[i] = value


def final_kernel(lone, count, *refs):
    sent = refs[:count]
    local, partner, query, response, query_heads, taps, table, tile, tile_step, *refs = refs[count:]
    out_ref, states, firsts, rounded_out, out_sem = refs
    rows = query.shape[0]
    groups, lanes = local.shape[1:]
    modes = table.shape[1]
    zero = jnp.zeros((groups, lanes), jnp.float32)
    index = lax.axis_index("ctx")
    odd = lax.rem(index, 2) == 1
    _, block, less_one, less_two, _ = powers(table)
    values = [
        [jnp.where(index >= 2 * (d + 1), ref[i], zero) for i in range(ref.shape[0])]
        for d, ref in enumerate(sent)
    ]
    rims = [value[-6:] for value in values] + [[zero] * 6]
    state = [zero] * modes
    for d in reversed(range(count)):
        end = values[d][:modes]
        if not lone:
            end = Summary(values[d], modes).complete(
                taps,
                rims[d + 1],
                [a * b for a, b in zip(block, less_one)],
                [a * b for a, b in zip(block, less_two)],
            )
        state = [d * d * x + y for d, x, y in zip(block, state, end)]
    before = Summary.read(partner, modes)
    end = before.complete(taps, rims[0], less_one, less_two)
    state = [jnp.where(odd, d * x + y, x) for d, x, y in zip(block, state, end)]
    rim = [jnp.where(odd, a, b) for a, b in zip(before.rims, rims[0])]

    leads = lead_sources(taps, Summary.read(local, modes).heads, rim)
    heads = edge(taps, 0, query_heads[0], query_heads[1], rim[0], rim[1])
    for t, u in enumerate(leads):
        state = [table[0, n] * state[n] + u for n in range(modes)]
        firsts[t] = heads[t] * tree_sum([table[4, n] * state[n] for n in range(modes)])
    for n in range(modes):
        states[n] = state[n]

    tall = tile.shape[1]
    row = lax.broadcasted_iota(jnp.int32, (tall, lanes), 0)
    copies = []
    for g in range(groups):
        cols = slice(g * lanes, (g + 1) * lanes)
        carried = [tile[n, :, cols] * states[n, g : g + 1, :] for n in range(modes)]
        step = [jnp.broadcast_to(tile_step[n : n + 1, cols], (tall, lanes)) for n in range(modes)]
        for i in range(0, rows, 2 * tall):
            pair = []
            for at in (slice(i, i + tall), slice(i + tall, i + 2 * tall)):
                value = query[at, cols] * (response[at, cols] + tree_sum(carried))
                if at.start == 0:
                    value = jnp.where(row == 0, firsts[0, g : g + 1, :], value)
                    value = jnp.where(row == 1, firsts[1, g : g + 1, :], value)
                pair.append(value)
                carried = [a * b for a, b in zip(carried, step)]
            rounded_out[i : i + 2 * tall, cols] = jnp.concatenate(pair, axis=0).astype(out_ref.dtype)
        if g % 2:
            wide = slice((g - 1) * lanes, (g + 1) * lanes)
            k = g // 2
            copies.append(
                pltpu.make_async_copy(rounded_out.at[:, wide], out_ref.at[:, wide], out_sem.at[k])
            )
            copies[-1].start()
    for copy in copies:
        copy.wait()


def on_device(tokens, in_weight, filter_taps, decay_rate, residue):
    rows, width = tokens.shape
    streams, chans = in_weight.shape[1:]
    lags = filter_taps.shape[0]
    modes = decay_rate.shape[0]
    groups = chans // LANES
    tp, ctx = lax.axis_size("tp"), lax.axis_size("ctx")
    order = ring_order(tp)
    weight = jnp.transpose(in_weight, (1, 0, 2))
    half = tp // 2
    ahead = [(order[i], order[(i + 1) % tp]) for i in range(tp)]
    back = [(b, a) for a, b in ahead]

    def f32(*shape):
        return jax.ShapeDtypeStruct(shape, jnp.float32)

    def held(count):
        return jax.ShapeDtypeStruct((count, streams, width, chans), jnp.bfloat16)

    def loads(step):
        return [step, -step] if step < half else [step]

    sums = f32(streams, rows, chans)
    params = pltpu.CompilerParams(vmem_limit_bytes=12 << 20)
    cost = pl.CostEstimate(flops=0, bytes_accessed=16 << 20, transcendentals=0)

    def blocks(step):
        return [0] + loads(1) if step == 1 else loads(step)

    def left(step):
        if step >= half:
            return []
        last, halfway = len(blocks(step)) - 1, (width // 2, width)
        return [(last, streams - 1, *halfway) if step < half - 1 else (last, streams - 1, 0, width)]

    def pieces(step):
        lacking = {(b, s): low for b, s, low, _ in left(step)}
        every = [(b, s) for s in range(streams) for b in range(len(blocks(step)))]
        found = [(b, s, 0, lacking.get((b, s), width)) for b, s in every]
        return [piece for piece in found if piece[3]]

    weights = pl.pallas_call(
        functools.partial(load_kernel, order, blocks(1), pieces(1)),
        out_shape=held(len(blocks(1))),
        in_specs=[HBM],
        out_specs=VMEM,
        scratch_shapes=[pltpu.SemaphoreType.DMA((len(pieces(1)),))],
        compiler_params=params,
        cost_estimate=cost,
        name="load_first",
    )(weight)
    fore, aft, total = tokens, tokens, None
    for step in range(1, half):
        fore = lax.ppermute(fore, "tp", ahead)
        aft = lax.ppermute(aft, "tp", back)
        fore, total, weights = lax.optimization_barrier((fore, total, weights))
        aft, total, weights = lax.optimization_barrier((aft, total, weights))
        first = step == 1
        xs = [tokens, fore, aft] if first else [fore, aft]
        extra = [filter_taps, decay_rate, residue] if first else [total]
        made = []
        if first:
            made = [f32(lags, streams, groups, LANES), f32(5, modes, groups, LANES)]
            made += [f32(modes, 8, chans), f32(modes, chans), f32(modes, 8, chans)]
        total, weights, *made = pl.pallas_call(
            functools.partial(
                middle_kernel, order, blocks(step), left(step), blocks(step + 1), pieces(step + 1),
                len(extra),
            ),
            out_shape=[sums, held(len(blocks(step + 1)))] + made,
            in_specs=[VMEM] * (len(xs) + 1) + [HBM] + [VMEM] * len(extra),
            out_specs=[VMEM] * (2 + len(made)),
            scratch_shapes=[
                pltpu.VMEM((2, width, chans), jnp.bfloat16),
                pltpu.SemaphoreType.DMA((2,)),
                pltpu.SemaphoreType.DMA((len(pieces(step + 1)),)),
            ],
            input_output_aliases={} if first else {len(xs) + 2: 0},
            compiler_params=params,
            cost_estimate=cost,
            name="project_blocks",
        )(*xs, weights, weight, *extra)
        if first:
            taps, table, tile, tile_step, fade = made
    fore = lax.ppermute(fore[:, : width // 2], "tp", ahead)
    aft = lax.ppermute(aft[:, width // 2 :], "tp", back)
    total = pl.pallas_call(
        half_kernel,
        out_shape=sums,
        in_specs=[VMEM] * 3,
        out_specs=VMEM,
        input_output_aliases={2: 0},
        compiler_params=params,
        cost_estimate=cost,
        name="project_half",
    )(fore, weights, total)
    total, source, local = pl.pallas_call(
        last_kernel,
        out_shape=[sums, f32(rows, chans), f32(modes + EDGE, groups, LANES)],
        in_specs=[VMEM] * 6,
        out_specs=[VMEM] * 3,
        input_output_aliases={5: 0},
        compiler_params=params,
        cost_estimate=cost,
        name="project_last",
    )(aft, weights, filter_taps, tile_step, fade, total)

    partner = lax.ppermute(local, "ctx", [(j, j ^ 1) for j in range(ctx)])
    lone = ctx == 4
    chip = pl.pallas_call(
        functools.partial(chip_kernel, lone),
        out_shape=f32(modes + (6 if lone else EDGE), groups, LANES),
        in_specs=[VMEM] * 4,
        out_specs=VMEM,
        compiler_params=params,
        name="chip_state",
    )(local, partner, taps, table)
    sent = [
        lax.ppermute(chip, "ctx", [(j, (j + d) % ctx) for j in range(ctx)])
        for d in range(2, ctx, 2)
    ]
    query, response, heads = pl.pallas_call(
        local_kernel,
        out_shape=[f32(rows, chans), f32(rows, chans), f32(2, groups, LANES)],
        in_specs=[VMEM] * 4,
        out_specs=[VMEM] * 3,
        scratch_shapes=[
            pltpu.VMEM((rows, groups, LANES), jnp.float32),
            pltpu.VMEM((8, groups, LANES), jnp.float32),
            pltpu.VMEM((rows, groups, LANES), jnp.float32),
        ],
        compiler_params=params,
        cost_estimate=cost,
        name="local_response",
    )(total, source, filter_taps, table)
    return pl.pallas_call(
        functools.partial(final_kernel, lone, len(sent)),
        out_shape=jax.ShapeDtypeStruct((rows, chans), jnp.bfloat16),
        in_specs=[VMEM] * (len(sent) + 9),
        out_specs=HBM,
        scratch_shapes=[
            pltpu.VMEM((modes, groups, LANES), jnp.float32),
            pltpu.VMEM((2, groups, LANES), jnp.float32),
            pltpu.VMEM((rows, chans), jnp.bfloat16),
            pltpu.SemaphoreType.DMA((groups // 2,)),
        ],
        compiler_params=params,
        name="carried_response",
    )(*sent, local, partner, query, response, heads, taps, table, tile, tile_step)


def solution(mesh):
    return jax.shard_map(
        on_device,
        mesh=mesh,
        in_specs=(
            P("ctx", "tp"),
            P(None, None, "tp"),
            P(None, None, "tp"),
            P(None, "tp"),
            P(None, "tp"),
        ),
        out_specs=P("ctx", "tp"),
        check_vma=False,
    )
```

```python
import functools

import jax
import jax.numpy as jnp
from jax import lax
from jax.experimental import pallas as pl
from jax.experimental.pallas import tpu as pltpu
from jax.sharding import PartitionSpec as P

LANES = 128
COLS = 256
WIDE = 512
SOON = 4
GRID_ROWS = 4
EDGE = 10
UNROLL = 16
VMEM = pl.BlockSpec(memory_space=pltpu.VMEM)
HBM = pl.BlockSpec(memory_space=pltpu.HBM)


def ring_order(count):
    if count % (2 * GRID_ROWS):
        return list(range(count))
    cols = count // GRID_ROWS
    cells = [(0, c) for c in range(cols)]
    for r in range(1, GRID_ROWS):
        inner = list(range(1, cols))
        cells += [(r, c) for c in (reversed(inner) if r % 2 else inner)]
    cells += [(r, 0) for r in range(GRID_ROWS - 1, 0, -1)]
    return [r * cols + c for r, c in cells]


def owner_at(order, step):
    me = lax.axis_index("tp")
    owner = jnp.int32(0)
    for place, index in enumerate(order):
        owner = jnp.where(me == index, order[(place - step) % len(order)], owner)
    return owner


def piece_loads(order, steps, pieces, w_ref, target, sem):
    width = w_ref.shape[1] // len(order)
    starts = [pl.multiple_of(owner_at(order, step) * width, width) for step in steps]
    return [
        pltpu.make_async_copy(
            w_ref.at[s, pl.ds(starts[b] + low, high - low), :], target(i, b, s, low, high), sem.at[i]
        )
        for i, (b, s, low, high) in enumerate(pieces)
    ]


def add_products(xs, weights, total, s, fresh=False, cols=COLS):
    cols = min(cols, total.shape[2])
    for c in range(0, total.shape[2], cols):
        at = slice(c, c + cols)
        terms = [
            jnp.dot(x, weights(b, at), preferred_element_type=jnp.float32) for b, x in enumerate(xs)
        ]
        total[s, :, at] = sum(terms) if fresh else total[s, :, at] + sum(terms)


def spread(out_ref, value):
    groups, lanes = out_ref.shape[-2:]
    for g in range(groups):
        out_ref[..., g, :] = value[..., g * lanes : (g + 1) * lanes]


def held_part(held):
    return lambda i, b, s, low, high: held.at[b, s, pl.ds(low, high - low), :]


def load_kernel(order, steps, pieces, w_ref, held, sem):
    copies = piece_loads(order, steps, pieces, w_ref, held_part(held), sem)
    for copy in copies:
        copy.start()
    for copy in copies:
        copy.wait()


def middle_kernel(order, here, missing, steps, pieces, inputs_count, *refs):
    xs, (held, w_ref, *refs) = refs[: len(here)], refs[len(here) :]
    *refs, rest, rest_sem, sem = refs
    inputs, (total, next_held, *made) = refs[:inputs_count], refs[inputs_count:]
    fresh = bool(made)
    late = piece_loads(
        order, here, missing, w_ref,
        lambda i, b, s, low, high: rest.at[i, pl.ds(0, high - low), :], rest_sem,
    )
    ahead = piece_loads(order, steps, pieces, w_ref, held_part(next_held), sem)
    soon = max(SOON - len(late), 0)
    for copy in late + ahead[:soon]:
        copy.start()
    if made:
        make_tables(*inputs, *made, total.shape[1])
    whole = min(s for _, s, _, _ in missing) if missing else held.shape[1]

    @pl.loop(0, whole)
    def _(s):
        add_products([x[...] for x in xs], lambda b, at: held[b, s, :, at], total, s, fresh)

    for copy in ahead[soon:]:
        copy.start()
    for copy in late:
        copy.wait()
    for s in range(whole, held.shape[1]):
        gaps = {b: (i, low, high) for i, (b, k, low, high) in enumerate(missing) if k == s}
        parts = []
        for b, x in enumerate(xs):
            i, low, high = gaps.get(b, (0, x.shape[1], x.shape[1]))
            if low:
                parts.append((x[:, :low], lambda at, b=b, low=low: held[b, s, :low, at]))
            if low < high:
                parts.append((x[:, low:], lambda at, i=i, n=high - low: rest[i, :n, at]))
        values, weights = zip(*parts)
        add_products(values, lambda k, at: weights[k](at), total, s, fresh)
    for copy in ahead:
        copy.wait()


def half_kernel(x_ref, held, _, total):
    depth = x_ref.shape[1]
    for s in range(total.shape[0]):
        add_products([x_ref[...]], lambda b, at: held[0, s, :depth, at], total, s, cols=WIDE)


def make_tables(taps_in, decay, residue, taps, table, tile, tile_step, fade, rows):
    rate = decay[...]
    coeffs = residue[...] * jnp.sqrt(1.0 - jnp.exp(-2.0 * rate))
    for i, power in enumerate((1, rows, rows - 1, rows - 2)):
        spread(table.at[i], jnp.exp(-rate * power))
    spread(table.at[4], coeffs)
    spread(taps, taps_in[...])
    for r in range(tile.shape[1]):
        tile[:, r, :] = coeffs * jnp.exp(-rate * (r - 1.0))
        fade[:, r, :] = jnp.exp(-rate * (fade.shape[1] - 1.0 - r))
    tile_step[...] = jnp.exp(-rate * tile.shape[1])


def over_rows(step, start, stop, carry):
    aligned = -(-start // UNROLL) * UNROLL
    for t in range(start, aligned):
        carry = step(t, carry)

    def group(i, carry):
        for j in range(UNROLL):
            carry = step(i * UNROLL + j, carry)
        return carry

    return lax.fori_loop(aligned // UNROLL, stop // UNROLL, group, carry)


def filtered(taps, s, value, cols):
    one, two = pltpu.roll(value, 1, 0), pltpu.roll(value, 2, 0)
    lags = [taps[j, s : s + 1, cols] for j in range(3)]
    return lags[0] * value + lags[1] * one + lags[2] * two


def last_kernel(x_ref, held, taps, tile_step, fade, _, total, source, out_ref):
    depth = x_ref.shape[1]
    for s in (1, 2):
        add_products([x_ref[...]], lambda b, at: held[0, s, depth:, at], total, s, cols=WIDE)
    rows, chans = source.shape
    modes, tall, _ = fade.shape
    groups, lanes = out_ref.shape[1:]
    row = lax.broadcasted_iota(jnp.int32, (tall, lanes), 0)
    for g in range(groups):
        cols = slice(g * lanes, (g + 1) * lanes)
        one, two = total[1, :, cols], total[2, :, cols]
        value = filtered(taps, 1, one, cols) * filtered(taps, 2, two, cols)
        source[:, cols] = value
        step = [jnp.broadcast_to(tile_step[n : n + 1, cols], (tall, lanes)) for n in range(modes)]
        first = jnp.where(row < 2, 0.0, value[:tall])
        state = [first] * modes
        for i in range(tall, rows, tall):
            state = [a * b + value[i : i + tall] for a, b in zip(state, step)]
        for n in range(modes):
            out_ref[n, g : g + 1, :] = jnp.sum(state[n] * fade[n, :, cols], axis=0, keepdims=True)
        for s, ends in ((1, one), (2, two)):
            out_ref[modes + s * 2 - 2 : modes + s * 2, g, :] = ends[:2]
            out_ref[modes + 4 + s * 2 : modes + 6 + s * 2, g, :] = ends[-2:]
        if not g * lanes % min(WIDE, chans):
            at = slice(g * lanes, g * lanes + min(WIDE, chans))
            total[0, :, at] += jnp.dot(
                x_ref[...], held[0, 0, depth:, at], preferred_element_type=jnp.float32
            )
    for g in range(groups):
        out_ref[modes + 4 : modes + 6, g, :] = total[0, rows - 2 :, g * lanes : (g + 1) * lanes]


def tree_sum(terms):
    while len(terms) > 1:
        terms = [a + b for a, b in zip(terms[::2], terms[1::2])] + terms[len(terms) & ~1 :]
    return terms[0]


def local_kernel(total, natural, taps, table, query, response, heads, work, low, source):
    rows, groups, lanes = source.shape
    modes = table.shape[1]
    for g in range(groups):
        cols = slice(g * lanes, (g + 1) * lanes)
        value = total[0, :, cols]
        query[:, cols] = filtered(taps, 0, value, cols)
        low[:, g, :] = value[:8]
        source[:, g, :] = natural[:, cols]
    for j in range(2):
        heads[j] = low[j]
        work[j] = jnp.zeros((groups, lanes), jnp.float32)

    def step_row(t, state):
        u = source[t]
        state = [table[0, n] * state[n] + u for n in range(modes)]
        work[t] = tree_sum([table[4, n] * state[n] for n in range(modes)])
        return state

    over_rows(step_row, 2, rows, [jnp.zeros((groups, lanes), jnp.float32)] * modes)
    for g in range(groups):
        response[:, g * lanes : (g + 1) * lanes] = work[:, g, :]


def edge(taps, s, first, second, before, last):
    return (
        taps[0, s] * first + taps[1, s] * last + taps[2, s] * before,
        taps[0, s] * second + taps[1, s] * first + taps[2, s] * last,
    )


def lead_sources(taps, heads, rims):
    one = edge(taps, 1, heads[0], heads[1], rims[2], rims[3])
    two = edge(taps, 2, heads[2], heads[3], rims[4], rims[5])
    return one[0] * two[0], one[1] * two[1]


class Summary:
    def __init__(self, rows, modes):
        self.state = rows[:modes]
        self.heads = rows[modes : modes + 4]
        self.rims = rows[modes + 4 :]

    @classmethod
    def read(cls, ref, modes):
        return cls([ref[i] for i in range(ref.shape[0])], modes)

    @classmethod
    def chosen(cls, odd, when_odd, when_even, modes):
        pairs = zip(when_odd.rows(), when_even.rows())
        return cls([jnp.where(odd, a, b) for a, b in pairs], modes)

    def rows(self):
        return self.state + self.heads + self.rims

    def complete(self, taps, rims, by_first, by_second):
        u0, u1 = lead_sources(taps, self.heads, rims)
        return [x + f * u0 + g * u1 for x, f, g in zip(self.state, by_first, by_second)]


def powers(table):
    return [[table[i, n] for n in range(table.shape[1])] for i in range(table.shape[0])]


def chip_kernel(lone, local, partner, taps, table, out_ref):
    modes = table.shape[1]
    odd = lax.rem(lax.axis_index("ctx"), 2) == 1
    mine, other = Summary.read(local, modes), Summary.read(partner, modes)
    first = Summary.chosen(odd, other, mine, modes)
    second = Summary.chosen(odd, mine, other, modes)
    _, block, less_one, less_two, _ = powers(table)
    start, heads = first.state, first.heads
    if lone:
        start, heads = first.complete(taps, [jnp.zeros_like(heads[0])] * 6, less_one, less_two), []
    end = second.complete(taps, first.rims, less_one, less_two)
    joined = [d * x + y for d, x, y in zip(block, start, end)]
    for i, value in enumerate(joined + heads + second.rims):
        out_ref[i] = value


def final_kernel(lone, count, *refs):
    sent = refs[:count]
    local, partner, query, response, query_heads, taps, table, tile, tile_step, *refs = refs[count:]
    out_ref, states, firsts, rounded_out, out_sem = refs
    rows = query.shape[0]
    groups, lanes = local.shape[1:]
    modes = table.shape[1]
    zero = jnp.zeros((groups, lanes), jnp.float32)
    index = lax.axis_index("ctx")
    odd = lax.rem(index, 2) == 1
    _, block, less_one, less_two, _ = powers(table)
    values = [
        [jnp.where(index >= 2 * (d + 1), ref[i], zero) for i in range(ref.shape[0])]
        for d, ref in enumerate(sent)
    ]
    rims = [value[-6:] for value in values] + [[zero] * 6]
    state = [zero] * modes
    for d in reversed(range(count)):
        end = values[d][:modes]
        if not lone:
            end = Summary(values[d], modes).complete(
                taps,
                rims[d + 1],
                [a * b for a, b in zip(block, less_one)],
                [a * b for a, b in zip(block, less_two)],
            )
        state = [d * d * x + y for d, x, y in zip(block, state, end)]
    before = Summary.read(partner, modes)
    end = before.complete(taps, rims[0], less_one, less_two)
    state = [jnp.where(odd, d * x + y, x) for d, x, y in zip(block, state, end)]
    rim = [jnp.where(odd, a, b) for a, b in zip(before.rims, rims[0])]

    leads = lead_sources(taps, Summary.read(local, modes).heads, rim)
    heads = edge(taps, 0, query_heads[0], query_heads[1], rim[0], rim[1])
    for t, u in enumerate(leads):
        state = [table[0, n] * state[n] + u for n in range(modes)]
        firsts[t] = heads[t] * tree_sum([table[4, n] * state[n] for n in range(modes)])
    for n in range(modes):
        states[n] = state[n]

    tall = tile.shape[1]
    row = lax.broadcasted_iota(jnp.int32, (tall, lanes), 0)
    copies = []
    for g in range(groups):
        cols = slice(g * lanes, (g + 1) * lanes)
        carried = [tile[n, :, cols] * states[n, g : g + 1, :] for n in range(modes)]
        step = [jnp.broadcast_to(tile_step[n : n + 1, cols], (tall, lanes)) for n in range(modes)]
        for i in range(0, rows, 2 * tall):
            pair = []
            for at in (slice(i, i + tall), slice(i + tall, i + 2 * tall)):
                value = query[at, cols] * (response[at, cols] + tree_sum(carried))
                if at.start == 0:
                    value = jnp.where(row == 0, firsts[0, g : g + 1, :], value)
                    value = jnp.where(row == 1, firsts[1, g : g + 1, :], value)
                pair.append(value)
                carried = [a * b for a, b in zip(carried, step)]
            rounded_out[i : i + 2 * tall, cols] = jnp.concatenate(pair, axis=0).astype(out_ref.dtype)
        if g % 2:
            wide = slice((g - 1) * lanes, (g + 1) * lanes)
            k = g // 2
            copies.append(
                pltpu.make_async_copy(rounded_out.at[:, wide], out_ref.at[:, wide], out_sem.at[k])
            )
            copies[-1].start()
    for copy in copies:
        copy.wait()


def on_device(tokens, in_weight, filter_taps, decay_rate, residue):
    rows, width = tokens.shape
    streams, chans = in_weight.shape[1:]
    lags = filter_taps.shape[0]
    modes = decay_rate.shape[0]
    groups = chans // LANES
    tp, ctx = lax.axis_size("tp"), lax.axis_size("ctx")
    order = ring_order(tp)
    weight = jnp.transpose(in_weight, (1, 0, 2))
    half = tp // 2
    ahead = [(order[i], order[(i + 1) % tp]) for i in range(tp)]
    back = [(b, a) for a, b in ahead]

    def f32(*shape):
        return jax.ShapeDtypeStruct(shape, jnp.float32)

    def held(count):
        return jax.ShapeDtypeStruct((count, streams, width, chans), jnp.bfloat16)

    def loads(step):
        return [step, -step] if step < half else [step]

    sums = f32(streams, rows, chans)
    params = pltpu.CompilerParams(vmem_limit_bytes=12 << 20)
    cost = pl.CostEstimate(flops=0, bytes_accessed=16 << 20, transcendentals=0)

    def blocks(step):
        return [0] + loads(1) if step == 1 else loads(step)

    def left(step):
        if step >= half:
            return []
        last, halfway = len(blocks(step)) - 1, (width // 2, width)
        return [(last, streams - 1, *halfway) if step < half - 1 else (last, streams - 1, 0, width)]

    def pieces(step):
        lacking = {(b, s): low for b, s, low, _ in left(step)}
        every = [(b, s) for s in range(streams) for b in range(len(blocks(step)))]
        found = [(b, s, 0, lacking.get((b, s), width)) for b, s in every]
        return [piece for piece in found if piece[3]]

    weights = pl.pallas_call(
        functools.partial(load_kernel, order, blocks(1), pieces(1)),
        out_shape=held(len(blocks(1))),
        in_specs=[HBM],
        out_specs=VMEM,
        scratch_shapes=[pltpu.SemaphoreType.DMA((len(pieces(1)),))],
        compiler_params=params,
        cost_estimate=cost,
        name="load_first",
    )(weight)
    fore, aft, total = tokens, tokens, None
    for step in range(1, half):
        fore = lax.ppermute(fore, "tp", ahead)
        aft = lax.ppermute(aft, "tp", back)
        fore, total, weights = lax.optimization_barrier((fore, total, weights))
        aft, total, weights = lax.optimization_barrier((aft, total, weights))
        first = step == 1
        xs = [tokens, fore, aft] if first else [fore, aft]
        extra = [filter_taps, decay_rate, residue] if first else [total]
        made = []
        if first:
            made = [f32(lags, streams, groups, LANES), f32(5, modes, groups, LANES)]
            made += [f32(modes, 8, chans), f32(modes, chans), f32(modes, 8, chans)]
        total, weights, *made = pl.pallas_call(
            functools.partial(
                middle_kernel, order, blocks(step), left(step), blocks(step + 1), pieces(step + 1),
                len(extra),
            ),
            out_shape=[sums, held(len(blocks(step + 1)))] + made,
            in_specs=[VMEM] * (len(xs) + 1) + [HBM] + [VMEM] * len(extra),
            out_specs=[VMEM] * (2 + len(made)),
            scratch_shapes=[
                pltpu.VMEM((2, width, chans), jnp.bfloat16),
                pltpu.SemaphoreType.DMA((2,)),
                pltpu.SemaphoreType.DMA((len(pieces(step + 1)),)),
            ],
            input_output_aliases={} if first else {len(xs) + 2: 0},
            compiler_params=params,
            cost_estimate=cost,
            name="project_blocks",
        )(*xs, weights, weight, *extra)
        if first:
            taps, table, tile, tile_step, fade = made
    fore = lax.ppermute(fore[:, : width // 2], "tp", ahead)
    aft = lax.ppermute(aft[:, width // 2 :], "tp", back)
    total = pl.pallas_call(
        half_kernel,
        out_shape=sums,
        in_specs=[VMEM] * 3,
        out_specs=VMEM,
        input_output_aliases={2: 0},
        compiler_params=params,
        cost_estimate=cost,
        name="project_half",
    )(fore, weights, total)
    total, source, local = pl.pallas_call(
        last_kernel,
        out_shape=[sums, f32(rows, chans), f32(modes + EDGE, groups, LANES)],
        in_specs=[VMEM] * 6,
        out_specs=[VMEM] * 3,
        input_output_aliases={5: 0},
        compiler_params=params,
        cost_estimate=cost,
        name="project_last",
    )(aft, weights, filter_taps, tile_step, fade, total)

    partner = lax.ppermute(local, "ctx", [(j, j ^ 1) for j in range(ctx)])
    lone = ctx == 4
    chip = pl.pallas_call(
        functools.partial(chip_kernel, lone),
        out_shape=f32(modes + (6 if lone else EDGE), groups, LANES),
        in_specs=[VMEM] * 4,
        out_specs=VMEM,
        compiler_params=params,
        name="chip_state",
    )(local, partner, taps, table)
    sent = [
        lax.ppermute(chip, "ctx", [(j, (j + d) % ctx) for j in range(ctx)])
        for d in range(2, ctx, 2)
    ]
    query, response, heads = pl.pallas_call(
        local_kernel,
        out_shape=[f32(rows, chans), f32(rows, chans), f32(2, groups, LANES)],
        in_specs=[VMEM] * 4,
        out_specs=[VMEM] * 3,
        scratch_shapes=[
            pltpu.VMEM((rows, groups, LANES), jnp.float32),
            pltpu.VMEM((8, groups, LANES), jnp.float32),
            pltpu.VMEM((rows, groups, LANES), jnp.float32),
        ],
        compiler_params=params,
        cost_estimate=cost,
        name="local_response",
    )(total, source, filter_taps, table)
    return pl.pallas_call(
        functools.partial(final_kernel, lone, len(sent)),
        out_shape=jax.ShapeDtypeStruct((rows, chans), jnp.bfloat16),
        in_specs=[VMEM] * (len(sent) + 9),
        out_specs=HBM,
        scratch_shapes=[
            pltpu.VMEM((modes, groups, LANES), jnp.float32),
            pltpu.VMEM((2, groups, LANES), jnp.float32),
            pltpu.VMEM((rows, chans), jnp.bfloat16),
            pltpu.SemaphoreType.DMA((groups // 2,)),
        ],
        compiler_params=params,
        name="carried_response",
    )(*sent, local, partner, query, response, heads, taps, table, tile, tile_step)


def solution(mesh):
    return jax.shard_map(
        on_device,
        mesh=mesh,
        in_specs=(
            P("ctx", "tp"),
            P(None, None, "tp"),
            P(None, None, "tp"),
            P(None, "tp"),
            P(None, "tp"),
        ),
        out_specs=P("ctx", "tp"),
        check_vma=False,
    )
```

```python
import functools

import jax
import jax.numpy as jnp
from jax import lax
from jax.experimental import pallas as pl
from jax.experimental.pallas import tpu as pltpu
from jax.sharding import PartitionSpec as P

LANES = 128
COLS = 256
WIDE = 512
SOON = 8
GRID_ROWS = 4
EDGE = 10
UNROLL = 16
VMEM = pl.BlockSpec(memory_space=pltpu.VMEM)
HBM = pl.BlockSpec(memory_space=pltpu.HBM)


def ring_order(count):
    if count % (2 * GRID_ROWS):
        return list(range(count))
    cols = count // GRID_ROWS
    cells = [(0, c) for c in range(cols)]
    for r in range(1, GRID_ROWS):
        inner = list(range(1, cols))
        cells += [(r, c) for c in (reversed(inner) if r % 2 else inner)]
    cells += [(r, 0) for r in range(GRID_ROWS - 1, 0, -1)]
    return [r * cols + c for r, c in cells]


def owner_at(order, step):
    me = lax.axis_index("tp")
    owner = jnp.int32(0)
    for place, index in enumerate(order):
        owner = jnp.where(me == index, order[(place - step) % len(order)], owner)
    return owner


def piece_loads(order, steps, pieces, w_ref, target, sem):
    width = w_ref.shape[1] // len(order)
    starts = [pl.multiple_of(owner_at(order, step) * width, width) for step in steps]
    return [
        pltpu.make_async_copy(
            w_ref.at[s, pl.ds(starts[b] + low, high - low), :], target(i, b, s, low, high), sem.at[i]
        )
        for i, (b, s, low, high) in enumerate(pieces)
    ]


def add_products(xs, weights, total, s, fresh=False, cols=COLS):
    cols = min(cols, total.shape[2])
    for c in range(0, total.shape[2], cols):
        at = slice(c, c + cols)
        terms = [
            jnp.dot(x, weights(b, at), preferred_element_type=jnp.float32) for b, x in enumerate(xs)
        ]
        total[s, :, at] = sum(terms) if fresh else total[s, :, at] + sum(terms)


def spread(out_ref, value):
    groups, lanes = out_ref.shape[-2:]
    for g in range(groups):
        out_ref[..., g, :] = value[..., g * lanes : (g + 1) * lanes]


def held_part(held):
    return lambda i, b, s, low, high: held.at[b, s, pl.ds(low, high - low), :]


def load_kernel(order, steps, pieces, w_ref, held, sem):
    copies = piece_loads(order, steps, pieces, w_ref, held_part(held), sem)
    for copy in copies:
        copy.start()
    for copy in copies:
        copy.wait()


def middle_kernel(order, here, missing, steps, pieces, inputs_count, *refs):
    xs, (held, w_ref, *refs) = refs[: len(here)], refs[len(here) :]
    *refs, rest, rest_sem, sem = refs
    inputs, (total, next_held, *made) = refs[:inputs_count], refs[inputs_count:]
    fresh = bool(made)
    late = piece_loads(
        order, here, missing, w_ref,
        lambda i, b, s, low, high: rest.at[i, pl.ds(0, high - low), :], rest_sem,
    )
    ahead = piece_loads(order, steps, pieces, w_ref, held_part(next_held), sem)
    soon = max(SOON - 2 * len(late), 0)
    for copy in late + ahead[:soon]:
        copy.start()
    if made:
        make_tables(*inputs, *made, total.shape[1])
    whole = min(s for _, s, _, _ in missing) if missing else held.shape[1]

    @pl.loop(0, whole)
    def _(s):
        add_products([x[...] for x in xs], lambda b, at: held[b, s, :, at], total, s, fresh)

    for copy in ahead[soon:]:
        copy.start()
    for copy in late:
        copy.wait()
    for s in range(whole, held.shape[1]):
        gaps = {b: (i, low, high) for i, (b, k, low, high) in enumerate(missing) if k == s}
        parts = []
        for b, x in enumerate(xs):
            i, low, high = gaps.get(b, (0, x.shape[1], x.shape[1]))
            if low:
                parts.append((x[:, :low], lambda at, b=b, low=low: held[b, s, :low, at]))
            if low < high:
                parts.append((x[:, low:], lambda at, i=i, n=high - low: rest[i, :n, at]))
        values, weights = zip(*parts)
        add_products(values, lambda k, at: weights[k](at), total, s, fresh)
    for copy in ahead:
        copy.wait()


def half_kernel(x_ref, held, _, total):
    depth = x_ref.shape[1]
    for s in range(total.shape[0]):
        add_products([x_ref[...]], lambda b, at: held[0, s, :depth, at], total, s, cols=WIDE)


def make_tables(taps_in, decay, residue, taps, table, tile, tile_step, fade, rows):
    rate = decay[...]
    coeffs = residue[...] * jnp.sqrt(1.0 - jnp.exp(-2.0 * rate))
    for i, power in enumerate((1, rows, rows - 1, rows - 2)):
        spread(table.at[i], jnp.exp(-rate * power))
    spread(table.at[4], coeffs)
    spread(taps, taps_in[...])
    for r in range(tile.shape[1]):
        tile[:, r, :] = coeffs * jnp.exp(-rate * (r - 1.0))
        fade[:, r, :] = jnp.exp(-rate * (fade.shape[1] - 1.0 - r))
    tile_step[...] = jnp.exp(-rate * tile.shape[1])


def over_rows(step, start, stop, carry):
    aligned = -(-start // UNROLL) * UNROLL
    for t in range(start, aligned):
        carry = step(t, carry)

    def group(i, carry):
        for j in range(UNROLL):
            carry = step(i * UNROLL + j, carry)
        return carry

    return lax.fori_loop(aligned // UNROLL, stop // UNROLL, group, carry)


def filtered(taps, s, value, cols):
    one, two = pltpu.roll(value, 1, 0), pltpu.roll(value, 2, 0)
    lags = [taps[j, s : s + 1, cols] for j in range(3)]
    return lags[0] * value + lags[1] * one + lags[2] * two


def last_kernel(x_ref, held, taps, tile_step, fade, _, total, source, out_ref):
    depth = x_ref.shape[1]
    for s in range(total.shape[0]):
        add_products([x_ref[...]], lambda b, at: held[0, s, depth:, at], total, s, cols=WIDE)
    rows = source.shape[0]
    modes, tall, _ = fade.shape
    groups, lanes = out_ref.shape[1:]
    row = lax.broadcasted_iota(jnp.int32, (tall, lanes), 0)
    for g in range(groups):
        cols = slice(g * lanes, (g + 1) * lanes)
        one, two = total[1, :, cols], total[2, :, cols]
        value = filtered(taps, 1, one, cols) * filtered(taps, 2, two, cols)
        source[:, cols] = value
        step = [jnp.broadcast_to(tile_step[n : n + 1, cols], (tall, lanes)) for n in range(modes)]
        first = jnp.where(row < 2, 0.0, value[:tall])
        state = [first] * modes
        for i in range(tall, rows, tall):
            state = [a * b + value[i : i + tall] for a, b in zip(state, step)]
        for n in range(modes):
            out_ref[n, g : g + 1, :] = jnp.sum(state[n] * fade[n, :, cols], axis=0, keepdims=True)
        query = total[0, rows - tall :, cols]
        for s, ends in ((1, one), (2, two)):
            out_ref[modes + s * 2 - 2 : modes + s * 2, g, :] = ends[:2]
        for s, ends in ((0, query), (1, one), (2, two)):
            low = modes + 4 + s * 2
            out_ref[low : low + 2, g, :] = ends[-2:]


def tree_sum(terms):
    while len(terms) > 1:
        terms = [a + b for a, b in zip(terms[::2], terms[1::2])] + terms[len(terms) & ~1 :]
    return terms[0]


def local_kernel(total, natural, taps, table, query, response, heads, work, low, source):
    rows, groups, lanes = source.shape
    modes = table.shape[1]
    for g in range(groups):
        cols = slice(g * lanes, (g + 1) * lanes)
        value = total[0, :, cols]
        query[:, cols] = filtered(taps, 0, value, cols)
        low[:, g, :] = value[:8]
        source[:, g, :] = natural[:, cols]
    for j in range(2):
        heads[j] = low[j]
        work[j] = jnp.zeros((groups, lanes), jnp.float32)

    def step_row(t, state):
        u = source[t]
        state = [table[0, n] * state[n] + u for n in range(modes)]
        work[t] = tree_sum([table[4, n] * state[n] for n in range(modes)])
        return state

    over_rows(step_row, 2, rows, [jnp.zeros((groups, lanes), jnp.float32)] * modes)
    for g in range(groups):
        response[:, g * lanes : (g + 1) * lanes] = work[:, g, :]


def edge(taps, s, first, second, before, last):
    return (
        taps[0, s] * first + taps[1, s] * last + taps[2, s] * before,
        taps[0, s] * second + taps[1, s] * first + taps[2, s] * last,
    )


def lead_sources(taps, heads, rims):
    one = edge(taps, 1, heads[0], heads[1], rims[2], rims[3])
    two = edge(taps, 2, heads[2], heads[3], rims[4], rims[5])
    return one[0] * two[0], one[1] * two[1]


class Summary:
    def __init__(self, rows, modes):
        self.state = rows[:modes]
        self.heads = rows[modes : modes + 4]
        self.rims = rows[modes + 4 :]

    @classmethod
    def read(cls, ref, modes):
        return cls([ref[i] for i in range(ref.shape[0])], modes)

    @classmethod
    def chosen(cls, odd, when_odd, when_even, modes):
        pairs = zip(when_odd.rows(), when_even.rows())
        return cls([jnp.where(odd, a, b) for a, b in pairs], modes)

    def rows(self):
        return self.state + self.heads + self.rims

    def complete(self, taps, rims, by_first, by_second):
        u0, u1 = lead_sources(taps, self.heads, rims)
        return [x + f * u0 + g * u1 for x, f, g in zip(self.state, by_first, by_second)]


def powers(table):
    return [[table[i, n] for n in range(table.shape[1])] for i in range(table.shape[0])]


def chip_kernel(lone, local, partner, taps, table, out_ref):
    modes = table.shape[1]
    odd = lax.rem(lax.axis_index("ctx"), 2) == 1
    mine, other = Summary.read(local, modes), Summary.read(partner, modes)
    first = Summary.chosen(odd, other, mine, modes)
    second = Summary.chosen(odd, mine, other, modes)
    _, block, less_one, less_two, _ = powers(table)
    start, heads = first.state, first.heads
    if lone:
        start, heads = first.complete(taps, [jnp.zeros_like(heads[0])] * 6, less_one, less_two), []
    end = second.complete(taps, first.rims, less_one, less_two)
    joined = [d * x + y for d, x, y in zip(block, start, end)]
    for i, value in enumerate(joined + heads + second.rims):
        out_ref[i] = value


def final_kernel(lone, count, *refs):
    sent = refs[:count]
    local, partner, query, response, query_heads, taps, table, tile, tile_step, *refs = refs[count:]
    out_ref, states, firsts, rounded_out, out_sem = refs
    rows = query.shape[0]
    groups, lanes = local.shape[1:]
    modes = table.shape[1]
    zero = jnp.zeros((groups, lanes), jnp.float32)
    index = lax.axis_index("ctx")
    odd = lax.rem(index, 2) == 1
    _, block, less_one, less_two, _ = powers(table)
    values = [
        [jnp.where(index >= 2 * (d + 1), ref[i], zero) for i in range(ref.shape[0])]
        for d, ref in enumerate(sent)
    ]
    rims = [value[-6:] for value in values] + [[zero] * 6]
    state = [zero] * modes
    for d in reversed(range(count)):
        end = values[d][:modes]
        if not lone:
            end = Summary(values[d], modes).complete(
                taps,
                rims[d + 1],
                [a * b for a, b in zip(block, less_one)],
                [a * b for a, b in zip(block, less_two)],
            )
        state = [d * d * x + y for d, x, y in zip(block, state, end)]
    before = Summary.read(partner, modes)
    end = before.complete(taps, rims[0], less_one, less_two)
    state = [jnp.where(odd, d * x + y, x) for d, x, y in zip(block, state, end)]
    rim = [jnp.where(odd, a, b) for a, b in zip(before.rims, rims[0])]

    leads = lead_sources(taps, Summary.read(local, modes).heads, rim)
    heads = edge(taps, 0, query_heads[0], query_heads[1], rim[0], rim[1])
    for t, u in enumerate(leads):
        state = [table[0, n] * state[n] + u for n in range(modes)]
        firsts[t] = heads[t] * tree_sum([table[4, n] * state[n] for n in range(modes)])
    for n in range(modes):
        states[n] = state[n]

    tall = tile.shape[1]
    row = lax.broadcasted_iota(jnp.int32, (tall, lanes), 0)
    copies = []
    for g in range(groups):
        cols = slice(g * lanes, (g + 1) * lanes)
        carried = [tile[n, :, cols] * states[n, g : g + 1, :] for n in range(modes)]
        step = [jnp.broadcast_to(tile_step[n : n + 1, cols], (tall, lanes)) for n in range(modes)]
        for i in range(0, rows, 2 * tall):
            pair = []
            for at in (slice(i, i + tall), slice(i + tall, i + 2 * tall)):
                value = query[at, cols] * (response[at, cols] + tree_sum(carried))
                if at.start == 0:
                    value = jnp.where(row == 0, firsts[0, g : g + 1, :], value)
                    value = jnp.where(row == 1, firsts[1, g : g + 1, :], value)
                pair.append(value)
                carried = [a * b for a, b in zip(carried, step)]
            rounded_out[i : i + 2 * tall, cols] = jnp.concatenate(pair, axis=0).astype(out_ref.dtype)
        if g % 2:
            wide = slice((g - 1) * lanes, (g + 1) * lanes)
            k = g // 2
            copies.append(
                pltpu.make_async_copy(rounded_out.at[:, wide], out_ref.at[:, wide], out_sem.at[k])
            )
            copies[-1].start()
    for copy in copies:
        copy.wait()


def on_device(tokens, in_weight, filter_taps, decay_rate, residue):
    rows, width = tokens.shape
    streams, chans = in_weight.shape[1:]
    lags = filter_taps.shape[0]
    modes = decay_rate.shape[0]
    groups = chans // LANES
    tp, ctx = lax.axis_size("tp"), lax.axis_size("ctx")
    order = ring_order(tp)
    weight = jnp.transpose(in_weight, (1, 0, 2))
    half = tp // 2
    ahead = [(order[i], order[(i + 1) % tp]) for i in range(tp)]
    back = [(b, a) for a, b in ahead]

    def f32(*shape):
        return jax.ShapeDtypeStruct(shape, jnp.float32)

    def held(count):
        return jax.ShapeDtypeStruct((count, streams, width, chans), jnp.bfloat16)

    def loads(step):
        return [step, -step] if step < half else [step]

    sums = f32(streams, rows, chans)
    params = pltpu.CompilerParams(vmem_limit_bytes=12 << 20)
    cost = pl.CostEstimate(flops=0, bytes_accessed=16 << 20, transcendentals=0)

    def blocks(step):
        return [0] + loads(1) if step == 1 else loads(step)

    def left(step):
        if step >= half:
            return []
        last, halfway = len(blocks(step)) - 1, (width // 2, width)
        return [(last, streams - 1, *halfway) if step < half - 1 else (last, streams - 1, 0, width)]

    def pieces(step):
        lacking = {(b, s): low for b, s, low, _ in left(step)}
        every = [(b, s) for s in range(streams) for b in range(len(blocks(step)))]
        found = [(b, s, 0, lacking.get((b, s), width)) for b, s in every]
        cuts = [(b, s, low, low + width // 2) for b, s, _, high in found for low in (0, width // 2)[: 2 * high // width]]
        return cuts

    weights = pl.pallas_call(
        functools.partial(load_kernel, order, blocks(1), pieces(1)),
        out_shape=held(len(blocks(1))),
        in_specs=[HBM],
        out_specs=VMEM,
        scratch_shapes=[pltpu.SemaphoreType.DMA((len(pieces(1)),))],
        compiler_params=params,
        cost_estimate=cost,
        name="load_first",
    )(weight)
    fore, aft, total = tokens, tokens, None
    for step in range(1, half):
        fore = lax.ppermute(fore, "tp", ahead)
        aft = lax.ppermute(aft, "tp", back)
        fore, total, weights = lax.optimization_barrier((fore, total, weights))
        aft, total, weights = lax.optimization_barrier((aft, total, weights))
        first = step == 1
        xs = [tokens, fore, aft] if first else [fore, aft]
        extra = [filter_taps, decay_rate, residue] if first else [total]
        made = []
        if first:
            made = [f32(lags, streams, groups, LANES), f32(5, modes, groups, LANES)]
            made += [f32(modes, 8, chans), f32(modes, chans), f32(modes, 8, chans)]
        total, weights, *made = pl.pallas_call(
            functools.partial(
                middle_kernel, order, blocks(step), left(step), blocks(step + 1), pieces(step + 1),
                len(extra),
            ),
            out_shape=[sums, held(len(blocks(step + 1)))] + made,
            in_specs=[VMEM] * (len(xs) + 1) + [HBM] + [VMEM] * len(extra),
            out_specs=[VMEM] * (2 + len(made)),
            scratch_shapes=[
                pltpu.VMEM((2, width, chans), jnp.bfloat16),
                pltpu.SemaphoreType.DMA((2,)),
                pltpu.SemaphoreType.DMA((len(pieces(step + 1)),)),
            ],
            input_output_aliases={} if first else {len(xs) + 2: 0},
            compiler_params=params,
            cost_estimate=cost,
            name="project_blocks",
        )(*xs, weights, weight, *extra)
        if first:
            taps, table, tile, tile_step, fade = made
    fore = lax.ppermute(fore[:, : width // 2], "tp", ahead)
    aft = lax.ppermute(aft[:, width // 2 :], "tp", back)
    total = pl.pallas_call(
        half_kernel,
        out_shape=sums,
        in_specs=[VMEM] * 3,
        out_specs=VMEM,
        input_output_aliases={2: 0},
        compiler_params=params,
        cost_estimate=cost,
        name="project_half",
    )(fore, weights, total)
    total, source, local = pl.pallas_call(
        last_kernel,
        out_shape=[sums, f32(rows, chans), f32(modes + EDGE, groups, LANES)],
        in_specs=[VMEM] * 6,
        out_specs=[VMEM] * 3,
        input_output_aliases={5: 0},
        compiler_params=params,
        cost_estimate=cost,
        name="project_last",
    )(aft, weights, filter_taps, tile_step, fade, total)

    partner = lax.ppermute(local, "ctx", [(j, j ^ 1) for j in range(ctx)])
    lone = ctx == 4
    chip = pl.pallas_call(
        functools.partial(chip_kernel, lone),
        out_shape=f32(modes + (6 if lone else EDGE), groups, LANES),
        in_specs=[VMEM] * 4,
        out_specs=VMEM,
        compiler_params=params,
        name="chip_state",
    )(local, partner, taps, table)
    sent = [
        lax.ppermute(chip, "ctx", [(j, (j + d) % ctx) for j in range(ctx)])
        for d in range(2, ctx, 2)
    ]
    query, response, heads = pl.pallas_call(
        local_kernel,
        out_shape=[f32(rows, chans), f32(rows, chans), f32(2, groups, LANES)],
        in_specs=[VMEM] * 4,
        out_specs=[VMEM] * 3,
        scratch_shapes=[
            pltpu.VMEM((rows, groups, LANES), jnp.float32),
            pltpu.VMEM((8, groups, LANES), jnp.float32),
            pltpu.VMEM((rows, groups, LANES), jnp.float32),
        ],
        compiler_params=params,
        cost_estimate=cost,
        name="local_response",
    )(total, source, filter_taps, table)
    return pl.pallas_call(
        functools.partial(final_kernel, lone, len(sent)),
        out_shape=jax.ShapeDtypeStruct((rows, chans), jnp.bfloat16),
        in_specs=[VMEM] * (len(sent) + 9),
        out_specs=HBM,
        scratch_shapes=[
            pltpu.VMEM((modes, groups, LANES), jnp.float32),
            pltpu.VMEM((2, groups, LANES), jnp.float32),
            pltpu.VMEM((rows, chans), jnp.bfloat16),
            pltpu.SemaphoreType.DMA((groups // 2,)),
        ],
        compiler_params=params,
        name="carried_response",
    )(*sent, local, partner, query, response, heads, taps, table, tile, tile_step)


def solution(mesh):
    return jax.shard_map(
        on_device,
        mesh=mesh,
        in_specs=(
            P("ctx", "tp"),
            P(None, None, "tp"),
            P(None, None, "tp"),
            P(None, "tp"),
            P(None, "tp"),
        ),
        out_specs=P("ctx", "tp"),
        check_vma=False,
    )
```

```python
import functools

import jax
import jax.numpy as jnp
from jax import lax
from jax.experimental import pallas as pl
from jax.experimental.pallas import tpu as pltpu
from jax.sharding import PartitionSpec as P

LANES = 128
COLS = 256
WIDE = 512
SOON = 4
GRID_ROWS = 4
EDGE = 10
UNROLL = 16
VMEM = pl.BlockSpec(memory_space=pltpu.VMEM)
HBM = pl.BlockSpec(memory_space=pltpu.HBM)


def ring_order(count):
    if count % (2 * GRID_ROWS):
        return list(range(count))
    cols = count // GRID_ROWS
    cells = [(0, c) for c in range(cols)]
    for r in range(1, GRID_ROWS):
        inner = list(range(1, cols))
        cells += [(r, c) for c in (reversed(inner) if r % 2 else inner)]
    cells += [(r, 0) for r in range(GRID_ROWS - 1, 0, -1)]
    return [r * cols + c for r, c in cells]


def owner_at(order, step):
    me = lax.axis_index("tp")
    owner = jnp.int32(0)
    for place, index in enumerate(order):
        owner = jnp.where(me == index, order[(place - step) % len(order)], owner)
    return owner


def piece_loads(order, steps, pieces, w_ref, target, sem):
    width = w_ref.shape[1] // len(order)
    starts = [pl.multiple_of(owner_at(order, step) * width, width) for step in steps]
    return [
        pltpu.make_async_copy(
            w_ref.at[s, pl.ds(starts[b] + low, high - low), :], target(i, b, s, low, high), sem.at[i]
        )
        for i, (b, s, low, high) in enumerate(pieces)
    ]


def add_products(xs, weights, total, s, fresh=False, cols=COLS):
    cols = min(cols, total.shape[2])
    for c in range(0, total.shape[2], cols):
        at = slice(c, c + cols)
        terms = [
            jnp.dot(x, weights(b, at), preferred_element_type=jnp.float32) for b, x in enumerate(xs)
        ]
        total[s, :, at] = sum(terms) if fresh else total[s, :, at] + sum(terms)


def spread(out_ref, value):
    groups, lanes = out_ref.shape[-2:]
    for g in range(groups):
        out_ref[..., g, :] = value[..., g * lanes : (g + 1) * lanes]


def held_part(held):
    return lambda i, b, s, low, high: held.at[b, s, pl.ds(low, high - low), :]


def load_kernel(order, steps, pieces, w_ref, held, sem):
    copies = piece_loads(order, steps, pieces, w_ref, held_part(held), sem)
    for copy in copies:
        copy.start()
    for copy in copies:
        copy.wait()


def middle_kernel(order, here, missing, steps, pieces, inputs_count, *refs):
    xs, (held, w_ref, *refs) = refs[: len(here)], refs[len(here) :]
    *refs, rest, rest_sem, sem = refs
    inputs, (total, next_held, *made) = refs[:inputs_count], refs[inputs_count:]
    fresh = bool(made)
    late = piece_loads(
        order, here, missing, w_ref,
        lambda i, b, s, low, high: rest.at[i, pl.ds(0, high - low), :], rest_sem,
    )
    ahead = piece_loads(order, steps, pieces, w_ref, held_part(next_held), sem)
    soon = max(SOON - len(late), 0)
    for copy in late + ahead[:soon]:
        copy.start()
    if made:
        make_tables(*inputs, *made, total.shape[1])
    whole = min(s for _, s, _, _ in missing) if missing else held.shape[1]

    @pl.loop(0, whole)
    def _(s):
        add_products([x[...] for x in xs], lambda b, at: held[b, s, :, at], total, s, fresh)

    for copy in ahead[soon:]:
        copy.start()
    for copy in late:
        copy.wait()
    for s in range(whole, held.shape[1]):
        gaps = {b: (i, low, high) for i, (b, k, low, high) in enumerate(missing) if k == s}
        parts = []
        for b, x in enumerate(xs):
            i, low, high = gaps.get(b, (0, x.shape[1], x.shape[1]))
            if low:
                parts.append((x[:, :low], lambda at, b=b, low=low: held[b, s, :low, at]))
            if low < high:
                parts.append((x[:, low:], lambda at, i=i, n=high - low: rest[i, :n, at]))
        values, weights = zip(*parts)
        add_products(values, lambda k, at: weights[k](at), total, s, fresh)
    for copy in ahead:
        copy.wait()


def half_kernel(x_ref, held, _, total):
    depth = x_ref.shape[1]
    for s in range(total.shape[0]):
        add_products([x_ref[...]], lambda b, at: held[0, s, :depth, at], total, s, cols=WIDE)


def make_tables(taps_in, decay, residue, taps, table, tile, tile_step, fade, rows):
    rate = decay[...]
    coeffs = residue[...] * jnp.sqrt(1.0 - jnp.exp(-2.0 * rate))
    for i, power in enumerate((1, rows, rows - 1, rows - 2)):
        spread(table.at[i], jnp.exp(-rate * power))
    spread(table.at[4], coeffs)
    spread(taps, taps_in[...])
    for r in range(tile.shape[1]):
        tile[:, r, :] = coeffs * jnp.exp(-rate * (r - 1.0))
        fade[:, r, :] = jnp.exp(-rate * (fade.shape[1] - 1.0 - r))
    tile_step[...] = jnp.exp(-rate * tile.shape[1])


def over_rows(step, start, stop, carry):
    aligned = -(-start // UNROLL) * UNROLL
    for t in range(start, aligned):
        carry = step(t, carry)

    def group(i, carry):
        for j in range(UNROLL):
            carry = step(i * UNROLL + j, carry)
        return carry

    return lax.fori_loop(aligned // UNROLL, stop // UNROLL, group, carry)


def filtered(taps, s, value, cols):
    one, two = pltpu.roll(value, 1, 0), pltpu.roll(value, 2, 0)
    lags = [taps[j, s : s + 1, cols] for j in range(3)]
    return lags[0] * value + lags[1] * one + lags[2] * two


def last_kernel(x_ref, held, taps, tile_step, fade, _, total, source, out_ref):
    depth = held.shape[2] - x_ref.shape[1]
    for s in range(total.shape[0]):
        add_products([x_ref[...]], lambda b, at: held[0, s, depth:, at], total, s, cols=WIDE)
    rows = source.shape[0]
    modes, tall, _ = fade.shape
    groups, lanes = out_ref.shape[1:]
    row = lax.broadcasted_iota(jnp.int32, (tall, lanes), 0)
    for g in range(groups):
        cols = slice(g * lanes, (g + 1) * lanes)
        one, two = total[1, :, cols], total[2, :, cols]
        value = filtered(taps, 1, one, cols) * filtered(taps, 2, two, cols)
        source[:, cols] = value
        step = [jnp.broadcast_to(tile_step[n : n + 1, cols], (tall, lanes)) for n in range(modes)]
        first = jnp.where(row < 2, 0.0, value[:tall])
        state = [first] * modes
        for i in range(tall, rows, tall):
            state = [a * b + value[i : i + tall] for a, b in zip(state, step)]
        for n in range(modes):
            out_ref[n, g : g + 1, :] = jnp.sum(state[n] * fade[n, :, cols], axis=0, keepdims=True)
        query = total[0, rows - tall :, cols]
        for s, ends in ((1, one), (2, two)):
            out_ref[modes + s * 2 - 2 : modes + s * 2, g, :] = ends[:2]
        for s, ends in ((0, query), (1, one), (2, two)):
            low = modes + 4 + s * 2
            out_ref[low : low + 2, g, :] = ends[-2:]


def tree_sum(terms):
    while len(terms) > 1:
        terms = [a + b for a, b in zip(terms[::2], terms[1::2])] + terms[len(terms) & ~1 :]
    return terms[0]


def local_kernel(total, natural, taps, table, query, response, heads, work, low, source):
    rows, groups, lanes = source.shape
    modes = table.shape[1]
    for g in range(groups):
        cols = slice(g * lanes, (g + 1) * lanes)
        value = total[0, :, cols]
        query[:, cols] = filtered(taps, 0, value, cols)
        low[:, g, :] = value[:8]
        source[:, g, :] = natural[:, cols]
    for j in range(2):
        heads[j] = low[j]
        work[j] = jnp.zeros((groups, lanes), jnp.float32)

    def step_row(t, state):
        u = source[t]
        state = [table[0, n] * state[n] + u for n in range(modes)]
        work[t] = tree_sum([table[4, n] * state[n] for n in range(modes)])
        return state

    over_rows(step_row, 2, rows, [jnp.zeros((groups, lanes), jnp.float32)] * modes)
    for g in range(groups):
        response[:, g * lanes : (g + 1) * lanes] = work[:, g, :]


def edge(taps, s, first, second, before, last):
    return (
        taps[0, s] * first + taps[1, s] * last + taps[2, s] * before,
        taps[0, s] * second + taps[1, s] * first + taps[2, s] * last,
    )


def lead_sources(taps, heads, rims):
    one = edge(taps, 1, heads[0], heads[1], rims[2], rims[3])
    two = edge(taps, 2, heads[2], heads[3], rims[4], rims[5])
    return one[0] * two[0], one[1] * two[1]


class Summary:
    def __init__(self, rows, modes):
        self.state = rows[:modes]
        self.heads = rows[modes : modes + 4]
        self.rims = rows[modes + 4 :]

    @classmethod
    def read(cls, ref, modes):
        return cls([ref[i] for i in range(ref.shape[0])], modes)

    @classmethod
    def chosen(cls, odd, when_odd, when_even, modes):
        pairs = zip(when_odd.rows(), when_even.rows())
        return cls([jnp.where(odd, a, b) for a, b in pairs], modes)

    def rows(self):
        return self.state + self.heads + self.rims

    def complete(self, taps, rims, by_first, by_second):
        u0, u1 = lead_sources(taps, self.heads, rims)
        return [x + f * u0 + g * u1 for x, f, g in zip(self.state, by_first, by_second)]


def powers(table):
    return [[table[i, n] for n in range(table.shape[1])] for i in range(table.shape[0])]


def chip_kernel(lone, local, partner, taps, table, out_ref):
    modes = table.shape[1]
    odd = lax.rem(lax.axis_index("ctx"), 2) == 1
    mine, other = Summary.read(local, modes), Summary.read(partner, modes)
    first = Summary.chosen(odd, other, mine, modes)
    second = Summary.chosen(odd, mine, other, modes)
    _, block, less_one, less_two, _ = powers(table)
    start, heads = first.state, first.heads
    if lone:
        start, heads = first.complete(taps, [jnp.zeros_like(heads[0])] * 6, less_one, less_two), []
    end = second.complete(taps, first.rims, less_one, less_two)
    joined = [d * x + y for d, x, y in zip(block, start, end)]
    for i, value in enumerate(joined + heads + second.rims):
        out_ref[i] = value


def final_kernel(lone, count, *refs):
    sent = refs[:count]
    local, partner, query, response, query_heads, taps, table, tile, tile_step, *refs = refs[count:]
    out_ref, states, firsts, rounded_out, out_sem = refs
    rows = query.shape[0]
    groups, lanes = local.shape[1:]
    modes = table.shape[1]
    zero = jnp.zeros((groups, lanes), jnp.float32)
    index = lax.axis_index("ctx")
    odd = lax.rem(index, 2) == 1
    _, block, less_one, less_two, _ = powers(table)
    values = [
        [jnp.where(index >= 2 * (d + 1), ref[i], zero) for i in range(ref.shape[0])]
        for d, ref in enumerate(sent)
    ]
    rims = [value[-6:] for value in values] + [[zero] * 6]
    state = [zero] * modes
    for d in reversed(range(count)):
        end = values[d][:modes]
        if not lone:
            end = Summary(values[d], modes).complete(
                taps,
                rims[d + 1],
                [a * b for a, b in zip(block, less_one)],
                [a * b for a, b in zip(block, less_two)],
            )
        state = [d * d * x + y for d, x, y in zip(block, state, end)]
    before = Summary.read(partner, modes)
    end = before.complete(taps, rims[0], less_one, less_two)
    state = [jnp.where(odd, d * x + y, x) for d, x, y in zip(block, state, end)]
    rim = [jnp.where(odd, a, b) for a, b in zip(before.rims, rims[0])]

    leads = lead_sources(taps, Summary.read(local, modes).heads, rim)
    heads = edge(taps, 0, query_heads[0], query_heads[1], rim[0], rim[1])
    for t, u in enumerate(leads):
        state = [table[0, n] * state[n] + u for n in range(modes)]
        firsts[t] = heads[t] * tree_sum([table[4, n] * state[n] for n in range(modes)])
    for n in range(modes):
        states[n] = state[n]

    tall = tile.shape[1]
    row = lax.broadcasted_iota(jnp.int32, (tall, lanes), 0)
    copies = []
    for g in range(groups):
        cols = slice(g * lanes, (g + 1) * lanes)
        carried = [tile[n, :, cols] * states[n, g : g + 1, :] for n in range(modes)]
        step = [jnp.broadcast_to(tile_step[n : n + 1, cols], (tall, lanes)) for n in range(modes)]
        for i in range(0, rows, 2 * tall):
            pair = []
            for at in (slice(i, i + tall), slice(i + tall, i + 2 * tall)):
                value = query[at, cols] * (response[at, cols] + tree_sum(carried))
                if at.start == 0:
                    value = jnp.where(row == 0, firsts[0, g : g + 1, :], value)
                    value = jnp.where(row == 1, firsts[1, g : g + 1, :], value)
                pair.append(value)
                carried = [a * b for a, b in zip(carried, step)]
            rounded_out[i : i + 2 * tall, cols] = jnp.concatenate(pair, axis=0).astype(out_ref.dtype)
        if g % 2:
            wide = slice((g - 1) * lanes, (g + 1) * lanes)
            k = g // 2
            copies.append(
                pltpu.make_async_copy(rounded_out.at[:, wide], out_ref.at[:, wide], out_sem.at[k])
            )
            copies[-1].start()
    for copy in copies:
        copy.wait()


def on_device(tokens, in_weight, filter_taps, decay_rate, residue):
    rows, width = tokens.shape
    streams, chans = in_weight.shape[1:]
    lags = filter_taps.shape[0]
    modes = decay_rate.shape[0]
    groups = chans // LANES
    tp, ctx = lax.axis_size("tp"), lax.axis_size("ctx")
    order = ring_order(tp)
    weight = jnp.transpose(in_weight, (1, 0, 2))
    half = tp // 2
    ahead = [(order[i], order[(i + 1) % tp]) for i in range(tp)]
    back = [(b, a) for a, b in ahead]

    def f32(*shape):
        return jax.ShapeDtypeStruct(shape, jnp.float32)

    def held(count):
        return jax.ShapeDtypeStruct((count, streams, width, chans), jnp.bfloat16)

    def loads(step):
        return [step, -step] if step < half else [step]

    sums = f32(streams, rows, chans)
    params = pltpu.CompilerParams(vmem_limit_bytes=12 << 20)
    cost = pl.CostEstimate(flops=0, bytes_accessed=16 << 20, transcendentals=0)

    def blocks(step):
        return [0] + loads(1) if step == 1 else loads(step)

    def left(step):
        if step >= half:
            return []
        last, halfway = len(blocks(step)) - 1, (width // 2, width)
        return [(last, streams - 1, *halfway) if step < half - 1 else (last, streams - 1, 0, width)]

    def pieces(step):
        lacking = {(b, s): low for b, s, low, _ in left(step)}
        every = [(b, s) for s in range(streams) for b in range(len(blocks(step)))]
        found = [(b, s, 0, lacking.get((b, s), width)) for b, s in every]
        return [piece for piece in found if piece[3]]

    weights = pl.pallas_call(
        functools.partial(load_kernel, order, blocks(1), pieces(1)),
        out_shape=held(len(blocks(1))),
        in_specs=[HBM],
        out_specs=VMEM,
        scratch_shapes=[pltpu.SemaphoreType.DMA((len(pieces(1)),))],
        compiler_params=params,
        cost_estimate=cost,
        name="load_first",
    )(weight)
    fore, aft, total = tokens, tokens, None
    for step in range(1, half):
        fore = lax.ppermute(fore, "tp", ahead)
        aft = lax.ppermute(aft, "tp", back)
        fore, total, weights = lax.optimization_barrier((fore, total, weights))
        aft, total, weights = lax.optimization_barrier((aft, total, weights))
        first = step == 1
        xs = [tokens, fore, aft] if first else [fore, aft]
        extra = [filter_taps, decay_rate, residue] if first else [total]
        made = []
        if first:
            made = [f32(lags, streams, groups, LANES), f32(5, modes, groups, LANES)]
            made += [f32(modes, 8, chans), f32(modes, chans), f32(modes, 8, chans)]
        total, weights, *made = pl.pallas_call(
            functools.partial(
                middle_kernel, order, blocks(step), left(step), blocks(step + 1), pieces(step + 1),
                len(extra),
            ),
            out_shape=[sums, held(len(blocks(step + 1)))] + made,
            in_specs=[VMEM] * (len(xs) + 1) + [HBM] + [VMEM] * len(extra),
            out_specs=[VMEM] * (2 + len(made)),
            scratch_shapes=[
                pltpu.VMEM((2, width, chans), jnp.bfloat16),
                pltpu.SemaphoreType.DMA((2,)),
                pltpu.SemaphoreType.DMA((len(pieces(step + 1)),)),
            ],
            input_output_aliases={} if first else {len(xs) + 2: 0},
            compiler_params=params,
            cost_estimate=cost,
            name="project_blocks",
        )(*xs, weights, weight, *extra)
        if first:
            taps, table, tile, tile_step, fade = made
    cut = width // 2 if width % (4 * LANES) else width * 3 // 4
    fore = lax.ppermute(fore[:, :cut], "tp", ahead)
    aft = lax.ppermute(aft[:, cut:], "tp", back)
    total = pl.pallas_call(
        half_kernel,
        out_shape=sums,
        in_specs=[VMEM] * 3,
        out_specs=VMEM,
        input_output_aliases={2: 0},
        compiler_params=params,
        cost_estimate=cost,
        name="project_half",
    )(fore, weights, total)
    total, source, local = pl.pallas_call(
        last_kernel,
        out_shape=[sums, f32(rows, chans), f32(modes + EDGE, groups, LANES)],
        in_specs=[VMEM] * 6,
        out_specs=[VMEM] * 3,
        input_output_aliases={5: 0},
        compiler_params=params,
        cost_estimate=cost,
        name="project_last",
    )(aft, weights, filter_taps, tile_step, fade, total)

    partner = lax.ppermute(local, "ctx", [(j, j ^ 1) for j in range(ctx)])
    lone = ctx == 4
    chip = pl.pallas_call(
        functools.partial(chip_kernel, lone),
        out_shape=f32(modes + (6 if lone else EDGE), groups, LANES),
        in_specs=[VMEM] * 4,
        out_specs=VMEM,
        compiler_params=params,
        name="chip_state",
    )(local, partner, taps, table)
    sent = [
        lax.ppermute(chip, "ctx", [(j, (j + d) % ctx) for j in range(ctx)])
        for d in range(2, ctx, 2)
    ]
    query, response, heads = pl.pallas_call(
        local_kernel,
        out_shape=[f32(rows, chans), f32(rows, chans), f32(2, groups, LANES)],
        in_specs=[VMEM] * 4,
        out_specs=[VMEM] * 3,
        scratch_shapes=[
            pltpu.VMEM((rows, groups, LANES), jnp.float32),
            pltpu.VMEM((8, groups, LANES), jnp.float32),
            pltpu.VMEM((rows, groups, LANES), jnp.float32),
        ],
        compiler_params=params,
        cost_estimate=cost,
        name="local_response",
    )(total, source, filter_taps, table)
    return pl.pallas_call(
        functools.partial(final_kernel, lone, len(sent)),
        out_shape=jax.ShapeDtypeStruct((rows, chans), jnp.bfloat16),
        in_specs=[VMEM] * (len(sent) + 9),
        out_specs=HBM,
        scratch_shapes=[
            pltpu.VMEM((modes, groups, LANES), jnp.float32),
            pltpu.VMEM((2, groups, LANES), jnp.float32),
            pltpu.VMEM((rows, chans), jnp.bfloat16),
            pltpu.SemaphoreType.DMA((groups // 2,)),
        ],
        compiler_params=params,
        name="carried_response",
    )(*sent, local, partner, query, response, heads, taps, table, tile, tile_step)


def solution(mesh):
    return jax.shard_map(
        on_device,
        mesh=mesh,
        in_specs=(
            P("ctx", "tp"),
            P(None, None, "tp"),
            P(None, None, "tp"),
            P(None, "tp"),
            P(None, "tp"),
        ),
        out_specs=P("ctx", "tp"),
        check_vma=False,
    )
```
